32 devices in a mesh: space: 8 (over z, y), nbr: 4 (over x, core).
Axes of the slice: x: 2, y: 2, z: 4, core: 2. Of those that a mesh axis runs over, the one named last changes fastest.
Arguments:
- nodes: bfloat16 [2, 3072, 512], P(None, 'space'), may hold values from -6 to 6
- edges: bfloat16 [2, 3072, 60, 192], P(None, 'space', 'nbr'), may hold values from -6 to 6
- neighbors: int32 [2, 3072, 60], P(None, 'space', 'nbr'), may hold values from 0 to 1215, as said below
- slot_live: int32 [2, 3072, 60], P(None, 'space', 'nbr'), may hold values from 0 to 1, as said below
- send_rows: int32 [2, 64, 8], P(None, 'space'), may hold values from 0 to 383
- message_self: bfloat16 [512, 512], replicated, may hold values from -0.25 to 0.25
- message_peer: bfloat16 [512, 512], replicated, may hold values from -0.25 to 0.25
- message_edge: bfloat16 [192, 512], replicated, may hold values from -0.4375 to 0.4375
- message_bias: bfloat16 [512], replicated, may hold values from -1.75 to 1.75
- message_out: bfloat16 [512, 512], replicated, may hold values from -0.25 to 0.25
- message_shift: bfloat16 [512], replicated, may hold values from -1.75 to 1.75
- first_gain: bfloat16 [512], replicated, may hold values from 0.5 to 1.5
- first_shift: bfloat16 [512], replicated, may hold values from -1.75 to 1.75
- hidden_in: bfloat16 [512, 2048], replicated, may hold values from -0.25 to 0.25
- hidden_bias: bfloat16 [2048], replicated, may hold values from -1.75 to 1.75
- hidden_out: bfloat16 [2048, 512], replicated, may hold values from -0.125 to 0.125
- output_bias: bfloat16 [512], replicated, may hold values from -1.75 to 1.75
- second_gain: bfloat16 [512], replicated, may hold values from 0.5 to 1.5
- second_shift: bfloat16 [512], replicated, may hold values from -1.75 to 1.75
- edge_self: bfloat16 [512, 192], replicated, may hold values from -0.25 to 0.25
- edge_peer: bfloat16 [512, 192], replicated, may hold values from -0.25 to 0.25
- edge_own: bfloat16 [192, 192], replicated, may hold values from -0.4375 to 0.4375
- edge_bias: bfloat16 [192], replicated, may hold values from -1.75 to 1.75
- edge_out: bfloat16 [192, 192], replicated, may hold values from -0.4375 to 0.4375
- edge_shift: bfloat16 [192], replicated, may hold values from -1.75 to 1.75
- third_gain: bfloat16 [192], replicated, may hold values from 0.5 to 1.5
- third_shift: bfloat16 [192], replicated, may hold values from -1.75 to 1.75
- node_cot: bfloat16 [2, 3072, 512], P(None, 'space'), may hold values from -6 to 6
- edge_cot: bfloat16 [2, 3072, 60, 192], P(None, 'space', 'nbr'), may hold values from -6 to 6
Outputs:
- new_nodes: bfloat16 [2, 3072, 512], P(None, 'space')
- new_edges: bfloat16 [2, 3072, 60, 192], P(None, 'space', 'nbr')
- node_grad: float32 [2, 3072, 512], P(None, 'space', 'nbr')
- edge_grad: bfloat16 [2, 3072, 60, 192], P(None, 'space', 'nbr')
- message_self_grad: float32 [512, 512], replicated
- message_peer_grad: float32 [512, 512], replicated
- message_edge_grad: float32 [192, 512], replicated
- message_bias_grad: float32 [512], replicated
- message_out_grad: float32 [512, 512], replicated
- message_shift_grad: float32 [512], replicated
- first_gain_grad: float32 [512], replicated
- first_shift_grad: float32 [512], replicated
- hidden_in_grad: float32 [512, 2048], replicated
- hidden_bias_grad: float32 [2048], replicated
- hidden_out_grad: float32 [2048, 512], replicated
- output_bias_grad: float32 [512], replicated
- second_gain_grad: float32 [512], replicated
- second_shift_grad: float32 [512], replicated
- edge_self_grad: float32 [512, 192], replicated
- edge_peer_grad: float32 [512, 192], replicated
- edge_own_grad: float32 [192, 192], replicated
- edge_bias_grad: float32 [192], replicated
- edge_out_grad: float32 [192, 192], replicated
- edge_shift_grad: float32 [192], replicated
- third_gain_grad: float32 [192], replicated
- third_shift_grad: float32 [192], replicated
The draws below stay inside these ranges and needn't reach their ends.
Inputs may be any that keep to these rules, and one draw needn't show every extreme that they name: `neighbors`: A table index of residue i: below 1152 it names a row of the block before, the own block or the block after; from 1152 on it names an entry of the rows that the blocks send to i's block. The first block names no row before it, the last none after it. `slot_live`: the last rows of a block may be padding with no live slot; at least half of each block's rows are real residues. `send_rows`: row indices within the sending block.
All inputs are finite; a program needn't handle non-finite values.
Results may differ from the reference program's by a relative error of at most 0.017.
Values may be sent and summed in bfloat16 or wider, within the bound.
A program may use at most 320 MiB of HBM per device.

```python
import jax
import jax.numpy as jnp
from jax import lax

DN = 512
DE = 192
FF = 2048
K = 60
RES = 384
CAP = 8
MB = 2
SLOTS = 15
NODES = 3072
PEERS = 64
N_SPACE = 8
N_NBR = 4


def draw_neighbors(key, part):
    key = jax.random.fold_in(key, 11)
    key_near, key_peer, key_entry, key_pick = jax.random.split(key, 4)
    shape = (MB, NODES, K)
    rows = jnp.arange(NODES, dtype=jnp.int32)
    block = (rows // RES)[None, :, None]
    within = (rows % RES)[None, :, None]
    lowest = jnp.where(block == 0, RES, 0)
    highest = jnp.where(block == N_SPACE - 1, 2 * RES, 3 * RES)
    near = jax.random.randint(key_near, shape, 0, 3 * RES)
    near = lowest + near % (highest - lowest)
    peer_random = jax.random.randint(key_peer, shape, 0, N_SPACE)
    forced_step = jnp.where(within == 0, N_SPACE // 2, jnp.where(within == 1, 1, N_SPACE - 1))
    peer_forced = (block + forced_step) % N_SPACE
    entry_random = jax.random.randint(key_entry, shape, 0, CAP)
    slot_place = jnp.arange(K, dtype=jnp.int32)[None, None, :]
    leading = (slot_place % SLOTS == 0) & (within < 3)
    peer = jnp.where(leading, peer_forced, peer_random)
    entry = jnp.where(leading & (within == 0), CAP - 1, entry_random)
    far = 3 * RES + peer * CAP + entry
    picked = jax.random.randint(key_pick, shape, 0, 4) == 0
    return jnp.where(leading | picked, far, near).astype(jnp.int32)


def draw_slot_live(key, part):
    key = jax.random.fold_in(key, 23)
    key_rows, key_slots = jax.random.split(key, 2)
    real_rows = jax.random.randint(key_rows, (MB, N_SPACE, 1), RES // 2, RES + 1)
    within = (jnp.arange(NODES, dtype=jnp.int32) % RES).reshape(1, N_SPACE, RES)
    row_live = (within < real_rows).reshape(MB, NODES, 1)
    slot_on = jax.random.randint(key_slots, (MB, NODES, K), 0, 10) > 0
    return (row_live & slot_on).astype(jnp.int32)


def place_ends(values, own_key, low, high):
    place = [jax.random.randint(jax.random.fold_in(own_key, axis), (), 0, length) for axis, length in enumerate(values.shape)]
    main_axis = values.shape.index(max(values.shape))
    beside = place[:main_axis] + [(place[main_axis] + 1) % values.shape[main_axis]] + place[main_axis + 1:]
    return values.at[tuple(place)].set(low).at[tuple(beside)].set(high)


def steps_of(stream_key, dims, cuts, smallest, high):
    def one(dim, shards_of):
        draws = jax.random.uniform(jax.random.fold_in(jax.random.fold_in(stream_key, 6), dim), (shards_of,), jnp.float32, smallest / len(cuts), high / len(cuts))
        return jnp.repeat(jnp.exp(draws), dims[dim] // shards_of).reshape((-1,) + (1,) * (len(dims) - dim - 1))

    level = one(*cuts[0])
    for cut in cuts[1:]:
        level = level * one(*cut)
    return level


def bell_draw(own_key, extent, scale, most, shards=(), held_as=jnp.bfloat16):
    level = steps_of(own_key, extent, shards, -0.22, 0.18) if shards else 1.0
    values = jax.random.normal(own_key, extent, jnp.float32) * scale * level
    return jnp.minimum(jnp.maximum(values, -most), most).astype(held_as)


def setup_inputs(seed: int = 0) -> dict:
    arg_keys = jax.random.split(jax.random.key(seed), 30)
    nodes = bell_draw(arg_keys[0], (MB, NODES, DN), 1.0, 6.0, ((1, 8),))
    edges = bell_draw(arg_keys[1], (MB, NODES, K, DE), 1.0, 6.0, ((1, 8), (2, 4)))
    neighbors = draw_neighbors(jax.random.fold_in(arg_keys[29], 71), 0)
    slot_live = draw_slot_live(jax.random.fold_in(arg_keys[29], 71), 0)
    send_rows = place_ends(jax.random.randint(arg_keys[4], (MB, PEERS, CAP), 0, RES), jax.random.fold_in(arg_keys[4], 1), 0, RES - 1).astype(jnp.int32)
    message_self = bell_draw(arg_keys[5], (DN, DN), DN ** -0.5, 0.25)
    message_peer = bell_draw(arg_keys[6], (DN, DN), DN ** -0.5, 0.25)
    message_edge = bell_draw(arg_keys[7], (DE, DN), DE ** -0.5, 0.4375)
    message_bias = bell_draw(arg_keys[8], (DN,), 0.3, 1.75)
    message_out = bell_draw(arg_keys[9], (DN, DN), DN ** -0.5, 0.25)
    message_shift = bell_draw(arg_keys[10], (DN,), 0.3, 1.75)
    first_gain = jnp.clip(1.0 + 0.1 * jax.random.normal(arg_keys[11], (DN,), jnp.float32), 0.5, 1.5).astype(jnp.bfloat16)
    first_shift = bell_draw(arg_keys[12], (DN,), 0.3, 1.75)
    hidden_in = bell_draw(arg_keys[13], (DN, FF), DN ** -0.5, 0.25)
    hidden_bias = bell_draw(arg_keys[14], (FF,), 0.3, 1.75)
    hidden_out = bell_draw(arg_keys[15], (FF, DN), FF ** -0.5, 0.125)
    output_bias = bell_draw(arg_keys[16], (DN,), 0.3, 1.75)
    second_gain = jnp.clip(1.0 + 0.1 * jax.random.normal(arg_keys[17], (DN,), jnp.float32), 0.5, 1.5).astype(jnp.bfloat16)
    second_shift = bell_draw(arg_keys[18], (DN,), 0.3, 1.75)
    edge_self = bell_draw(arg_keys[19], (DN, DE), DN ** -0.5, 0.25)
    edge_peer = bell_draw(arg_keys[20], (DN, DE), DN ** -0.5, 0.25)
    edge_own = bell_draw(arg_keys[21], (DE, DE), DE ** -0.5, 0.4375)
    edge_bias = bell_draw(arg_keys[22], (DE,), 0.3, 1.75)
    edge_out = bell_draw(arg_keys[23], (DE, DE), DE ** -0.5, 0.4375)
    edge_shift = bell_draw(arg_keys[24], (DE,), 0.3, 1.75)
    third_gain = jnp.clip(1.0 + 0.1 * jax.random.normal(arg_keys[25], (DE,), jnp.float32), 0.5, 1.5).astype(jnp.bfloat16)
    third_shift = bell_draw(arg_keys[26], (DE,), 0.3, 1.75)
    node_cot = bell_draw(arg_keys[27], (MB, NODES, DN), 1.0, 6.0, ((1, 8),))
    edge_cot = bell_draw(arg_keys[28], (MB, NODES, K, DE), 1.0, 6.0, ((1, 8), (2, 4)))
    return {"nodes": nodes, "edges": edges, "neighbors": neighbors, "slot_live": slot_live, "send_rows": send_rows, "message_self": message_self, "message_peer": message_peer, "message_edge": message_edge, "message_bias": message_bias, "message_out": message_out, "message_shift": message_shift, "first_gain": first_gain, "first_shift": first_shift, "hidden_in": hidden_in, "hidden_bias": hidden_bias, "hidden_out": hidden_out, "output_bias": output_bias, "second_gain": second_gain, "second_shift": second_shift, "edge_self": edge_self, "edge_peer": edge_peer, "edge_own": edge_own, "edge_bias": edge_bias, "edge_out": edge_out, "edge_shift": edge_shift, "third_gain": third_gain, "third_shift": third_shift, "node_cot": node_cot, "edge_cot": edge_cot}


EPS = 1e-05
HIGH = lax.Precision.HIGHEST

@jax.custom_vjp
def low(v):
    return lax.optimization_barrier(v.astype(jnp.bfloat16)).astype(jnp.float32)

@jax.custom_vjp
def low_back(v):
    return v

def low_keep(v):
    return (low(v), None)

def low_pass(kept, grad):
    return (grad,)

def back_keep(v):
    return (v, None)

def back_low(kept, grad):
    return (low(grad),)
low.defvjp(low_keep, low_pass)
low_back.defvjp(back_keep, back_low)

def product(left, right):
    return jnp.dot(left, right, precision=HIGH, preferred_element_type=jnp.float32)

def slot_product(left, right):
    return jnp.einsum('nsc,cd->nsd', left, right, precision=HIGH)

def norm_apply(value, gain, shift):
    centre = value - lax.optimization_barrier(jnp.mean(value, -1, keepdims=True))
    spread = lax.optimization_barrier(jnp.mean(centre * centre, -1, keepdims=True))
    return centre * lax.rsqrt(spread + EPS) * gain + shift

def smooth(value):
    return jax.nn.gelu(value)

def neighbor_rows(neighbors, send_rows):
    rows = jnp.arange(NODES, dtype=jnp.int32)
    block = (rows // RES)[:, None]
    near = (block - 1) * RES + neighbors
    offset = jnp.maximum(neighbors - 3 * RES, 0)
    source_block = offset // CAP
    entry = offset % CAP
    far = source_block * RES + send_rows[source_block * N_SPACE + block, entry]
    return jnp.where(neighbors < 3 * RES, near, far).astype(jnp.int32)

def message_group(self_term, peer_term, edge_block, index_block, live_block, message_edge, message_bias, message_out, message_shift):
    inner = low_back(self_term[:, None, :] + peer_term[index_block] + slot_product(edge_block, message_edge) + message_bias)
    active = low(smooth(inner))
    message = low_back(slot_product(active, message_out) + message_shift)
    return lax.optimization_barrier(jnp.sum(message * live_block[:, :, None], 1))

def edge_group(self_term, peer_term, edge_block, index_block, edge_own, edge_bias, edge_out, edge_shift, third_gain, third_shift):
    inner = low_back(self_term[:, None, :] + peer_term[index_block] + slot_product(edge_block, edge_own) + edge_bias)
    active = low(smooth(inner))
    update = low_back(slot_product(active, edge_out) + edge_shift)
    return norm_apply(edge_block + update, third_gain, third_shift)

def forward_one(nodes_f, edges_f, index, live, params):
    message_self, message_peer, message_edge, message_bias, message_out, message_shift, first_gain, first_shift, hidden_in, hidden_bias, hidden_out, output_bias, second_gain, second_shift, edge_self, edge_peer, edge_own, edge_bias, edge_out, edge_shift, third_gain, third_shift = params
    message_fn = jax.checkpoint(message_group)
    edge_fn = jax.checkpoint(edge_group)
    self_term = product(nodes_f, message_self)
    peer_term = low(product(nodes_f, message_peer))
    summed = jnp.zeros((NODES, DN), jnp.float32)
    for member in range(N_NBR):
        window = slice(member * SLOTS, (member + 1) * SLOTS)
        summed = summed + message_fn(low_back(self_term), low_back(peer_term), edges_f[:, window], index[:, window], live[:, window], message_edge, message_bias, message_out, message_shift)
    counted = lax.optimization_barrier(jnp.sum(live, 1))
    updated = nodes_f + summed / jnp.maximum(counted, 1.0)[:, None]
    node_hidden = norm_apply(updated, first_gain, first_shift)
    ffn_in = low_back(product(low(node_hidden), hidden_in) + hidden_bias)
    ffn_out = low_back(product(low(smooth(ffn_in)), hidden_out) + output_bias)
    node_final = norm_apply(node_hidden + ffn_out, second_gain, second_shift)
    final_low = low(node_final)
    edge_self_term = product(final_low, edge_self)
    edge_peer_term = low(product(final_low, edge_peer))
    pieces = []
    for member in range(N_NBR):
        window = slice(member * SLOTS, (member + 1) * SLOTS)
        pieces.append(edge_fn(low_back(edge_self_term), low_back(edge_peer_term), edges_f[:, window], index[:, window], edge_own, edge_bias, edge_out, edge_shift, third_gain, third_shift))
    return (node_final, jnp.concatenate(pieces, 1))

def reference(nodes, edges, neighbors, slot_live, send_rows, message_self, message_peer, message_edge, message_bias, message_out, message_shift, first_gain, first_shift, hidden_in, hidden_bias, hidden_out, output_bias, second_gain, second_shift, edge_self, edge_peer, edge_own, edge_bias, edge_out, edge_shift, third_gain, third_shift, node_cot, edge_cot):
    params = tuple((value.astype(jnp.float32) for value in (message_self, message_peer, message_edge, message_bias, message_out, message_shift, first_gain, first_shift, hidden_in, hidden_bias, hidden_out, output_bias, second_gain, second_shift, edge_self, edge_peer, edge_own, edge_bias, edge_out, edge_shift, third_gain, third_shift)))
    index = jax.vmap(neighbor_rows)(neighbors, send_rows)
    live = slot_live.astype(jnp.float32)

    def whole(nodes_v, edges_v, params_v):
        node_list = []
        edge_list = []
        for sample in range(MB):
            node_out, edge_out_v = forward_one(nodes_v[sample], edges_v[sample], index[sample], live[sample], params_v)
            node_list.append(node_out)
            edge_list.append(edge_out_v)
        return (jnp.stack(node_list), jnp.stack(edge_list))
    primal, backward = jax.vjp(whole, nodes.astype(jnp.float32), edges.astype(jnp.float32), params)
    node_in_grad, edge_in_grad, grads = backward((node_cot.astype(jnp.float32), edge_cot.astype(jnp.float32)))
    return (primal[0].astype(jnp.bfloat16), primal[1].astype(jnp.bfloat16), node_in_grad, edge_in_grad.astype(jnp.bfloat16), grads[0], grads[1], grads[2], grads[3], grads[4], grads[5], grads[6], grads[7], grads[8], grads[9], grads[10], grads[11], grads[12], grads[13], grads[14], grads[15], grads[16], grads[17], grads[18], grads[19], grads[20], grads[21])
```

```python
import itertools
from types import SimpleNamespace

import jax
import jax.numpy as jnp
from jax import lax
from jax.experimental import pallas as pl
from jax.experimental.pallas import tpu as pltpu
from jax.sharding import PartitionSpec as P

EPS = 1e-05
F32 = jnp.float32
BF = jnp.bfloat16
MESH = pl.DeviceIdType.MESH
VMEM_LIMIT = 62 << 20
C0 = 0.7978845608028654
C1 = C0 * 0.044715
GROUP = 3
LANES = 128
SPLITS = 5


def dot(left, right):
    return jnp.dot(left, right, preferred_element_type=F32)


def dot_nt(left, right):
    return lax.dot_general(left, right, (((1,), (1,)), ((), ())), preferred_element_type=F32)


def dot_tn(left, right):
    return lax.dot_general(left, right, (((0,), (0,)), ((), ())), preferred_element_type=F32)


def gelu_both(x):
    x2 = x * x
    half = 0.5 * jnp.tanh(x * (C0 + C1 * x2)) + 0.5
    act = x * half
    return act, half + act * (1.0 - half) * (2 * C0 + 6 * C1 * x2)


def norm_rows(value):
    centre = value - jnp.mean(value, -1, keepdims=True)
    rstd = lax.rsqrt(jnp.mean(centre * centre, -1, keepdims=True) + EPS)
    return centre * rstd, rstd


def norm_rows_back(xhat, rstd, grad):
    return rstd * (
        grad
        - jnp.mean(grad, -1, keepdims=True)
        - xhat * jnp.mean(grad * xhat, -1, keepdims=True)
    )


def hot(index, rows):
    it = lax.broadcasted_iota(jnp.int32, (rows, index.shape[1]), 0)
    return jnp.where(it == index, 1.0, 0.0).astype(BF)


def side(refs):
    return jnp.concatenate(refs, 1)


def row_sum(value):
    return jnp.sum(value, 0, keepdims=True)


def vm(array):
    return (array, pl.BlockSpec(memory_space=pltpu.VMEM))


def out(shape, dtype):
    return (jax.ShapeDtypeStruct(shape, dtype), pl.BlockSpec(memory_space=pltpu.VMEM))


def dma(*shape):
    return pltpu.SemaphoreType.DMA(shape)


def remote(src, dst, send, recv, device):
    return pltpu.make_async_remote_copy(
        src_ref=src, dst_ref=dst, send_sem=send, recv_sem=recv, device_id=device, device_id_type=MESH
    )


def build(ids, parts, partners, steps, before, after):
    ins, outs, scr, bodies = {}, {}, {}, []
    for part in parts:
        ins.update(part.ins)
        outs.update(part.outs)
        scr.update(part.scr)
        if hasattr(part, "body"):
            bodies.append(part.body)
    names = list(ins) + list(outs) + list(scr)

    def kernel(*refs):
        e = SimpleNamespace(**dict(zip(names, refs, strict=True)))
        step = pl.program_id(0)

        def enter():
            barrier = pltpu.get_barrier_semaphore()
            devices = partners()
            for device in devices:
                pl.semaphore_signal(barrier, inc=1, device_id=device, device_id_type=MESH)
            pl.semaphore_wait(barrier, len(devices))

        def run(listed):
            for stage in listed:
                stage(e)

        for t in range(steps):
            if t == 0 or t in before:

                @pl.when(step == t)
                def _(t=t):
                    if t == 0:
                        enter()
                    run(before.get(t, ()))

        for body in bodies:
            body(e, step)
        for t in sorted(after):
            pl.when(step == t)(lambda t=t: run(after[t]))

    got = pl.pallas_call(
        kernel,
        grid=(steps,),
        out_shape=[shape for shape, _ in outs.values()],
        in_specs=[spec for _, spec in ins.values()],
        out_specs=[spec for _, spec in outs.values()],
        scratch_shapes=list(scr.values()),
        compiler_params=pltpu.CompilerParams(
            vmem_limit_bytes=VMEM_LIMIT, collective_id=next(ids), has_side_effects=True
        ),
    )(*[array for array, _ in ins.values()])
    return SimpleNamespace(**dict(zip(outs, got, strict=True)))


def place():
    return lax.axis_index("space"), lax.axis_index("nbr")


def wrap(value, count):
    return lax.rem(value + count, count)


def flip(value, bit):
    return value + (1 - 2 * (lax.rem(value // (1 << bit), 2))) * (1 << bit)


def across(axis, bit):
    s, n = place()
    return (s, flip(n, bit)) if axis == "nbr" else (flip(s, bit), n)


def near_cross(z):
    s, n = place()
    found = [(s, wrap(n + k, z.nn)) for k in range(1, z.nn)]
    sides = (1, -1) if z.ns > 2 else (1,)
    return found + [(wrap(s + d, z.ns), wrap(n + k, z.nn)) for d in sides for k in range(1, z.nn)]


def same_lane(z):
    s, n = place()
    return [(wrap(s + k, z.ns), n) for k in range(1, z.ns)]


def quarter(z):
    s, n = place()
    return pl.ds(pl.multiple_of(n * z.Q, 16), z.Q)


def far_copies(z, send, recv, fs, fr):
    s, n = place()
    found = []
    for k in range(1, z.ns):
        p = wrap(s + k, z.ns)
        found.append(
            remote(
                send.at[pl.ds(p * z.CAP, z.CAP)], recv.at[pl.ds(s * z.CAP, z.CAP)], fs.at[k], fr.at[k], (p, n)
            )
        )
    return found


def far_own(z, send, recv):
    s, n = place()
    here = pl.ds(pl.multiple_of(s * z.CAP, 8), z.CAP)
    recv[here] = send[here]


def setup_part(z, a):
    lines = (
        a.message_bias,
        a.edge_bias,
        a.edge_shift,
        a.third_gain,
        a.third_shift,
        a.message_shift,
        a.first_gain,
        a.first_shift,
        a.output_bias,
        a.second_gain,
        a.second_shift,
    )
    at = (0, 1, 2, 3, 4, 8, 9, 10, 11, 12, 13)

    def begin(e):
        e.vecs[...] = jnp.zeros_like(e.vecs)
        given = (e.va, e.vb, e.vc, e.vd, e.ve, e.vf, e.vg, e.vh, e.vi, e.vj, e.vk)
        for row, line in zip(at, given, strict=True):
            wide = line.shape[0]
            e.vecs[row : row + 1, 0:wide] = line[...].astype(F32).reshape(1, wide)
        hidden = e.vl[...].astype(F32).reshape(1, z.FF)
        for k in range(z.FF // z.DN):
            e.vecs[16 + k : 17 + k] = hidden[:, k * z.DN : (k + 1) * z.DN]
        p = lax.broadcasted_iota(jnp.int32, (z.CAP, z.FAR), 0)
        q = lax.broadcasted_iota(jnp.int32, (z.CAP, z.FAR), 1)
        spread = jnp.where(lax.rem(q, z.CAP) == p, 1.0, 0.0)
        b = lax.broadcasted_iota(jnp.int32, (z.ns, z.FAR), 0)
        c = lax.broadcasted_iota(jnp.int32, (z.ns, z.FAR), 1)
        for k in range(z.B):
            wide = jnp.dot(
                e.send_rows[k].astype(F32), spread, precision=lax.Precision.HIGHEST, preferred_element_type=F32
            )
            e.send[k] = (row_sum(jnp.where(c // z.CAP == b, wide, 0.0)) + 0.5).astype(jnp.int32)

    given = dict(zip("abcdefghijkl", lines + (a.hidden_bias,)))
    return SimpleNamespace(
        begin=begin,
        ins=dict({"v" + k: vm(v) for k, v in given.items()}, send_rows=vm(a.send_rows)),
        outs=dict(vecs=out((24, z.DN), F32), send=out((z.B, 1, z.FAR), jnp.int32)),
        scr={},
    )


def table_part(z, a):
    R, DN, FAR, TP, ns, B = z.R, z.DN, z.FAR, z.TP, z.ns, z.B
    half = R // 2

    def far(e, b):
        return far_copies(z, e.t_fsend.at[b], e.t_frecv.at[b], e.t_fs.at[b], e.t_fr.at[b])

    def near(e, b):
        s, n = place()
        h = pl.multiple_of(lax.rem(n, 2) * half, 16)
        src = e.nodes.at[b, pl.ds(h, half)]
        return [
            remote(
                src, e.t_tab.at[b, pl.ds(base + h, half)], e.t_ns.at[b, k], e.t_nr.at[b, k], (wrap(s + step, ns), n)
            )
            for k, (step, base) in enumerate(((1, 0), (-1, 2 * R)))
        ]

    def mate(e, b):
        s, n = place()
        h = pl.multiple_of(lax.rem(n, 2) * half, 16)
        found = []
        for k, base in enumerate((0, 2 * R)):
            rows = e.t_tab.at[b, pl.ds(base + h, half)]
            found.append(remote(rows, rows, e.t_ms.at[b, k], e.t_mr.at[b, k], (s, flip(n, 0))))
        return found

    def begin(b):
        def stage(e):
            for copy in near(e, b):
                copy.start()
            own = e.nodes[b]
            e.t_fsend[b] = dot_tn(hot(e.send[b], R), own)
            for copy in far(e, b):
                copy.start()
            e.t_tab[b, R : 2 * R] = own
            if TP > 3 * R + FAR:
                e.t_tab[b, 3 * R + FAR :] = jnp.zeros((TP - 3 * R - FAR, DN), BF)

        return stage

    def middle(b):
        def stage(e):
            for one, two in zip(near(e, b), mate(e, b), strict=True):
                one.wait_recv()
                two.start()

        return stage

    def finish(b):
        def stage(e):
            far_own(z, e.t_fsend.at[b], e.t_frecv.at[b])
            for copy in far(e, b):
                copy.wait()
            for copy in near(e, b):
                copy.wait_send()
            for copy in mate(e, b):
                copy.wait()
            e.t_tab[b, 3 * R : 3 * R + FAR] = e.t_frecv[b].astype(BF)
            e.tables[b] = e.t_tab[b]

        return stage

    return SimpleNamespace(
        begin=begin,
        middle=middle,
        finish=finish,
        ins=dict(nodes=vm(a.nodes)),
        outs=dict(tables=out((B, TP, DN), BF)),
        scr=dict(
            t_tab=pltpu.VMEM((B, TP, DN), BF),
            t_fsend=pltpu.VMEM((B, FAR, DN), F32),
            t_frecv=pltpu.VMEM((B, FAR, DN), F32),
            t_fs=dma(B, ns),
            t_fr=dma(B, ns),
            t_ns=dma(B, 2),
            t_nr=dma(B, 2),
            t_ms=dma(B, 2),
            t_mr=dma(B, 2),
        ),
    )


def message_part(z, a):
    R, DN, DE, TP, S, B = z.R, z.DN, z.DE, z.TP, z.S, z.B
    T = S // GROUP

    def body(e, step):
        sample, own = step // T, lax.rem(step, T)

        @pl.when(step == 0)
        def _():
            e.m_wst[...] = e.w_self[...].T
            e.m_wpt[...] = e.w_peer[...].T
            e.m_wet[...] = e.w_edge[...].T

        @pl.when(own == 0)
        def _():
            e.m_tabt[...] = dot_nt(e.m_wpt[...], e.t_tab[sample]).astype(BF)
            e.m_selft[...] = dot_nt(e.m_wst[...], e.nodes[sample]) + e.vecs[0:8].T[:, 0:1]
            e.m_acc[...] = jnp.zeros_like(e.m_acc)

        slots = [own * GROUP + g for g in range(GROUP)]
        line = pl.ds(sample, 1)
        value = dot(e.m_tabt[...], hot(side([e.nbr[s, line] for s in slots]), TP)) + dot(
            e.m_wet[...], side([e.m_edges[0, g] for g in range(GROUP)])
        )
        acc = e.m_acc[0:DN]
        count = e.m_acc[DN:]
        for g, s in enumerate(slots):
            live = e.live[s, line].astype(F32)
            act, slope = gelu_both(value[:, g * R : (g + 1) * R] + e.m_selft[...])
            e.slope[0, g] = slope.astype(BF)
            acc = acc + act * live
            count = count + live
        e.m_acc[0:DN] = acc
        e.m_acc[DN:] = count
        for b, ref in enumerate((e.part_a, e.part_b)):

            @pl.when(step == (b + 1) * T - 1)
            def _(ref=ref):
                ref[...] = e.m_acc[...].T.astype(BF)

    return SimpleNamespace(
        body=body,
        ins=dict(
            nodes=vm(a.nodes),
            m_edges=(a.edges_t, pl.BlockSpec((1, GROUP, DE, R), lambda i: (i // T, lax.rem(i, T), 0, 0))),
            nbr=vm(a.nbr),
            live=vm(a.live),
            w_self=vm(a.message_self),
            w_peer=vm(a.message_peer),
            w_edge=vm(a.message_edge),
        ),
        outs=dict(
            slope=(
                jax.ShapeDtypeStruct((B, S, DN, R), BF),
                pl.BlockSpec((1, GROUP, DN, R), lambda i: (i // T, lax.rem(i, T), 0, 0)),
            ),
            part_b=out((R, DN + LANES), BF),
        ),
        scr=dict(
            part_a=pltpu.VMEM((R, DN + LANES), BF),
            m_tabt=pltpu.VMEM((DN, TP), BF),
            m_selft=pltpu.VMEM((DN, R), F32),
            m_wst=pltpu.VMEM((DN, DN), BF),
            m_wpt=pltpu.VMEM((DN, DN), BF),
            m_wet=pltpu.VMEM((DN, DE), BF),
            m_acc=pltpu.VMEM((DN + LANES, R), F32),
        ),
    )


def forward_part(z, a, b, part):
    R, DN, DE, FF, Q, FAR, TP, ns, nn = z.R, z.DN, z.DE, z.FF, z.Q, z.FAR, z.TP, z.ns, z.nn
    W = DN + LANES

    def sums(e):
        s, n = place()
        found = []
        for k in range(1, nn):
            q = wrap(n + k, nn)
            rows = pl.ds(pl.multiple_of(q * Q, 16), Q)
            found.append(remote(part(e).at[rows], e.f_sum.at[k], e.f_ss.at[k], e.f_sr.at[k], (s, q)))
        return found

    def alls(e):
        s, n = place()
        rows = e.f_new.at[quarter(z)]
        return [
            remote(rows, rows, e.f_as.at[k], e.f_ar.at[k], (s, wrap(n + k, nn))) for k in range(1, nn)
        ]

    def near(e):
        s, n = place()
        found = []
        for i, (step, base) in enumerate(((1, 0), (-1, 2 * R))):
            rows = pl.ds(pl.multiple_of(base + n * Q, 16), Q)
            for k in range(nn):
                to = (wrap(s + step, ns), wrap(n + k, nn))
                found.append(remote(e.f_pe, e.f_tab.at[rows], e.f_ns.at[i, k], e.f_nr.at[i, k], to))
        return found

    def far(e):
        return far_copies(z, e.f_fsend, e.f_frecv, e.f_fs, e.f_fr)

    def begin(e):
        for copy in sums(e):
            copy.start()

    def compute(e):
        mine = quarter(z)
        for copy in sums(e):
            copy.wait()
        total = part(e)[mine].astype(F32)
        for k in range(1, nn):
            total = total + e.f_sum[k].astype(F32)
        count = total[:, DN : DN + 1]
        summed_act = total[:, :DN].astype(BF)
        summed = dot(summed_act, e.w_out[...]) + count * e.vecs[8:9]
        updated = e.nodes[b, mine].astype(F32) + summed / jnp.maximum(count, 1.0)
        xhat1, rstd1 = norm_rows(updated)
        hidden = xhat1 * e.vecs[9:10] + e.vecs[10:11]
        low = hidden.astype(BF)
        bias = side([e.vecs[16 + k : 17 + k] for k in range(FF // DN)])
        act, slope = gelu_both(dot(low, e.w_in[...]) + bias)
        act = act.astype(BF)
        xhat2, rstd2 = norm_rows(hidden + dot(act, e.w_ffn[...]) + e.vecs[11:12])
        fresh = (xhat2 * e.vecs[12:13] + e.vecs[13:14]).astype(BF)
        e.f_new[mine] = fresh
        e.f_pe[...] = dot_nt(fresh, e.ept[...]).astype(BF)
        for copy in alls(e):
            copy.start()
        for copy in near(e):
            copy.start()
        e.f_osum[...] = summed_act
        e.f_ocount[...] = total[:, DN:]
        e.f_ox1[...] = xhat1
        e.f_or1[...] = jnp.broadcast_to(rstd1, (Q, LANES))
        e.f_olow[...] = low
        e.f_oslope[...] = slope.astype(BF)
        e.f_oact[...] = act
        e.f_ox2[...] = xhat2
        e.f_or2[...] = jnp.broadcast_to(rstd2, (Q, LANES))
        e.f_oq[...] = fresh

    def spread(e):
        for copy in alls(e):
            copy.wait()
        own = dot_nt(e.f_new[...], e.ept[...]).astype(BF)
        e.f_tab[R : 2 * R] = own
        e.f_fsend[...] = dot_tn(hot(e.send[b], R), own)
        for copy in far(e):
            copy.start()
        e.f_onew[...] = e.f_new[...]
        if TP > 3 * R + FAR:
            e.f_tab[3 * R + FAR :] = jnp.zeros((TP - 3 * R - FAR, DE), BF)

    def finish(e):
        far_own(z, e.f_fsend, e.f_frecv)
        for copy in near(e):
            copy.wait()
        for copy in far(e):
            copy.wait()
        e.f_tab[3 * R : 3 * R + FAR] = e.f_frecv[...].astype(BF)
        e.f_otab[...] = e.f_tab[...]

    return SimpleNamespace(
        begin=begin,
        compute=compute,
        spread=spread,
        finish=finish,
        ins=dict(
            nodes=vm(a.nodes),
            w_out=vm(a.message_out),
            w_in=vm(a.hidden_in),
            w_ffn=vm(a.hidden_out),
            ept=vm(a.edge_peer_t),
        ),
        outs=dict(
            f_onew=out((R, DN), BF),
            f_otab=out((TP, DE), BF),
            f_osum=out((Q, DN), BF),
            f_ocount=out((Q, LANES), F32),
            f_ox1=out((Q, DN), F32),
            f_or1=out((Q, LANES), F32),
            f_olow=out((Q, DN), BF),
            f_oslope=out((Q, FF), BF),
            f_oact=out((Q, FF), BF),
            f_ox2=out((Q, DN), F32),
            f_or2=out((Q, LANES), F32),
            f_oq=out((Q, DN), BF),
        ),
        scr=dict(
            f_sum=pltpu.VMEM((nn, Q, W), BF),
            f_new=pltpu.VMEM((R, DN), BF),
            f_pe=pltpu.VMEM((Q, DE), BF),
            f_tab=pltpu.VMEM((TP, DE), BF),
            f_fsend=pltpu.VMEM((FAR, DE), F32),
            f_frecv=pltpu.VMEM((FAR, DE), F32),
            f_ss=dma(nn),
            f_sr=dma(nn),
            f_as=dma(nn),
            f_ar=dma(nn),
            f_ns=dma(2, nn),
            f_nr=dma(2, nn),
            f_fs=dma(ns),
            f_fr=dma(ns),
        ),
    )


def edge_part(z, a, first):
    R, DN, DE, TP, S, FAR, B = z.R, z.DN, z.DE, z.TP, z.S, z.FAR, z.B
    T = S // GROUP

    def body(e, step):
        sample, own = step // T, lax.rem(step, T)

        @pl.when(step == 0)
        def _():
            e.e_cols[...] = e.vecs[0:8].T[:DE]
            e.e_wnt[...] = e.e_wn[...].astype(F32).T.astype(BF)
            e.e_wot[...] = e.e_wo[...].astype(F32).T.astype(BF)
            for ref in (e.e_gacc, e.e_hacc, e.e_uacc, e.e_vacc, e.e_dwo, e.e_dwn):
                ref[...] = jnp.zeros_like(ref)

        for b, (table, fresh) in enumerate(((e.a_tab, e.a_new), (e.f_tab, e.f_new))):

            @pl.when(step == b * T)
            def _(table=table, fresh=fresh):
                e.e_tabt[...] = table[...].astype(F32).T.astype(BF)
                e.e_selft[...] = dot_nt(e.est[...], fresh[...]) + e.e_cols[:, 1:2]
                e.e_ptab[...] = jnp.zeros_like(e.e_ptab)
                e.e_sacc[...] = jnp.zeros_like(e.e_sacc)

        line = pl.ds(sample, 1)
        index = hot(side([e.nbr[own * GROUP + g, line] for g in range(GROUP)]), TP)
        edge = side([e.m_edges[0, g] for g in range(GROUP)])
        value = dot(e.e_tabt[...], index) + dot(e.e_wnt[...], edge)
        value = value + side([e.e_selft[...]] * GROUP)
        act, slope = gelu_both(value)
        act = act.astype(BF)
        shift_c, gain_c, bias_c = e.e_cols[:, 2:3], e.e_cols[:, 3:4], e.e_cols[:, 4:5]
        full = edge.astype(F32) + dot(e.e_wot[...], act) + shift_c
        full = full - jnp.mean(full, 0, keepdims=True)
        rstd = lax.rsqrt(jnp.mean(full * full, 0, keepdims=True) + EPS)
        xhat = full * rstd
        final = (xhat * gain_c + bias_c).astype(BF)
        cot = side([e.e_cot[0, g] for g in range(GROUP)]).astype(F32)
        scaled = cot * gain_c
        back = rstd * (
            scaled - jnp.mean(scaled, 0, keepdims=True) - xhat * jnp.mean(scaled * xhat, 0, keepdims=True)
        )
        low = back.astype(BF)
        e.e_dwo[...] += dot_nt(act, low)
        inner = (slope * dot(e.e_wo[...], low)).astype(BF)
        e.e_dwn[...] += dot_nt(edge, inner)
        part = (back + dot(e.e_wn[...], inner)).astype(BF)
        e.e_ptab[...] += dot_nt(inner, index)
        gain_g = cot * xhat
        low_f = low.astype(F32)
        inner_f = inner.astype(F32)
        s_acc, g_acc, h_acc, u_acc = e.e_sacc[...], e.e_gacc[...], e.e_hacc[...], e.e_uacc[...]
        for g in range(GROUP):
            cut = slice(g * R, (g + 1) * R)
            e.e_final[0, g] = final[:, cut]
            e.e_part[0, g] = part[:, cut]
            s_acc = s_acc + inner_f[:, cut]
            g_acc = g_acc + gain_g[:, cut]
            h_acc = h_acc + cot[:, cut]
            u_acc = u_acc + low_f[:, cut]
        e.e_sacc[...] = s_acc
        e.e_gacc[...] = g_acc
        e.e_hacc[...] = h_acc
        e.e_uacc[...] = u_acc
        ends = ((e.a_tgrad, e.a_fgrad, e.a_sgrad), (e.e_tgrad, e.e_fgrad, e.e_sgrad))
        for b, (tgrad, fgrad, sgrad) in enumerate(ends):

            @pl.when(step == (b + 1) * T - 1)
            def _(tgrad=tgrad, fgrad=fgrad, sgrad=sgrad):
                rows = e.e_ptab[...].T
                tgrad[...] = rows.astype(BF)
                fgrad[...] = rows[3 * R : 3 * R + FAR]
                turned = e.e_sacc[...].T
                sgrad[...] = turned.astype(BF)
                e.e_vacc[0:1] += row_sum(turned)

        @pl.when(step == B * T - 1)
        def _():
            for k, ref in enumerate((e.e_uacc, e.e_gacc, e.e_hacc)):
                e.e_vacc[k + 1 : k + 2] = row_sum(ref[...].T)
            e.e_vgrad[...] = e.e_vacc[...]

    stream = pl.BlockSpec((1, GROUP, DE, R), lambda i: (i // T, lax.rem(i, T), 0, 0))
    return SimpleNamespace(
        body=body,
        ins=dict(
            a_tab=vm(first.f_otab),
            a_new=vm(first.f_onew),
            m_edges=(a.edges_t, stream),
            e_cot=(a.cot_t, stream),
            nbr=vm(a.nbr),
            est=vm(a.edge_self_t),
            e_wn=vm(a.edge_own),
            e_wo=vm(a.edge_out),
        ),
        outs=dict(
            e_final=(jax.ShapeDtypeStruct((B, S, DE, R), BF), stream),
            e_part=(jax.ShapeDtypeStruct((B, S, DE, R), BF), stream),
            e_tgrad=out((TP, DE), BF),
            e_fgrad=out((FAR, DE), F32),
            e_sgrad=out((R, DE), BF),
            e_vgrad=out((8, DE), F32),
            e_dwo=out((DE, DE), F32),
            e_dwn=out((DE, DE), F32),
        ),
        scr=dict(
            a_tgrad=pltpu.VMEM((TP, DE), BF),
            a_fgrad=pltpu.VMEM((FAR, DE), F32),
            a_sgrad=pltpu.VMEM((R, DE), BF),
            e_tabt=pltpu.VMEM((DE, TP), BF),
            e_cols=pltpu.VMEM((DE, 8), F32),
            e_selft=pltpu.VMEM((DE, R), F32),
            e_wnt=pltpu.VMEM((DE, DE), BF),
            e_wot=pltpu.VMEM((DE, DE), BF),
            e_ptab=pltpu.VMEM((DE, TP), F32),
            e_sacc=pltpu.VMEM((DE, R), F32),
            e_gacc=pltpu.VMEM((DE, R), F32),
            e_hacc=pltpu.VMEM((DE, R), F32),
            e_uacc=pltpu.VMEM((DE, R), F32),
            e_vacc=pltpu.VMEM((8, DE), F32),
        ),
    )


def backward_part(z, a, b, node, grads):
    R, DN, DE, FF, Q, FAR, TP, ns, nn = z.R, z.DN, z.DE, z.FF, z.Q, z.FAR, z.TP, z.ns, z.nn
    W = DN + LANES

    def near(e):
        s, n = place()
        tgrad = grads(e)[0]
        return [
            remote(
                tgrad.at[pl.ds(base, R)], e.b_near.at[k], e.b_ns.at[k], e.b_nr.at[k], (wrap(s + step, ns), n)
            )
            for k, (step, base) in enumerate(((-1, 0), (1, 2 * R)))
        ]

    def far(e):
        return far_copies(z, grads(e)[1], e.b_frecv, e.b_fs, e.b_fr)

    def sums(e):
        s, n = place()
        found = []
        for k in range(1, nn):
            q = wrap(n + k, nn)
            rows = pl.ds(pl.multiple_of(q * Q, 16), Q)
            found.append(remote(e.b_pair.at[:, rows], e.b_sum.at[k], e.b_ss.at[k], e.b_sr.at[k], (s, q)))
        return found

    def alls(e):
        s, n = place()
        rows = e.b_all.at[quarter(z)]
        return [
            remote(rows, rows, e.b_as.at[k], e.b_ar.at[k], (s, wrap(n + k, nn))) for k in range(1, nn)
        ]

    def begin(e):
        for copy in near(e):
            copy.start()
        for copy in far(e):
            copy.start()

    def gather(e):
        tgrad, fgrad, sgrad = grads(e)
        far_own(z, fgrad, e.b_frecv)
        for copy in near(e):
            copy.wait()
        for copy in far(e):
            copy.wait()
        peer = (
            tgrad[R : 2 * R].astype(F32)
            + e.b_near[0].astype(F32)
            + e.b_near[1].astype(F32)
            + dot(hot(e.send[b], R), e.b_frecv[...].astype(BF))
        )
        e.b_pair[0] = peer.astype(BF)
        e.b_pair[1] = sgrad[...]
        for copy in sums(e):
            copy.start()

    def compute(e):
        mine = quarter(z)
        for copy in sums(e):
            copy.wait()
        peer = e.b_pair[0, mine].astype(F32)
        own = e.b_pair[1, mine].astype(F32)
        for k in range(1, nn):
            peer = peer + e.b_sum[k, 0].astype(F32)
            own = own + e.b_sum[k, 1].astype(F32)
        peer = peer.astype(BF)
        own = own.astype(BF)
        final = e.cot[b, mine].astype(F32) + dot(own, e.est[...]) + dot(peer, e.ept[...])
        xhat2 = e.b_x2[...]
        mid = norm_rows_back(xhat2, e.b_r2[:, 0:1], final * e.vecs[12:13])
        mid_low = mid.astype(BF)
        ffn = (e.b_slope[...].astype(F32) * dot_nt(mid_low, e.w_ffn[...])).astype(BF)
        hidden = mid + dot_nt(ffn, e.w_in[...])
        xhat1 = e.b_x1[...]
        grad = norm_rows_back(xhat1, e.b_r1[:, 0:1], hidden * e.vecs[9:10])
        count = e.b_count[:, 0:1]
        low = (grad / jnp.maximum(count, 1.0)).astype(BF)
        e.b_all[mine] = side([low, e.b_count[...].astype(BF)])
        for copy in alls(e):
            copy.start()
        e.b_omid[...] = mid_low
        e.b_offn[...] = ffn
        e.b_olow[...] = low
        e.b_opeer[...] = peer
        e.b_oself[...] = own
        wide = row_sum(ffn.astype(F32))
        e.b_ovec[...] = jnp.concatenate(
            [
                row_sum(low.astype(F32) * count),
                row_sum(hidden * xhat1),
                row_sum(hidden),
                row_sum(mid_low.astype(F32)),
                row_sum(final * xhat2),
                row_sum(final),
            ]
            + [wide[:, k * DN : (k + 1) * DN] for k in range(FF // DN)]
            + [jnp.zeros((6, DN), F32)],
            0,
        )

    def finish(e):
        for copy in alls(e):
            copy.wait()
        e.b_oall[...] = e.b_all[...]

    return SimpleNamespace(
        begin=begin,
        gather=gather,
        compute=compute,
        finish=finish,
        ins=dict(
            b_count=vm(node.f_ocount),
            b_x1=vm(node.f_ox1),
            b_r1=vm(node.f_or1),
            b_slope=vm(node.f_oslope),
            b_x2=vm(node.f_ox2),
            b_r2=vm(node.f_or2),
            cot=vm(a.node_cot),
            w_in=vm(a.hidden_in),
            w_ffn=vm(a.hidden_out),
            est=vm(a.edge_self_t),
            ept=vm(a.edge_peer_t),
        ),
        outs=dict(
            b_oall=out((R, W), BF),
            b_omid=out((Q, DN), BF),
            b_offn=out((Q, FF), BF),
            b_olow=out((Q, DN), BF),
            b_opeer=out((Q, DE), BF),
            b_oself=out((Q, DE), BF),
            b_ovec=out((16, DN), F32),
        ),
        scr=dict(
            b_near=pltpu.VMEM((2, R, DE), BF),
            b_frecv=pltpu.VMEM((FAR, DE), F32),
            b_pair=pltpu.VMEM((2, R, DE), BF),
            b_sum=pltpu.VMEM((nn, 2, Q, DE), BF),
            b_all=pltpu.VMEM((R, W), BF),
            b_ns=dma(2),
            b_nr=dma(2),
            b_fs=dma(ns),
            b_fr=dma(ns),
            b_ss=dma(nn),
            b_sr=dma(nn),
            b_as=dma(nn),
            b_ar=dma(nn),
        ),
    )


def last_part(z, a, spread, slope, part, tables):
    R, DN, DE, TP, S, FAR, B = z.R, z.DN, z.DE, z.TP, z.S, z.FAR, z.B
    T = S // GROUP

    def body(e, step):
        sample, own = step // T, lax.rem(step, T)
        for b, ref in enumerate((e.a_all, e.b_all)):

            @pl.when(step == b * T)
            def _(ref=ref, b=b):
                pltpu.make_async_copy(e.g_tables.at[b], e.g_tab, e.g_ts.at[b]).start()
                e.g_ht[...] = dot_nt(e.w_out[...], ref[:, 0:DN])
                e.g_ptab[...] = jnp.zeros_like(e.g_ptab)
                e.g_sacc[...] = jnp.zeros_like(e.g_sacc)
                if b == 0:
                    e.g_dwe[...] = jnp.zeros_like(e.g_dwe)
                    e.g_vec[...] = jnp.zeros_like(e.g_vec)

        line = pl.ds(sample, 1)
        slots = [own * GROUP + g for g in range(GROUP)]
        index = hot(side([e.nbr[s, line] for s in slots]), TP)
        edge = side([e.m_edges[0, g] for g in range(GROUP)])
        inner = []
        acc = e.g_sacc[...]
        for g, s in enumerate(slots):
            piece = (e.g_slope[0, g].astype(F32) * (e.g_ht[...] * e.live[s, line].astype(F32))).astype(BF)
            acc = acc + piece.astype(F32)
            inner.append(piece)
        e.g_sacc[...] = acc
        inner = side(inner)
        e.g_ptab[...] += dot_nt(inner, index)
        e.g_dwe[...] += dot_nt(edge, inner)
        back = dot(e.w_edge[...], inner)
        for g in range(GROUP):
            e.g_edge[0, g] = (back[:, g * R : (g + 1) * R] + e.g_part[0, g].astype(F32)).astype(BF)
        for b in range(B):

            @pl.when(step == (b + 1) * T - 1)
            def _(b=b):
                self_t = e.g_sacc[...].astype(BF)
                peer_t = e.g_ptab[...].astype(BF)
                pltpu.make_async_copy(e.g_tables.at[b], e.g_tab, e.g_ts.at[b]).wait()
                dself = dot(self_t, e.nodes[b])
                dpeer = dot(peer_t, e.g_tab[...])
                e.g_dself[...] = dself if b == 0 else e.g_dself[...] + dself
                e.g_dpeer[...] = dpeer if b == 0 else e.g_dpeer[...] + dpeer
                e.g_vec[0:1] += row_sum(e.g_sacc[...].T)
                e.o_rows[b] = dot(e.w_peer[...], peer_t).astype(BF)
                e.o_rows[b, :, R : 2 * R] = (
                    dot(e.w_peer[...], peer_t[:, R : 2 * R]) + dot(e.w_self[...], self_t)
                ).astype(BF)

    stream = pl.BlockSpec((1, GROUP, DE, R), lambda i: (i // T, lax.rem(i, T), 0, 0))
    return SimpleNamespace(
        body=body,
        ins=dict(
            a_all=vm(spread),
            g_slope=(slope, pl.BlockSpec((1, GROUP, DN, R), lambda i: (i // T, lax.rem(i, T), 0, 0))),
            g_part=(part, stream),
            g_tables=(tables, pl.BlockSpec(memory_space=pl.ANY)),
            nodes=vm(a.nodes),
            m_edges=(a.edges_t, stream),
            nbr=vm(a.nbr),
            live=vm(a.live),
            w_self=vm(a.message_self),
            w_peer=vm(a.message_peer),
            w_edge=vm(a.message_edge),
            w_out=vm(a.message_out),
        ),
        outs=dict(g_edge=(jax.ShapeDtypeStruct((B, S, DE, R), BF), stream)),
        scr=dict(
            g_tab=pltpu.VMEM((TP, DN), BF),
            g_ts=dma(B),
            g_ht=pltpu.VMEM((DN, R), F32),
            g_ptab=pltpu.VMEM((DN, TP), F32),
            g_sacc=pltpu.VMEM((DN, R), F32),
            g_dself=pltpu.VMEM((DN, DN), F32),
            g_dpeer=pltpu.VMEM((DN, DN), F32),
            g_dwe=pltpu.VMEM((DE, DN), F32),
            g_vec=pltpu.VMEM((8, DN), F32),
            o_rows=pltpu.VMEM((B, DN, TP), BF),
        ),
    )


def nodes_part(z, a, spreads):
    R, DN, FAR, TP, ns, nn, B = z.R, z.DN, z.FAR, z.TP, z.ns, z.nn, z.B
    L = DN // nn

    def sums(e, b):
        s, n = place()
        found = []
        for k in range(1, nn):
            q = wrap(n + k, nn)
            rows = pl.ds(pl.multiple_of(q * L, 16), L)
            found.append(remote(e.o_rows.at[b, rows], e.o_sum.at[b, k - 1], e.o_ss.at[b, k], e.o_sr.at[b, k], (s, q)))
        return found

    def near(e, b):
        s, n = place()
        return [
            remote(
                e.o_send.at[b, pl.ds(2 * k * R, R)],
                e.o_near.at[b, k],
                e.o_ns.at[b, k],
                e.o_nr.at[b, k],
                (wrap(s + step, ns), n),
            )
            for k, step in enumerate((-1, 1))
        ]

    def far(e, b):
        return far_copies(z, e.o_fsend.at[b], e.o_frecv.at[b], e.o_fs.at[b], e.o_fr.at[b])

    def begin(b):
        def stage(e):
            for copy in sums(e, b):
                copy.start()

        return stage

    def middle(b):
        def stage(e):
            s, n = place()
            for copy in sums(e, b):
                copy.wait()
            total = e.o_rows[b, pl.ds(pl.multiple_of(n * L, 16), L)].astype(F32)
            for k in range(1, nn):
                total = total + e.o_sum[b, k - 1].astype(F32)
            turned = total.T
            e.o_send[b] = turned.astype(BF)
            e.o_fsend[b] = turned[3 * R : 3 * R + FAR]
            for copy in near(e, b):
                copy.start()
            for copy in far(e, b):
                copy.start()
            column = pl.ds(pl.multiple_of(n * L, L), L)
            spread = spreads(e)[b]
            count = spread[:, DN : DN + 1].astype(F32)
            e.o_grad[b] = turned[R : 2 * R] + spread[:, column].astype(F32) * jnp.maximum(count, 1.0)

        return stage

    def finish(b):
        def stage(e):
            far_own(z, e.o_fsend.at[b], e.o_frecv.at[b])
            for copy in near(e, b):
                copy.wait()
            for copy in far(e, b):
                copy.wait()
            e.o_grad[b] += (
                e.o_near[b, 0].astype(F32)
                + e.o_near[b, 1].astype(F32)
                + dot(hot(e.send[b], R), e.o_frecv[b].astype(BF))
            )

        return stage

    return SimpleNamespace(
        begin=begin,
        middle=middle,
        finish=finish,
        ins={},
        outs=dict(o_grad=out((B, R, L), F32)),
        scr=dict(
            o_sum=pltpu.VMEM((B, nn - 1, L, TP), BF),
            o_send=pltpu.VMEM((B, TP, L), BF),
            o_near=pltpu.VMEM((B, 2, R, L), BF),
            o_fsend=pltpu.VMEM((B, FAR, L), F32),
            o_frecv=pltpu.VMEM((B, FAR, L), F32),
            o_ss=dma(B, nn),
            o_sr=dma(B, nn),
            o_ns=dma(B, 2),
            o_nr=dma(B, 2),
            o_fs=dma(B, ns),
            o_fr=dma(B, ns),
        ),
    )


def cut(z, total, start):
    unit = 16 << SPLITS
    units = max(3, -(-total // unit))
    sizes = [units // 3 + (1 if k < units % 3 else 0) for k in range(3)]
    starts = [start + sum(sizes[:k]) * unit for k in range(3)]
    return start + units * unit, [(at, size * unit) for at, size in zip(starts, sizes)]


def bit_orders(z):
    nbr = [("nbr", k) for k in range(z.nn.bit_length() - 1)]
    space = [("space", k) for k in range(z.ns.bit_length() - 1)]
    first, ring, rest = nbr[:1], [nbr[1], space[0], space[1]], nbr[2:] + space[2:]
    return [first + ring[k:] + ring[:k] + rest[: SPLITS - 4] for k in range(3)], rest[SPLITS - 4 :]


def pack_rows(z):
    DN, DE, FF = z.DN, z.DE, z.FF
    early = dict(wi=FF, wf=FF, wo=DN, es=DE, ep=DE)
    late = dict(ws=DN, wp=DN, we=DE, own=DE, vec=32)
    at, row = SimpleNamespace(), 0
    for group in (early, late):
        first = row
        for name, size in group.items():
            setattr(at, name, row)
            row += size
        used = row
        row, parts = cut(z, used - first, first)
        if group is early:
            at.early, at.early_end = parts, used
        else:
            at.late, at.late_end = parts, used
    at.rows = row
    at.middle = at.late[0][0]
    return at


def sum_part(z, a, at, early):
    DN, DE, FF, B = z.DN, z.DE, z.FF, z.B
    orders, whole = bit_orders(z)
    phases = len(orders[0])
    most = max(size for _, size in at.early + at.late) >> phases
    parts = at.early + at.late
    groups = (range(3), range(3, 6))

    def bit_value(axis, bit):
        s, n = place()
        return lax.rem((n if axis == "nbr" else s) // (1 << bit), 2)

    def segment(part, depth):
        start, size = parts[part]
        for axis, bit in orders[part % 3][:depth]:
            size //= 2
            start = start + bit_value(axis, bit) * size
        return start, size

    def down(e, part, depth):
        axis, bit = orders[part % 3][depth]
        start, size = segment(part, depth)
        size //= 2
        give = pl.multiple_of(start + (1 - bit_value(axis, bit)) * size, 16)
        base = parts[part][0] + parts[part][1] - 2 * size
        copy = remote(
            e.s_buf.at[pl.ds(give, size)],
            e.s_recv.at[pl.ds(base, size)],
            e.s_ds.at[part, depth],
            e.s_dr.at[part, depth],
            across(axis, bit),
        )
        return copy, size, base

    def up(e, part, depth):
        start, size = segment(part, depth + 1)
        rows = pl.ds(pl.multiple_of(start, 16), size)
        src = e.s_buf if depth == phases - 1 else e.s_out
        return remote(
            src.at[rows],
            e.s_out.at[rows],
            e.s_us.at[part, depth],
            e.s_ur.at[part, depth],
            across(*orders[part % 3][depth]),
        )

    def keep_own(e, part):
        start, size = segment(part, phases)
        rows = pl.ds(pl.multiple_of(start, 16), size)
        return pltpu.make_async_copy(e.s_buf.at[rows], e.s_out.at[rows], e.s_os.at[part])

    def begin(group):
        def stage(e):
            for part in groups[group]:
                down(e, part, 0)[0].start()

        return stage

    def fold(group, depth):
        def stage(e):
            for part in groups[group]:
                copy, size, base = down(e, part, depth)
                copy.wait()
                start, _ = segment(part, depth + 1)
                keep = pl.ds(pl.multiple_of(start, 16), size)
                value = (e.s_buf[keep].astype(F32) + e.s_recv[pl.ds(base, size)].astype(F32)).astype(BF)
                if depth + 1 < phases:
                    e.s_buf[keep] = value
                    down(e, part, depth + 1)[0].start()
                    continue
                for k, (axis, bit) in enumerate(whole):
                    e.s_buf[keep] = value
                    copy = remote(
                        e.s_buf.at[keep],
                        e.s_more.at[part, k, pl.ds(0, size)],
                        e.s_ms.at[part, k],
                        e.s_mr.at[part, k],
                        across(axis, bit),
                    )
                    copy.start()
                    copy.wait()
                    value = (value.astype(F32) + e.s_more[part, k, 0:size].astype(F32)).astype(BF)
                e.s_buf[keep] = value
                keep_own(e, part).start()
                up(e, part, depth).start()

        return stage

    def spread(group, depth):
        def stage(e):
            for part in groups[group]:
                up(e, part, depth).wait()
                if depth == phases - 1:
                    keep_own(e, part).wait()
                if depth:
                    up(e, part, depth - 1).start()

        return stage

    def put(e, row, value):
        e.s_buf[row : row + value.shape[0], : value.shape[1]] = value.astype(BF)

    def clear(e, first, last):
        if last > first:
            e.s_buf[first:last] = jnp.zeros((last - first, DN), BF)

    def pack_early(e):
        def two(one, other):
            return jnp.concatenate([one[...], other[...]], 0)

        low, ffn = two(e.p_low0, e.p_low1), two(e.p_ffn0, e.b_offn)
        act, mid = two(e.p_act0, e.p_act1), two(e.p_mid0, e.b_omid)
        for k in range(FF // DN):
            put(e, at.wi + k * DN, dot_tn(low, ffn[:, k * DN : (k + 1) * DN]))
        for k in range(FF // DN):
            put(e, at.wf + k * DN, dot_tn(act[:, k * DN : (k + 1) * DN], mid))
        put(e, at.wo, dot_tn(two(e.p_sum0, e.p_sum1), two(e.p_grad0, e.b_olow)))
        fresh = two(e.p_new0, e.p_new1)
        put(e, at.es, dot_tn(two(e.p_self0, e.b_oself), fresh))
        put(e, at.ep, dot_tn(two(e.p_peer0, e.b_opeer), fresh))
        clear(e, at.early_end, at.middle)

    def pack_late(e):
        put(e, at.ws, e.g_dself[...].T)
        put(e, at.wp, e.g_dpeer[...].T)
        put(e, at.we, e.g_dwe[...])
        gap = jnp.zeros((DE, 256 - DE), F32)
        put(e, at.own, side([e.p_dwn[...], gap, e.p_dwo[...], gap]))
        narrow = side([e.p_vec[...], jnp.zeros((8, DN - DE), F32)])
        put(e, at.vec, jnp.concatenate([e.p_vec0[...] + e.b_ovec[...], narrow, e.g_vec[...]], 0))
        clear(e, at.late_end, at.rows)

    f0, f1, b0, ee = early
    return SimpleNamespace(
        begin=begin,
        fold=fold,
        spread=spread,
        pack_early=pack_early,
        pack_late=pack_late,
        phases=phases,
        ins=dict(
            p_low0=vm(f0.f_olow),
            p_low1=vm(f1.f_olow),
            p_act0=vm(f0.f_oact),
            p_act1=vm(f1.f_oact),
            p_sum0=vm(f0.f_osum),
            p_sum1=vm(f1.f_osum),
            p_new0=vm(f0.f_oq),
            p_new1=vm(f1.f_oq),
            p_ffn0=vm(b0.b_offn),
            p_mid0=vm(b0.b_omid),
            p_grad0=vm(b0.b_olow),
            p_self0=vm(b0.b_oself),
            p_peer0=vm(b0.b_opeer),
            p_vec0=vm(b0.b_ovec),
            p_vec=vm(ee.e_vgrad),
            p_dwo=vm(ee.e_dwo),
            p_dwn=vm(ee.e_dwn),
        ),
        outs=dict(s_out=(jax.ShapeDtypeStruct((at.rows, DN), BF), pl.BlockSpec(memory_space=pl.ANY))),
        scr=dict(
            s_buf=pltpu.VMEM((at.rows, DN), BF),
            s_recv=pltpu.VMEM((at.rows, DN), BF),
            s_os=dma(6),
            s_more=pltpu.VMEM((6, len(whole), most, DN) if whole else (16, DN), BF),
            s_ms=dma(6, max(1, len(whole))),
            s_mr=dma(6, max(1, len(whole))),
            s_ds=dma(6, phases),
            s_dr=dma(6, phases),
            s_us=dma(6, phases),
            s_ur=dma(6, phases),
        ),
    )


def unpack_kernel(z, packed, at):
    DN, DE, FF = z.DN, z.DE, z.FF

    def kernel(p, ws, wp, we, wo, wi, wf, es, ep, own, eo, *vectors):
        def get(row, size):
            return p[row : row + size].astype(F32)

        ws[...] = get(at.ws, DN)
        wp[...] = get(at.wp, DN)
        we[...] = get(at.we, DE)
        wo[...] = get(at.wo, DN)
        for k in range(FF // DN):
            wi[:, k * DN : (k + 1) * DN] = get(at.wi + k * DN, DN)
        wf[...] = get(at.wf, FF)
        es[...] = get(at.es, DE)
        ep[...] = get(at.ep, DE)
        pair = get(at.own, DE)
        own[...] = pair[:, :DE]
        eo[...] = pair[:, 256 : 256 + DE]
        vec = get(at.vec, 32)
        hidden = side([vec[6 + k : 7 + k] for k in range(FF // DN)])
        vectors[0][...] = hidden.reshape(FF)
        for ref, row in zip(vectors[1:], (24, 0, 1, 2, 3, 4, 5, 16, 17, 18, 19), strict=True):
            wide = ref.shape[0]
            ref[...] = vec[row : row + 1, :wide].reshape(wide)

    shapes = [(DN, DN), (DN, DN), (DE, DN), (DN, DN), (DN, FF), (FF, DN), (DE, DN), (DE, DN), (DE, DE), (DE, DE)]
    shapes += [(FF,)] + [(DN,)] * 7 + [(DE,)] * 4
    return pl.pallas_call(
        kernel,
        out_shape=[jax.ShapeDtypeStruct(shape, F32) for shape in shapes],
        in_specs=[pl.BlockSpec(memory_space=pltpu.VMEM)],
        out_specs=[pl.BlockSpec(memory_space=pltpu.VMEM)] * len(shapes),
        compiler_params=pltpu.CompilerParams(vmem_limit_bytes=VMEM_LIMIT),
    )(packed)


def local(
    nodes,
    edges,
    neighbors,
    slot_live,
    send_rows,
    message_self,
    message_peer,
    message_edge,
    message_bias,
    message_out,
    message_shift,
    first_gain,
    first_shift,
    hidden_in,
    hidden_bias,
    hidden_out,
    output_bias,
    second_gain,
    second_shift,
    edge_self,
    edge_peer,
    edge_own,
    edge_bias,
    edge_out,
    edge_shift,
    third_gain,
    third_shift,
    node_cot,
    edge_cot,
):
    a = SimpleNamespace(**locals())
    B, R, DN = nodes.shape
    S, DE = edges.shape[2:]
    ns, nn = lax.axis_size("space"), lax.axis_size("nbr")
    CAP = send_rows.shape[2]
    FAR = ns * CAP
    TP = -(-(3 * R + FAR) // LANES) * LANES
    z = SimpleNamespace(
        B=B, R=R, DN=DN, S=S, DE=DE, ns=ns, nn=nn, CAP=CAP, FAR=FAR, TP=TP, FF=hidden_in.shape[1], Q=R // nn
    )
    ids = itertools.count(1)
    a.edges_t = edges.transpose(0, 2, 3, 1)
    a.cot_t = edge_cot.transpose(0, 2, 3, 1)
    a.nbr = neighbors.transpose(2, 0, 1)
    a.live = slot_live.transpose(2, 0, 1)
    a.edge_self_t, a.edge_peer_t = edge_self.T, edge_peer.T
    T = S // GROUP

    def plain(part):
        return SimpleNamespace(ins=part, outs={}, scr={})

    small, table, message = setup_part(z, a), table_part(z, a), message_part(z, a)
    node0 = forward_part(z, a, 0, lambda e: e.part_a)
    f0 = build(
        ids,
        [small, table, message, node0],
        lambda: near_cross(z) + same_lane(z),
        2 * T,
        {0: [small.begin, table.begin(0), table.middle(0), table.begin(1), table.finish(0)], T: [node0.begin]},
        {
            1: [table.middle(1)],
            3: [table.finish(1)],
            T + 1: [node0.compute],
            T + 3: [node0.spread],
            2 * T - 1: [node0.finish],
        },
    )
    shared = plain(dict(vecs=vm(f0.vecs), send=vm(f0.send)))

    edge = edge_part(z, a, f0)
    node1 = forward_part(z, a, 1, lambda e: e.part_b)
    back0 = backward_part(z, a, 0, f0, lambda e: (e.a_tgrad, e.a_fgrad, e.a_sgrad))
    f1 = build(
        ids,
        [shared, plain(dict(part_b=vm(f0.part_b))), edge, node1, back0],
        lambda: near_cross(z) + same_lane(z),
        2 * T,
        {0: [node1.begin], T: [back0.begin]},
        {
            1: [node1.compute],
            3: [node1.spread],
            T - 1: [node1.finish],
            T + 1: [back0.gather],
            T + 2: [back0.compute],
            2 * T - 1: [back0.finish],
        },
    )

    at = pack_rows(z)
    last = last_part(z, a, f1.b_oall, f0.slope, f1.e_part, f0.tables)
    back1 = backward_part(z, a, 1, f1, lambda e: (e.e_tgrad, e.e_fgrad, e.e_sgrad))
    outer = nodes_part(z, a, lambda e: (e.a_all, e.b_all))
    total = sum_part(z, a, at, (f0, f1, f1, f1))
    for name, (shape, spec) in back1.outs.items():
        back1.scr[name] = pltpu.VMEM(shape.shape, shape.dtype)
    back1.outs = {}
    D = total.phases
    tail = [outer.begin(1), total.pack_late, total.begin(1), total.fold(0, D - 1)]
    tail += [total.fold(1, 0), outer.middle(1)]
    for d in reversed(range(D)):
        tail.append(total.spread(0, d))
        if D - d < D:
            tail.append(total.fold(1, D - d))
        if d == D - 3:
            tail.append(outer.finish(1))
    tail += [total.spread(1, d) for d in reversed(range(D))]
    after = {
        1: [back1.gather],
        2: [back1.compute, total.pack_early, total.begin(0)],
        3: [total.fold(0, 0)],
        T - 1: [back1.finish],
        T + 1: [total.fold(0, 1)],
        T + 2: [outer.middle(0), total.fold(0, 2)],
        2 * T - 1: [outer.finish(0)] + [total.fold(0, d) for d in range(3, D - 1)] + tail,
    }
    grads = dict(e_tgrad=vm(f1.e_tgrad), e_fgrad=vm(f1.e_fgrad), e_sgrad=vm(f1.e_sgrad))
    f2 = build(
        ids,
        [shared, plain(grads), last, back1, outer, total],
        lambda: [(lax.axis_index("space"), wrap(lax.axis_index("nbr") + k, nn)) for k in range(1, nn)] + same_lane(z),
        2 * T,
        {0: [back1.begin], T: [outer.begin(0)]},
        after,
    )
    ws, wp, we, wo, wi, wf, es, ep, own, eo, *vectors = unpack_kernel(z, f2.s_out, at)
    hidden, mb, ms, fg, fs, ob, sg, ss, eb, esh, tg, ts = vectors
    return (
        jnp.stack([f0.f_onew, f1.f_onew]),
        f1.e_final.transpose(0, 3, 1, 2),
        f2.o_grad,
        f2.g_edge.transpose(0, 3, 1, 2),
        ws,
        wp,
        we,
        mb,
        wo,
        ms,
        fg,
        fs,
        wi,
        hidden,
        wf,
        ob,
        sg,
        ss,
        es.T,
        ep.T,
        own,
        eb,
        eo,
        esh,
        tg,
        ts,
    )


def solution(mesh):
    tall = P(None, "space", None)
    slots = P(None, "space", "nbr", None)
    marks = P(None, "space", "nbr")
    return jax.shard_map(
        local,
        mesh=mesh,
        in_specs=(tall, slots, marks, marks, tall) + (P(),) * 22 + (tall, slots),
        out_specs=(tall, slots, marks, slots) + (P(),) * 22,
        check_vma=False,
    )
```

```python
import itertools
from types import SimpleNamespace

import jax
import jax.numpy as jnp
from jax import lax
from jax.experimental import pallas as pl
from jax.experimental.pallas import tpu as pltpu
from jax.sharding import PartitionSpec as P

EPS = 1e-05
F32 = jnp.float32
BF = jnp.bfloat16
MESH = pl.DeviceIdType.MESH
VMEM_LIMIT = 62 << 20
C0 = 0.7978845608028654
C1 = C0 * 0.044715
GROUP = 3
LANES = 128
SPLITS = 5
ROUNDS = 2


def dot(left, right):
    return jnp.dot(left, right, preferred_element_type=F32)


def dot_nt(left, right):
    return lax.dot_general(left, right, (((1,), (1,)), ((), ())), preferred_element_type=F32)


def dot_tn(left, right):
    return lax.dot_general(left, right, (((0,), (0,)), ((), ())), preferred_element_type=F32)


def gelu_both(x):
    one = jnp.ones((), x.dtype)
    a, b = one * C0, one * C1
    x2 = x * x
    half = one * 0.5 * jnp.tanh(x * (a + b * x2)) + one * 0.5
    act = x * half
    return act, half + act * (one - half) * (one * (2 * C0) + one * (6 * C1) * x2)


def norm_rows(value):
    centre = value - jnp.mean(value, -1, keepdims=True)
    rstd = lax.rsqrt(jnp.mean(centre * centre, -1, keepdims=True) + EPS)
    return centre * rstd, rstd


def norm_rows_back(xhat, rstd, grad):
    return rstd * (
        grad
        - jnp.mean(grad, -1, keepdims=True)
        - xhat * jnp.mean(grad * xhat, -1, keepdims=True)
    )


def hot(index, rows):
    it = lax.broadcasted_iota(jnp.int32, (rows, index.shape[1]), 0)
    return jnp.where(it == index, 1.0, 0.0).astype(BF)


def side(refs):
    return jnp.concatenate(refs, 1)


def row_sum(value):
    return jnp.sum(value, 0, keepdims=True)


def vm(array):
    return (array, pl.BlockSpec(memory_space=pltpu.VMEM))


def out(shape, dtype):
    return (jax.ShapeDtypeStruct(shape, dtype), pl.BlockSpec(memory_space=pltpu.VMEM))


def dma(*shape):
    return pltpu.SemaphoreType.DMA(shape)


def remote(src, dst, send, recv, device):
    return pltpu.make_async_remote_copy(
        src_ref=src, dst_ref=dst, send_sem=send, recv_sem=recv, device_id=device, device_id_type=MESH
    )


def build(ids, parts, partners, steps, before, after, later=()):
    ins, outs, scr, bodies = {}, {}, {}, []
    for part in parts:
        ins.update(part.ins)
        outs.update(part.outs)
        scr.update(part.scr)
        if hasattr(part, "body"):
            bodies.append(part.body)
    for name in later:
        array, _ = ins.pop(name)
        ins["h_" + name] = (array, pl.BlockSpec(memory_space=pl.ANY))
        scr[name] = pltpu.VMEM(array.shape, array.dtype)
    scr["l_sem"] = dma(max(1, len(later)))
    names = list(ins) + list(outs) + list(scr)

    def kernel(*refs):
        e = SimpleNamespace(**dict(zip(names, refs, strict=True)))
        step = pl.program_id(0)

        def bring():
            return [
                pltpu.make_async_copy(getattr(e, "h_" + name), getattr(e, name), e.l_sem.at[k])
                for k, name in enumerate(later)
            ]

        def enter():
            barrier = pltpu.get_barrier_semaphore()
            devices = partners()
            for device in devices:
                pl.semaphore_signal(barrier, inc=1, device_id=device, device_id_type=MESH)
            pl.semaphore_wait(barrier, len(devices))

        def run(listed):
            for stage in listed:
                if stage is ready:
                    for copy in bring():
                        copy.wait()
                else:
                    stage(e)

        for t in range(steps):
            if t == 0 or t in before:

                @pl.when(step == t)
                def _(t=t):
                    if t == 0:
                        for copy in bring():
                            copy.start()
                        enter()
                    run(before.get(t, ()))

        for body in bodies:
            body(e, step)
        for t in sorted(after):
            pl.when(step == t)(lambda t=t: run(after[t]))

    got = pl.pallas_call(
        kernel,
        grid=(steps,),
        out_shape=[shape for shape, _ in outs.values()],
        in_specs=[spec for _, spec in ins.values()],
        out_specs=[spec for _, spec in outs.values()],
        scratch_shapes=list(scr.values()),
        compiler_params=pltpu.CompilerParams(
            vmem_limit_bytes=VMEM_LIMIT, collective_id=next(ids), has_side_effects=True
        ),
    )(*[array for array, _ in ins.values()])
    return SimpleNamespace(**dict(zip(outs, got, strict=True)))


def ready(e):
    raise NotImplementedError


def place():
    return lax.axis_index("space"), lax.axis_index("nbr")


def wrap(value, count):
    return lax.rem(value + count, count)


def flip(value, bit):
    return value + (1 - 2 * (lax.rem(value // (1 << bit), 2))) * (1 << bit)


def across(axis, bit):
    s, n = place()
    return (s, flip(n, bit)) if axis == "nbr" else (flip(s, bit), n)


def near_cross(z):
    s, n = place()
    found = [(s, wrap(n + k, z.nn)) for k in range(1, z.nn)]
    sides = (1, -1) if z.ns > 2 else (1,)
    return found + [(wrap(s + d, z.ns), wrap(n + k, z.nn)) for d in sides for k in range(1, z.nn)]


def same_lane(z):
    s, n = place()
    return [(wrap(s + k, z.ns), n) for k in range(1, z.ns)]


def quarter(z):
    s, n = place()
    return pl.ds(pl.multiple_of(n * z.Q, 16), z.Q)


def far_copies(z, send, recv, fs, fr):
    s, n = place()
    found = []
    for k in range(1, z.ns):
        p = wrap(s + k, z.ns)
        found.append(
            remote(
                send.at[pl.ds(p * z.CAP, z.CAP)], recv.at[pl.ds(s * z.CAP, z.CAP)], fs.at[k], fr.at[k], (p, n)
            )
        )
    return found


def far_own(z, send, recv):
    s, n = place()
    here = pl.ds(pl.multiple_of(s * z.CAP, 8), z.CAP)
    recv[here] = send[here]


def setup_part(z, a):
    lines = (
        a.message_bias,
        a.edge_bias,
        a.edge_shift,
        a.third_gain,
        a.third_shift,
        a.message_shift,
        a.first_gain,
        a.first_shift,
        a.output_bias,
        a.second_gain,
        a.second_shift,
    )
    at = (0, 1, 2, 3, 4, 8, 9, 10, 11, 12, 13)

    def begin(e):
        e.vecs[...] = jnp.zeros_like(e.vecs)
        given = (e.va, e.vb, e.vc, e.vd, e.ve, e.vf, e.vg, e.vh, e.vi, e.vj, e.vk)
        for row, line in zip(at, given, strict=True):
            wide = line.shape[0]
            e.vecs[row : row + 1, 0:wide] = line[...].astype(F32).reshape(1, wide)
        hidden = e.vl[...].astype(F32).reshape(1, z.FF)
        for k in range(z.FF // z.DN):
            e.vecs[16 + k : 17 + k] = hidden[:, k * z.DN : (k + 1) * z.DN]
        p = lax.broadcasted_iota(jnp.int32, (z.CAP, z.FAR), 0)
        q = lax.broadcasted_iota(jnp.int32, (z.CAP, z.FAR), 1)
        spread = jnp.where(lax.rem(q, z.CAP) == p, 1.0, 0.0)
        b = lax.broadcasted_iota(jnp.int32, (z.ns, z.FAR), 0)
        c = lax.broadcasted_iota(jnp.int32, (z.ns, z.FAR), 1)
        for k in range(z.B):
            wide = jnp.dot(
                e.send_rows[k].astype(F32), spread, precision=lax.Precision.HIGHEST, preferred_element_type=F32
            )
            e.send[k] = (row_sum(jnp.where(c // z.CAP == b, wide, 0.0)) + 0.5).astype(jnp.int32)

    given = dict(zip("abcdefghijkl", lines + (a.hidden_bias,)))
    return SimpleNamespace(
        begin=begin,
        ins=dict({"v" + k: vm(v) for k, v in given.items()}, send_rows=vm(a.send_rows)),
        outs=dict(vecs=out((24, z.DN), F32), send=out((z.B, 1, z.FAR), jnp.int32)),
        scr={},
    )


def table_part(z, a):
    R, DN, FAR, TP, ns, B = z.R, z.DN, z.FAR, z.TP, z.ns, z.B
    half = R // 2

    def far(e, b):
        return far_copies(z, e.t_fsend.at[b], e.t_frecv.at[b], e.t_fs.at[b], e.t_fr.at[b])

    def near(e, b):
        s, n = place()
        h = pl.multiple_of(lax.rem(n, 2) * half, 16)
        src = e.nodes.at[b, pl.ds(h, half)]
        return [
            remote(
                src, e.t_tab.at[b, pl.ds(base + h, half)], e.t_ns.at[b, k], e.t_nr.at[b, k], (wrap(s + step, ns), n)
            )
            for k, (step, base) in enumerate(((1, 0), (-1, 2 * R)))
        ]

    def mate(e, b):
        s, n = place()
        h = pl.multiple_of(lax.rem(n, 2) * half, 16)
        found = []
        for k, base in enumerate((0, 2 * R)):
            rows = e.t_tab.at[b, pl.ds(base + h, half)]
            found.append(remote(rows, rows, e.t_ms.at[b, k], e.t_mr.at[b, k], (s, flip(n, 0))))
        return found

    def begin(b):
        def stage(e):
            for copy in near(e, b):
                copy.start()
            own = e.nodes[b]
            e.t_fsend[b] = dot_tn(hot(e.send[b], R), own)
            for copy in far(e, b):
                copy.start()
            e.t_tab[b, R : 2 * R] = own
            if TP > 3 * R + FAR:
                e.t_tab[b, 3 * R + FAR :] = jnp.zeros((TP - 3 * R - FAR, DN), BF)

        return stage

    def middle(b):
        def stage(e):
            for one, two in zip(near(e, b), mate(e, b), strict=True):
                one.wait_recv()
                two.start()

        return stage

    def finish(b):
        def stage(e):
            far_own(z, e.t_fsend.at[b], e.t_frecv.at[b])
            for copy in far(e, b):
                copy.wait()
            for copy in near(e, b):
                copy.wait_send()
            for copy in mate(e, b):
                copy.wait()
            e.t_tab[b, 3 * R : 3 * R + FAR] = e.t_frecv[b].astype(BF)
            e.tables[b] = e.t_tab[b]

        return stage

    return SimpleNamespace(
        begin=begin,
        middle=middle,
        finish=finish,
        ins=dict(nodes=vm(a.nodes)),
        outs=dict(tables=out((B, TP, DN), BF)),
        scr=dict(
            t_tab=pltpu.VMEM((B, TP, DN), BF),
            t_fsend=pltpu.VMEM((B, FAR, DN), F32),
            t_frecv=pltpu.VMEM((B, FAR, DN), F32),
            t_fs=dma(B, ns),
            t_fr=dma(B, ns),
            t_ns=dma(B, 2),
            t_nr=dma(B, 2),
            t_ms=dma(B, 2),
            t_mr=dma(B, 2),
        ),
    )


def message_part(z, a):
    R, DN, DE, TP, S, B = z.R, z.DN, z.DE, z.TP, z.S, z.B
    T = S // GROUP

    def body(e, step):
        sample, own = step // T, lax.rem(step, T)

        @pl.when(step == 0)
        def _():
            e.m_wst[...] = e.w_self[...].T
            e.m_wpt[...] = e.w_peer[...].T
            e.m_wet[...] = e.w_edge[...].T

        @pl.when(own == 0)
        def _():
            e.m_tabt[...] = dot_nt(e.m_wpt[...], e.t_tab[sample]).astype(BF)
            e.m_selft[...] = dot_nt(e.m_wst[...], e.nodes[sample]) + e.vecs[0:8].T[:, 0:1]
            e.m_acc[...] = jnp.zeros_like(e.m_acc)

        slots = [own * GROUP + g for g in range(GROUP)]
        line = pl.ds(sample, 1)
        value = dot(e.m_tabt[...], hot(side([e.nbr[s, line] for s in slots]), TP)) + dot(
            e.m_wet[...], side([e.m_edges[0, g] for g in range(GROUP)])
        )
        acc = e.m_acc[0:DN]
        count = e.m_acc[DN:]
        for g, s in enumerate(slots):
            live = e.live[s, line].astype(F32)
            act, slope = gelu_both(value[:, g * R : (g + 1) * R] + e.m_selft[...])
            e.slope[0, g] = slope.astype(BF)
            acc = acc + act * live
            count = count + live
        e.m_acc[0:DN] = acc
        e.m_acc[DN:] = count
        for b, ref in enumerate((e.part_a, e.part_b)):

            @pl.when(step == (b + 1) * T - 1)
            def _(ref=ref):
                ref[...] = e.m_acc[...].T.astype(BF)

    return SimpleNamespace(
        body=body,
        ins=dict(
            nodes=vm(a.nodes),
            m_edges=(a.edges_t, pl.BlockSpec((1, GROUP, DE, R), lambda i: (i // T, lax.rem(i, T), 0, 0))),
            nbr=vm(a.nbr),
            live=vm(a.live),
            w_self=vm(a.message_self),
            w_peer=vm(a.message_peer),
            w_edge=vm(a.message_edge),
        ),
        outs=dict(
            slope=(
                jax.ShapeDtypeStruct((B, S, DN, R), BF),
                pl.BlockSpec((1, GROUP, DN, R), lambda i: (i // T, lax.rem(i, T), 0, 0)),
            ),
            part_b=out((R, DN + LANES), BF),
        ),
        scr=dict(
            part_a=pltpu.VMEM((R, DN + LANES), BF),
            m_tabt=pltpu.VMEM((DN, TP), BF),
            m_selft=pltpu.VMEM((DN, R), F32),
            m_wst=pltpu.VMEM((DN, DN), BF),
            m_wpt=pltpu.VMEM((DN, DN), BF),
            m_wet=pltpu.VMEM((DN, DE), BF),
            m_acc=pltpu.VMEM((DN + LANES, R), F32),
        ),
    )


def forward_part(z, a, b, part):
    R, DN, DE, FF, Q, FAR, TP, ns, nn = z.R, z.DN, z.DE, z.FF, z.Q, z.FAR, z.TP, z.ns, z.nn
    W = DN + LANES

    def sums(e):
        s, n = place()
        found = []
        for k in range(1, nn):
            q = wrap(n + k, nn)
            rows = pl.ds(pl.multiple_of(q * Q, 16), Q)
            found.append(remote(part(e).at[rows], e.f_sum.at[k], e.f_ss.at[k], e.f_sr.at[k], (s, q)))
        return found

    def alls(e):
        s, n = place()
        rows = e.f_new.at[quarter(z)]
        return [
            remote(rows, rows, e.f_as.at[k], e.f_ar.at[k], (s, wrap(n + k, nn))) for k in range(1, nn)
        ]

    def near(e):
        s, n = place()
        found = []
        for i, (step, base) in enumerate(((1, 0), (-1, 2 * R))):
            rows = pl.ds(pl.multiple_of(base + n * Q, 16), Q)
            for k in range(nn):
                to = (wrap(s + step, ns), wrap(n + k, nn))
                found.append(remote(e.f_pe, e.f_tab.at[rows], e.f_ns.at[i, k], e.f_nr.at[i, k], to))
        return found

    def far(e):
        return far_copies(z, e.f_fsend, e.f_frecv, e.f_fs, e.f_fr)

    def begin(e):
        for copy in sums(e):
            copy.start()

    def compute(e):
        mine = quarter(z)
        for copy in sums(e):
            copy.wait()
        total = part(e)[mine].astype(F32)
        for k in range(1, nn):
            total = total + e.f_sum[k].astype(F32)
        count = total[:, DN : DN + 1]
        summed_act = total[:, :DN].astype(BF)
        summed = dot(summed_act, e.w_out[...]) + count * e.vecs[8:9]
        updated = e.nodes[b, mine].astype(F32) + summed / jnp.maximum(count, 1.0)
        xhat1, rstd1 = norm_rows(updated)
        hidden = xhat1 * e.vecs[9:10] + e.vecs[10:11]
        low = hidden.astype(BF)
        bias = side([e.vecs[16 + k : 17 + k] for k in range(FF // DN)])
        act, slope = gelu_both(dot(low, e.w_in[...]) + bias)
        act = act.astype(BF)
        xhat2, rstd2 = norm_rows(hidden + dot(act, e.w_ffn[...]) + e.vecs[11:12])
        fresh = (xhat2 * e.vecs[12:13] + e.vecs[13:14]).astype(BF)
        e.f_new[mine] = fresh
        e.f_pe[...] = dot_nt(fresh, e.ept[...]).astype(BF)
        for copy in alls(e):
            copy.start()
        for copy in near(e):
            copy.start()
        e.f_osum[...] = summed_act
        e.f_ocount[...] = total[:, DN:]
        e.f_ox1[...] = xhat1
        e.f_or1[...] = jnp.broadcast_to(rstd1, (Q, LANES))
        e.f_olow[...] = low
        e.f_oslope[...] = slope.astype(BF)
        e.f_oact[...] = act
        e.f_ox2[...] = xhat2
        e.f_or2[...] = jnp.broadcast_to(rstd2, (Q, LANES))
        e.f_oq[...] = fresh

    def spread(e):
        for copy in alls(e):
            copy.wait()
        own = dot_nt(e.f_new[...], e.ept[...]).astype(BF)
        e.f_tab[R : 2 * R] = own
        e.f_fsend[...] = dot_tn(hot(e.send[b], R), own)
        for copy in far(e):
            copy.start()
        e.f_onew[...] = e.f_new[...]
        if TP > 3 * R + FAR:
            e.f_tab[3 * R + FAR :] = jnp.zeros((TP - 3 * R - FAR, DE), BF)

    def finish(e):
        far_own(z, e.f_fsend, e.f_frecv)
        for copy in near(e):
            copy.wait()
        for copy in far(e):
            copy.wait()
        e.f_tab[3 * R : 3 * R + FAR] = e.f_frecv[...].astype(BF)
        e.f_otab[...] = e.f_tab[...]

    return SimpleNamespace(
        begin=begin,
        compute=compute,
        spread=spread,
        finish=finish,
        ins=dict(
            nodes=vm(a.nodes),
            w_out=vm(a.message_out),
            w_in=vm(a.hidden_in),
            w_ffn=vm(a.hidden_out),
            ept=vm(a.edge_peer_t),
        ),
        outs=dict(
            f_onew=out((R, DN), BF),
            f_otab=out((TP, DE), BF),
            f_osum=out((Q, DN), BF),
            f_ocount=out((Q, LANES), F32),
            f_ox1=out((Q, DN), F32),
            f_or1=out((Q, LANES), F32),
            f_olow=out((Q, DN), BF),
            f_oslope=out((Q, FF), BF),
            f_oact=out((Q, FF), BF),
            f_ox2=out((Q, DN), F32),
            f_or2=out((Q, LANES), F32),
            f_oq=out((Q, DN), BF),
        ),
        scr=dict(
            f_sum=pltpu.VMEM((nn, Q, W), BF),
            f_new=pltpu.VMEM((R, DN), BF),
            f_pe=pltpu.VMEM((Q, DE), BF),
            f_tab=pltpu.VMEM((TP, DE), BF),
            f_fsend=pltpu.VMEM((FAR, DE), F32),
            f_frecv=pltpu.VMEM((FAR, DE), F32),
            f_ss=dma(nn),
            f_sr=dma(nn),
            f_as=dma(nn),
            f_ar=dma(nn),
            f_ns=dma(2, nn),
            f_nr=dma(2, nn),
            f_fs=dma(ns),
            f_fr=dma(ns),
        ),
    )


def edge_part(z, a, first):
    R, DN, DE, TP, S, FAR, B = z.R, z.DN, z.DE, z.TP, z.S, z.FAR, z.B
    T = S // GROUP

    def body(e, step):
        sample, own = step // T, lax.rem(step, T)

        @pl.when(step == 0)
        def _():
            e.e_cols[...] = e.vecs[0:8].T[:DE]
            e.e_wnt[...] = e.e_wn[...].astype(F32).T.astype(BF)
            e.e_wot[...] = e.e_wo[...].astype(F32).T.astype(BF)
            for ref in (e.e_gacc, e.e_hacc, e.e_uacc, e.e_vacc, e.e_dwo, e.e_dwn):
                ref[...] = jnp.zeros_like(ref)

        for b, (table, fresh) in enumerate(((e.a_tab, e.a_new), (e.f_tab, e.f_new))):

            @pl.when(step == b * T)
            def _(table=table, fresh=fresh):
                e.e_tabt[...] = table[...].astype(F32).T.astype(BF)
                e.e_selft[...] = dot_nt(e.est[...], fresh[...]) + e.e_cols[:, 1:2]
                e.e_ptab[...] = jnp.zeros_like(e.e_ptab)
                e.e_sacc[...] = jnp.zeros_like(e.e_sacc)

        line = pl.ds(sample, 1)
        index = hot(side([e.nbr[own * GROUP + g, line] for g in range(GROUP)]), TP)
        edge = side([e.m_edges[0, g] for g in range(GROUP)])
        value = dot(e.e_tabt[...], index) + dot(e.e_wnt[...], edge)
        value = value + side([e.e_selft[...]] * GROUP)
        act, slope = gelu_both(value)
        act = act.astype(BF)
        shift_c, gain_c, bias_c = e.e_cols[:, 2:3], e.e_cols[:, 3:4], e.e_cols[:, 4:5]
        full = edge.astype(F32) + dot(e.e_wot[...], act) + shift_c
        full = full - jnp.mean(full, 0, keepdims=True)
        rstd = lax.rsqrt(jnp.mean(full * full, 0, keepdims=True) + EPS)
        xhat = full * rstd
        final = (xhat * gain_c + bias_c).astype(BF)
        cot = side([e.e_cot[0, g] for g in range(GROUP)]).astype(F32)
        scaled = cot * gain_c
        back = rstd * (
            scaled - jnp.mean(scaled, 0, keepdims=True) - xhat * jnp.mean(scaled * xhat, 0, keepdims=True)
        )
        low = back.astype(BF)
        e.e_dwo[...] += dot_nt(act, low)
        inner = (slope * dot(e.e_wo[...], low)).astype(BF)
        e.e_dwn[...] += dot_nt(edge, inner)
        part = (back + dot(e.e_wn[...], inner)).astype(BF)
        e.e_ptab[...] += dot_nt(index, inner)
        gain_g = cot * xhat
        low_f = low.astype(F32)
        inner_f = inner.astype(F32)
        s_acc, g_acc, h_acc, u_acc = e.e_sacc[...], e.e_gacc[...], e.e_hacc[...], e.e_uacc[...]
        for g in range(GROUP):
            cut = slice(g * R, (g + 1) * R)
            e.e_final[0, g] = final[:, cut]
            e.e_part[0, g] = part[:, cut]
            s_acc = s_acc + inner_f[:, cut]
            g_acc = g_acc + gain_g[:, cut]
            h_acc = h_acc + cot[:, cut]
            u_acc = u_acc + low_f[:, cut]
        e.e_sacc[...] = s_acc
        e.e_gacc[...] = g_acc
        e.e_hacc[...] = h_acc
        e.e_uacc[...] = u_acc
        ends = ((e.a_tgrad, e.a_fgrad, e.a_sgrad), (e.e_tgrad, e.e_fgrad, e.e_sgrad))
        for b, (tgrad, fgrad, sgrad) in enumerate(ends):

            @pl.when(step == (b + 1) * T - 1)
            def _(tgrad=tgrad, fgrad=fgrad, sgrad=sgrad):
                rows = e.e_ptab[...]
                tgrad[...] = rows.astype(BF)
                fgrad[...] = rows[3 * R : 3 * R + FAR]
                turned = e.e_sacc[...].T
                sgrad[...] = turned.astype(BF)
                e.e_vacc[0:1] += row_sum(turned)

        @pl.when(step == B * T - 1)
        def _():
            for k, ref in enumerate((e.e_uacc, e.e_gacc, e.e_hacc)):
                e.e_vacc[k + 1 : k + 2] = row_sum(ref[...].T)
            e.e_vgrad[...] = e.e_vacc[...]

    stream = pl.BlockSpec((1, GROUP, DE, R), lambda i: (i // T, lax.rem(i, T), 0, 0))
    return SimpleNamespace(
        body=body,
        ins=dict(
            a_tab=vm(first.f_otab),
            a_new=vm(first.f_onew),
            m_edges=(a.edges_t, stream),
            e_cot=(a.cot_t, stream),
            nbr=vm(a.nbr),
            est=vm(a.edge_self_t),
            e_wn=vm(a.edge_own),
            e_wo=vm(a.edge_out),
        ),
        outs=dict(
            e_final=(jax.ShapeDtypeStruct((B, S, DE, R), BF), stream),
            e_part=(jax.ShapeDtypeStruct((B, S, DE, R), BF), stream),
            e_tgrad=out((TP, DE), BF),
            e_fgrad=out((FAR, DE), F32),
            e_sgrad=out((R, DE), BF),
            e_vgrad=out((8, DE), F32),
            e_dwo=out((DE, DE), F32),
            e_dwn=out((DE, DE), F32),
        ),
        scr=dict(
            a_tgrad=pltpu.VMEM((TP, DE), BF),
            a_fgrad=pltpu.VMEM((FAR, DE), F32),
            a_sgrad=pltpu.VMEM((R, DE), BF),
            e_tabt=pltpu.VMEM((DE, TP), BF),
            e_cols=pltpu.VMEM((DE, 8), F32),
            e_selft=pltpu.VMEM((DE, R), F32),
            e_wnt=pltpu.VMEM((DE, DE), BF),
            e_wot=pltpu.VMEM((DE, DE), BF),
            e_ptab=pltpu.VMEM((TP, DE), F32),
            e_sacc=pltpu.VMEM((DE, R), F32),
            e_gacc=pltpu.VMEM((DE, R), F32),
            e_hacc=pltpu.VMEM((DE, R), F32),
            e_uacc=pltpu.VMEM((DE, R), F32),
            e_vacc=pltpu.VMEM((8, DE), F32),
        ),
    )


def backward_part(z, a, b, node, grads):
    R, DN, DE, FF, Q, FAR, TP, ns, nn = z.R, z.DN, z.DE, z.FF, z.Q, z.FAR, z.TP, z.ns, z.nn
    W = DN + LANES

    def near(e):
        s, n = place()
        tgrad = grads(e)[0]
        return [
            remote(
                tgrad.at[pl.ds(base, R)], e.b_near.at[k], e.b_ns.at[k], e.b_nr.at[k], (wrap(s + step, ns), n)
            )
            for k, (step, base) in enumerate(((-1, 0), (1, 2 * R)))
        ]

    def far(e):
        return far_copies(z, grads(e)[1], e.b_frecv, e.b_fs, e.b_fr)

    def sums(e):
        s, n = place()
        found = []
        for k in range(1, nn):
            q = wrap(n + k, nn)
            rows = pl.ds(pl.multiple_of(q * Q, 16), Q)
            found.append(remote(e.b_pair.at[:, rows], e.b_sum.at[k], e.b_ss.at[k], e.b_sr.at[k], (s, q)))
        return found

    def alls(e):
        s, n = place()
        rows = e.b_all.at[quarter(z)]
        return [
            remote(rows, rows, e.b_as.at[k], e.b_ar.at[k], (s, wrap(n + k, nn))) for k in range(1, nn)
        ]

    def begin(e):
        for copy in near(e):
            copy.start()
        for copy in far(e):
            copy.start()

    def gather(e):
        tgrad, fgrad, sgrad = grads(e)
        far_own(z, fgrad, e.b_frecv)
        for copy in near(e):
            copy.wait()
        for copy in far(e):
            copy.wait()
        peer = (
            tgrad[R : 2 * R].astype(F32)
            + e.b_near[0].astype(F32)
            + e.b_near[1].astype(F32)
            + dot(hot(e.send[b], R), e.b_frecv[...].astype(BF))
        )
        e.b_pair[0] = peer.astype(BF)
        e.b_pair[1] = sgrad[...]
        for copy in sums(e):
            copy.start()

    def compute(e):
        mine = quarter(z)
        for copy in sums(e):
            copy.wait()
        peer = e.b_pair[0, mine].astype(F32)
        own = e.b_pair[1, mine].astype(F32)
        for k in range(1, nn):
            peer = peer + e.b_sum[k, 0].astype(F32)
            own = own + e.b_sum[k, 1].astype(F32)
        peer = peer.astype(BF)
        own = own.astype(BF)
        final = e.cot[b, mine].astype(F32) + dot(own, e.est[...]) + dot(peer, e.ept[...])
        xhat2 = e.b_x2[...]
        mid = norm_rows_back(xhat2, e.b_r2[:, 0:1], final * e.vecs[12:13])
        mid_low = mid.astype(BF)
        ffn = (e.b_slope[...].astype(F32) * dot_nt(mid_low, e.w_ffn[...])).astype(BF)
        hidden = mid + dot_nt(ffn, e.w_in[...])
        xhat1 = e.b_x1[...]
        grad = norm_rows_back(xhat1, e.b_r1[:, 0:1], hidden * e.vecs[9:10])
        count = e.b_count[:, 0:1]
        low = (grad / jnp.maximum(count, 1.0)).astype(BF)
        e.b_all[mine] = side([low, e.b_count[...].astype(BF)])
        for copy in alls(e):
            copy.start()
        e.b_omid[...] = mid_low
        e.b_offn[...] = ffn
        e.b_olow[...] = low
        e.b_opeer[...] = peer
        e.b_oself[...] = own
        wide = row_sum(ffn.astype(F32))
        e.b_ovec[...] = jnp.concatenate(
            [
                row_sum(low.astype(F32) * count),
                row_sum(hidden * xhat1),
                row_sum(hidden),
                row_sum(mid_low.astype(F32)),
                row_sum(final * xhat2),
                row_sum(final),
            ]
            + [wide[:, k * DN : (k + 1) * DN] for k in range(FF // DN)]
            + [jnp.zeros((6, DN), F32)],
            0,
        )

    def finish(e):
        for copy in alls(e):
            copy.wait()
        e.b_oall[...] = e.b_all[...]

    return SimpleNamespace(
        begin=begin,
        gather=gather,
        compute=compute,
        finish=finish,
        ins=dict(
            b_count=vm(node.f_ocount),
            b_x1=vm(node.f_ox1),
            b_r1=vm(node.f_or1),
            b_slope=vm(node.f_oslope),
            b_x2=vm(node.f_ox2),
            b_r2=vm(node.f_or2),
            cot=vm(a.node_cot),
            w_in=vm(a.hidden_in),
            w_ffn=vm(a.hidden_out),
            est=vm(a.edge_self_t),
            ept=vm(a.edge_peer_t),
        ),
        outs=dict(
            b_oall=out((R, W), BF),
            b_omid=out((Q, DN), BF),
            b_offn=out((Q, FF), BF),
            b_olow=out((Q, DN), BF),
            b_opeer=out((Q, DE), BF),
            b_oself=out((Q, DE), BF),
            b_ovec=out((16, DN), F32),
        ),
        scr=dict(
            b_near=pltpu.VMEM((2, R, DE), BF),
            b_frecv=pltpu.VMEM((FAR, DE), F32),
            b_pair=pltpu.VMEM((2, R, DE), BF),
            b_sum=pltpu.VMEM((nn, 2, Q, DE), BF),
            b_all=pltpu.VMEM((R, W), BF),
            b_ns=dma(2),
            b_nr=dma(2),
            b_fs=dma(ns),
            b_fr=dma(ns),
            b_ss=dma(nn),
            b_sr=dma(nn),
            b_as=dma(nn),
            b_ar=dma(nn),
        ),
    )


def last_part(z, a, spread, slope, part, tables):
    R, DN, DE, TP, S, FAR, B = z.R, z.DN, z.DE, z.TP, z.S, z.FAR, z.B
    T = S // GROUP

    def body(e, step):
        sample, own = step // T, lax.rem(step, T)
        for b, ref in enumerate((e.a_all, e.b_all)):

            @pl.when(step == b * T)
            def _(ref=ref, b=b):
                pltpu.make_async_copy(e.g_tables.at[b], e.g_tab, e.g_ts.at[b]).start()
                e.g_ht[...] = dot_nt(e.w_out[...], ref[:, 0:DN])
                e.g_ptab[...] = jnp.zeros_like(e.g_ptab)
                e.g_sacc[...] = jnp.zeros_like(e.g_sacc)
                if b == 0:
                    e.g_dwe[...] = jnp.zeros_like(e.g_dwe)
                    e.g_vec[...] = jnp.zeros_like(e.g_vec)

        line = pl.ds(sample, 1)
        slots = [own * GROUP + g for g in range(GROUP)]
        index = hot(side([e.nbr[s, line] for s in slots]), TP)
        edge = side([e.m_edges[0, g] for g in range(GROUP)])
        inner = []
        acc = e.g_sacc[...]
        for g, s in enumerate(slots):
            piece = (e.g_slope[0, g].astype(F32) * (e.g_ht[...] * e.live[s, line].astype(F32))).astype(BF)
            acc = acc + piece.astype(F32)
            inner.append(piece)
        e.g_sacc[...] = acc
        inner = side(inner)
        e.g_ptab[...] += dot_nt(inner, index)
        e.g_dwe[...] += dot_nt(edge, inner)
        back = dot(e.w_edge[...], inner)
        for g in range(GROUP):
            e.g_edge[0, g] = (back[:, g * R : (g + 1) * R] + e.g_part[0, g].astype(F32)).astype(BF)
        for b in range(B):

            @pl.when(step == (b + 1) * T - 1)
            def _(b=b):
                self_t = e.g_sacc[...].astype(BF)
                peer_t = e.g_ptab[...].astype(BF)
                pltpu.make_async_copy(e.g_tables.at[b], e.g_tab, e.g_ts.at[b]).wait()
                dself = dot(self_t, e.nodes[b])
                dpeer = dot(peer_t, e.g_tab[...])
                e.g_dself[...] = dself if b == 0 else e.g_dself[...] + dself
                e.g_dpeer[...] = dpeer if b == 0 else e.g_dpeer[...] + dpeer
                e.g_vec[0:1] += row_sum(e.g_sacc[...].T)
                e.o_rows[b] = dot(e.w_peer[...], peer_t).astype(BF)
                e.o_rows[b, :, R : 2 * R] = (
                    dot(e.w_peer[...], peer_t[:, R : 2 * R]) + dot(e.w_self[...], self_t)
                ).astype(BF)

    stream = pl.BlockSpec((1, GROUP, DE, R), lambda i: (i // T, lax.rem(i, T), 0, 0))
    return SimpleNamespace(
        body=body,
        ins=dict(
            a_all=vm(spread),
            g_slope=(slope, pl.BlockSpec((1, GROUP, DN, R), lambda i: (i // T, lax.rem(i, T), 0, 0))),
            g_part=(part, stream),
            g_tables=(tables, pl.BlockSpec(memory_space=pl.ANY)),
            nodes=vm(a.nodes),
            m_edges=(a.edges_t, stream),
            nbr=vm(a.nbr),
            live=vm(a.live),
            w_self=vm(a.message_self),
            w_peer=vm(a.message_peer),
            w_edge=vm(a.message_edge),
            w_out=vm(a.message_out),
        ),
        outs=dict(g_edge=(jax.ShapeDtypeStruct((B, S, DE, R), BF), stream)),
        scr=dict(
            g_tab=pltpu.VMEM((TP, DN), BF),
            g_ts=dma(B),
            g_ht=pltpu.VMEM((DN, R), F32),
            g_ptab=pltpu.VMEM((DN, TP), F32),
            g_sacc=pltpu.VMEM((DN, R), F32),
            g_dself=pltpu.VMEM((DN, DN), F32),
            g_dpeer=pltpu.VMEM((DN, DN), F32),
            g_dwe=pltpu.VMEM((DE, DN), F32),
            g_vec=pltpu.VMEM((8, DN), F32),
            o_rows=pltpu.VMEM((B, DN, TP), BF),
        ),
    )


def nodes_part(z, a, spreads):
    R, DN, FAR, TP, ns, nn, B = z.R, z.DN, z.FAR, z.TP, z.ns, z.nn, z.B
    L = DN // nn

    pairs = nn // 2

    def mates(e, b):
        s, n = place()
        other = flip(n, 0)
        found = []
        for k in range(pairs):
            q = lax.rem(other, 2) + 2 * k
            rows = pl.ds(pl.multiple_of(q * L, 16), L)
            found.append(
                remote(e.o_rows.at[b, rows], e.o_half.at[b, k], e.o_hs.at[b, k], e.o_hr.at[b, k], (s, other))
            )
        return found

    def sums(e, b):
        s, n = place()
        found = []
        for k in range(1, pairs):
            q = wrap(n + 2 * k, nn)
            found.append(
                remote(e.o_pair.at[b, q // 2], e.o_sum.at[b, k - 1], e.o_ss.at[b, k], e.o_sr.at[b, k], (s, q))
            )
        return found

    def near(e, b):
        s, n = place()
        return [
            remote(
                e.o_send.at[b, pl.ds(2 * k * R, R)],
                e.o_near.at[b, k],
                e.o_ns.at[b, k],
                e.o_nr.at[b, k],
                (wrap(s + step, ns), n),
            )
            for k, step in enumerate((-1, 1))
        ]

    def far(e, b):
        return far_copies(z, e.o_fsend.at[b], e.o_frecv.at[b], e.o_fs.at[b], e.o_fr.at[b])

    def begin(b):
        def stage(e):
            for copy in mates(e, b):
                copy.start()

        return stage

    def pair(b):
        def stage(e):
            s, n = place()
            for copy in mates(e, b):
                copy.wait()
            for k in range(pairs):
                q = lax.rem(n, 2) + 2 * k
                rows = pl.ds(pl.multiple_of(q * L, 16), L)
                e.o_pair[b, k] = (e.o_rows[b, rows].astype(F32) + e.o_half[b, k].astype(F32)).astype(BF)
            for copy in sums(e, b):
                copy.start()

        return stage

    def middle(b):
        def stage(e):
            s, n = place()
            for copy in sums(e, b):
                copy.wait()
            total = e.o_pair[b, n // 2].astype(F32)
            for k in range(1, pairs):
                total = total + e.o_sum[b, k - 1].astype(F32)
            turned = total.T
            e.o_send[b] = turned.astype(BF)
            e.o_fsend[b] = turned[3 * R : 3 * R + FAR]
            for copy in near(e, b):
                copy.start()
            for copy in far(e, b):
                copy.start()
            column = pl.ds(pl.multiple_of(n * L, L), L)
            spread = spreads(e)[b]
            count = spread[:, DN : DN + 1].astype(F32)
            e.o_grad[b] = turned[R : 2 * R] + spread[:, column].astype(F32) * jnp.maximum(count, 1.0)

        return stage

    def finish(b):
        def stage(e):
            far_own(z, e.o_fsend.at[b], e.o_frecv.at[b])
            for copy in near(e, b):
                copy.wait()
            for copy in far(e, b):
                copy.wait()
            e.o_grad[b] += (
                e.o_near[b, 0].astype(F32)
                + e.o_near[b, 1].astype(F32)
                + dot(hot(e.send[b], R), e.o_frecv[b].astype(BF))
            )

        return stage

    return SimpleNamespace(
        begin=begin,
        pair=pair,
        middle=middle,
        finish=finish,
        ins={},
        outs=dict(o_grad=out((B, R, L), F32)),
        scr=dict(
            o_half=pltpu.VMEM((B, pairs, L, TP), BF),
            o_pair=pltpu.VMEM((B, pairs, L, TP), BF),
            o_sum=pltpu.VMEM((B, pairs - 1, L, TP), BF),
            o_hs=dma(B, pairs),
            o_hr=dma(B, pairs),
            o_send=pltpu.VMEM((B, TP, L), BF),
            o_near=pltpu.VMEM((B, 2, R, L), BF),
            o_fsend=pltpu.VMEM((B, FAR, L), F32),
            o_frecv=pltpu.VMEM((B, FAR, L), F32),
            o_ss=dma(B, pairs),
            o_sr=dma(B, pairs),
            o_ns=dma(B, 2),
            o_nr=dma(B, 2),
            o_fs=dma(B, ns),
            o_fr=dma(B, ns),
        ),
    )


def cut(total, start, rounds):
    unit = 16 << SPLITS
    units = max(3 * rounds, -(-total // unit))
    count = 3 * rounds
    sizes = [units // count + (1 if k < units % count else 0) for k in range(count)]
    starts = [start + sum(sizes[:k]) * unit for k in range(count)]
    return start + units * unit, [(at, size * unit) for at, size in zip(starts, sizes)]


def bit_orders(z):
    nbr = [("nbr", k) for k in range(z.nn.bit_length() - 1)]
    space = [("space", k) for k in range(z.ns.bit_length() - 1)]
    first, ring, rest = nbr[:1], [nbr[1], space[0], space[1]], nbr[2:] + space[2:]
    return [first + ring[k:] + ring[:k] + rest[: SPLITS - 4] for k in range(3)], rest[SPLITS - 4 :]


def pack_rows(z):
    DN, DE, FF = z.DN, z.DE, z.FF
    early = dict(wi=FF, wf=FF, wo=DN, es=DE, ep=DE)
    late = dict(ws=DN, wp=DN, we=DE, own=DE, vec=32)
    at, row = SimpleNamespace(), 0
    for group in (early, late):
        first = row
        for name, size in group.items():
            setattr(at, name, row)
            row += size
        used = row
        row, parts = cut(used - first, first, ROUNDS if group is early else 1)
        if group is early:
            at.early, at.early_end = parts, used
        else:
            at.late, at.late_end = parts, used
    at.span = row
    at.rows = -(-row // (2 * DN)) * 2 * DN
    at.middle = at.late[0][0]
    return at


def sum_part(z, a, at, early):
    DN, DE, FF, B = z.DN, z.DE, z.FF, z.B
    orders, whole = bit_orders(z)
    phases = len(orders[0])
    most = max(size for _, size in at.early + at.late) >> phases
    parts = at.early + at.late
    groups = [range(k, k + 3) for k in range(0, len(parts), 3)]
    count = len(parts)

    def bit_value(axis, bit):
        s, n = place()
        return lax.rem((n if axis == "nbr" else s) // (1 << bit), 2)

    def segment(part, depth):
        start, size = parts[part]
        for axis, bit in orders[part % 3][:depth]:
            size //= 2
            start = start + bit_value(axis, bit) * size
        return start, size

    def down(e, part, depth):
        axis, bit = orders[part % 3][depth]
        start, size = segment(part, depth)
        size //= 2
        give = pl.multiple_of(start + (1 - bit_value(axis, bit)) * size, 16)
        base = parts[part][0] + parts[part][1] - 2 * size
        copy = remote(
            e.s_buf.at[pl.ds(give, size)],
            e.s_recv.at[pl.ds(base, size)],
            e.s_ds.at[part, depth],
            e.s_dr.at[part, depth],
            across(axis, bit),
        )
        return copy, size, base

    def up(e, part, depth):
        start, size = segment(part, depth + 1)
        rows = pl.ds(pl.multiple_of(start, 16), size)
        src = e.s_buf if depth == phases - 1 else e.s_out
        return remote(
            src.at[rows],
            e.s_out.at[rows],
            e.s_us.at[part, depth],
            e.s_ur.at[part, depth],
            across(*orders[part % 3][depth]),
        )

    def keep_own(e, part):
        start, size = segment(part, phases)
        rows = pl.ds(pl.multiple_of(start, 16), size)
        return pltpu.make_async_copy(e.s_buf.at[rows], e.s_out.at[rows], e.s_os.at[part])

    def begin(group):
        def stage(e):
            for part in groups[group]:
                down(e, part, 0)[0].start()

        return stage

    def fold(group, depth):
        def stage(e):
            for part in groups[group]:
                copy, size, base = down(e, part, depth)
                copy.wait()
                start, _ = segment(part, depth + 1)
                keep = pl.ds(pl.multiple_of(start, 16), size)
                value = (e.s_buf[keep].astype(F32) + e.s_recv[pl.ds(base, size)].astype(F32)).astype(BF)
                if depth + 1 < phases:
                    e.s_buf[keep] = value
                    down(e, part, depth + 1)[0].start()
                    continue
                for k, (axis, bit) in enumerate(whole):
                    e.s_buf[keep] = value
                    copy = remote(
                        e.s_buf.at[keep],
                        e.s_more.at[part, k, pl.ds(0, size)],
                        e.s_ms.at[part, k],
                        e.s_mr.at[part, k],
                        across(axis, bit),
                    )
                    copy.start()
                    copy.wait()
                    value = (value.astype(F32) + e.s_more[part, k, 0:size].astype(F32)).astype(BF)
                e.s_buf[keep] = value
                keep_own(e, part).start()
                up(e, part, depth).start()

        return stage

    def spread(group, depth):
        def stage(e):
            for part in groups[group]:
                up(e, part, depth).wait()
                if depth == phases - 1:
                    keep_own(e, part).wait()
                if depth:
                    up(e, part, depth - 1).start()

        return stage

    def put(e, row, value):
        e.s_buf[row : row + value.shape[0], : value.shape[1]] = value.astype(BF)

    def clear(e, first, last):
        if last > first:
            e.s_buf[first:last] = jnp.zeros((last - first, DN), BF)

    def pack_early(e):
        def two(one, other):
            return jnp.concatenate([one[...], other[...]], 0)

        low, ffn = two(e.p_low0, e.p_low1), two(e.p_ffn0, e.b_offn)
        act, mid = two(e.p_act0, e.p_act1), two(e.p_mid0, e.b_omid)
        for k in range(FF // DN):
            put(e, at.wi + k * DN, dot_tn(low, ffn[:, k * DN : (k + 1) * DN]))
        for k in range(FF // DN):
            put(e, at.wf + k * DN, dot_tn(act[:, k * DN : (k + 1) * DN], mid))
        put(e, at.wo, dot_tn(two(e.p_sum0, e.p_sum1), two(e.p_grad0, e.b_olow)))
        fresh = two(e.p_new0, e.p_new1)
        put(e, at.es, dot_tn(two(e.p_self0, e.b_oself), fresh))
        put(e, at.ep, dot_tn(two(e.p_peer0, e.b_opeer), fresh))
        clear(e, at.early_end, at.middle)

    def pack_late(e):
        put(e, at.ws, e.g_dself[...].T)
        put(e, at.wp, e.g_dpeer[...].T)
        put(e, at.we, e.g_dwe[...])
        gap = jnp.zeros((DE, 256 - DE), F32)
        put(e, at.own, side([e.p_dwn[...], gap, e.p_dwo[...], gap]))
        narrow = side([e.p_vec[...], jnp.zeros((8, DN - DE), F32)])
        put(e, at.vec, jnp.concatenate([e.p_vec0[...] + e.b_ovec[...], narrow, e.g_vec[...]], 0))
        clear(e, at.late_end, at.span)

    f0, f1, b0, ee = early
    return SimpleNamespace(
        begin=begin,
        fold=fold,
        spread=spread,
        pack_early=pack_early,
        pack_late=pack_late,
        phases=phases,
        ins=dict(
            p_low0=vm(f0.f_olow),
            p_low1=vm(f1.f_olow),
            p_act0=vm(f0.f_oact),
            p_act1=vm(f1.f_oact),
            p_sum0=vm(f0.f_osum),
            p_sum1=vm(f1.f_osum),
            p_new0=vm(f0.f_oq),
            p_new1=vm(f1.f_oq),
            p_ffn0=vm(b0.b_offn),
            p_mid0=vm(b0.b_omid),
            p_grad0=vm(b0.b_olow),
            p_self0=vm(b0.b_oself),
            p_peer0=vm(b0.b_opeer),
            p_vec0=vm(b0.b_ovec),
            p_vec=vm(ee.e_vgrad),
            p_dwo=vm(ee.e_dwo),
            p_dwn=vm(ee.e_dwn),
        ),
        outs=dict(s_out=(jax.ShapeDtypeStruct((at.rows, DN), BF), pl.BlockSpec(memory_space=pl.ANY))),
        scr=dict(
            s_buf=pltpu.VMEM((at.span, DN), BF),
            s_recv=pltpu.VMEM((at.span, DN), BF),
            s_os=dma(count),
            s_more=pltpu.VMEM((count, len(whole), most, DN) if whole else (16, DN), BF),
            s_ms=dma(count, max(1, len(whole))),
            s_mr=dma(count, max(1, len(whole))),
            s_ds=dma(count, phases),
            s_dr=dma(count, phases),
            s_us=dma(count, phases),
            s_ur=dma(count, phases),
        ),
    )


def unpack_kernel(z, packed, at, edge, final, node, fresh):
    DN, DE, FF, B, S, R = z.DN, z.DE, z.FF, z.B, z.S, z.R
    size, wide = 2 * DN, FF // DN
    half = wide // 2
    steps = at.rows // size
    slots = S // 3
    blocks = B * 3

    def kernel(p, *refs):
        given, (ws, wp, we, wo, wi, wf, es, ep, own, eo, *vectors), rest = refs[: B + 3], refs[B + 3 : B + 25], refs[B + 25 :]
        step = pl.program_id(0)

        @pl.when(step < blocks)
        def _():
            rest[0][...] = given[0][...]
            rest[1][...] = given[1][...]

        @pl.when(step == 0)
        def _():
            rest[2][...] = given[2][...]
            for b in range(B):
                rest[3][b] = given[3 + b][...]

        def take(row, count):
            return p[row % size : row % size + count].astype(F32)

        def at_row(row):
            return pl.when(step == row // size)

        @pl.when(step < half)
        def _():
            wi[:, :DN] = p[:DN].astype(F32)
            wi[:, DN:] = p[DN:].astype(F32)

        @pl.when(jnp.logical_and(step >= half, step < 2 * half))
        def _():
            wf[...] = p[...].astype(F32)

        @at_row(at.wo)
        def _():
            wo[...] = take(at.wo, DN)

        @at_row(at.es)
        def _():
            es[...] = take(at.es, DE)
            ep[...] = take(at.ep, DE)

        @at_row(at.ws)
        def _():
            ws[...] = take(at.ws, DN)

        @at_row(at.wp)
        def _():
            wp[...] = take(at.wp, DN)

        @at_row(at.we)
        def _():
            we[...] = take(at.we, DE)
            both = take(at.own, DE)
            own[...] = both[:, :DE]
            eo[...] = both[:, 256 : 256 + DE]
            vec = take(at.vec, 32)
            vectors[0][...] = side([vec[6 + k : 7 + k] for k in range(wide)]).reshape(FF)
            for ref, row in zip(vectors[1:], (24, 0, 1, 2, 3, 4, 5, 16, 17, 18, 19), strict=True):
                count = ref.shape[0]
                ref[...] = vec[row : row + 1, :count].reshape(count)

    shapes = [(DN, DN), (DN, DN), (DE, DN), (DN, DN), (DN, FF), (FF, DN), (DE, DN), (DE, DN), (DE, DE), (DE, DE)]
    shapes += [(FF,)] + [(DN,)] * 7 + [(DE,)] * 4
    here = pl.BlockSpec(memory_space=pltpu.VMEM)
    specs = [here] * len(shapes)
    specs[4] = pl.BlockSpec((DN, size), lambda i: (0, jnp.clip(i, 0, half - 1)))
    specs[5] = pl.BlockSpec((size, DN), lambda i: (jnp.clip(i - half, 0, half - 1), 0))

    def turn(i):
        k = jnp.minimum(i, blocks - 1)
        return (k // 3, lax.rem(k, 3), 0, 0)

    stream = pl.BlockSpec((1, slots, DE, R), turn)
    return pl.pallas_call(
        kernel,
        grid=(steps,),
        out_shape=[jax.ShapeDtypeStruct(shape, F32) for shape in shapes]
        + [jax.ShapeDtypeStruct(x.shape, x.dtype) for x in (edge, final, node)]
        + [jax.ShapeDtypeStruct((B,) + fresh[0].shape, fresh[0].dtype)],
        in_specs=[pl.BlockSpec((size, DN), lambda i: (i, 0)), stream, stream, here] + [here] * B,
        out_specs=specs + [stream, stream, here, here],
        compiler_params=pltpu.CompilerParams(vmem_limit_bytes=VMEM_LIMIT),
    )(packed, edge, final, node, *fresh)


def local(
    nodes,
    edges,
    neighbors,
    slot_live,
    send_rows,
    message_self,
    message_peer,
    message_edge,
    message_bias,
    message_out,
    message_shift,
    first_gain,
    first_shift,
    hidden_in,
    hidden_bias,
    hidden_out,
    output_bias,
    second_gain,
    second_shift,
    edge_self,
    edge_peer,
    edge_own,
    edge_bias,
    edge_out,
    edge_shift,
    third_gain,
    third_shift,
    node_cot,
    edge_cot,
):
    a = SimpleNamespace(**locals())
    B, R, DN = nodes.shape
    S, DE = edges.shape[2:]
    ns, nn = lax.axis_size("space"), lax.axis_size("nbr")
    CAP = send_rows.shape[2]
    FAR = ns * CAP
    TP = -(-(3 * R + FAR) // LANES) * LANES
    z = SimpleNamespace(
        B=B, R=R, DN=DN, S=S, DE=DE, ns=ns, nn=nn, CAP=CAP, FAR=FAR, TP=TP, FF=hidden_in.shape[1], Q=R // nn
    )
    ids = itertools.count(1)
    a.edges_t = edges.transpose(0, 2, 3, 1)
    a.cot_t = edge_cot.transpose(0, 2, 3, 1)
    a.nbr = neighbors.transpose(2, 0, 1)
    a.live = slot_live.transpose(2, 0, 1)
    a.edge_self_t, a.edge_peer_t = edge_self.T, edge_peer.T
    T = S // GROUP

    def plain(part):
        return SimpleNamespace(ins=part, outs={}, scr={})

    heavy = ("w_in", "w_ffn")
    small, table, message = setup_part(z, a), table_part(z, a), message_part(z, a)
    node0 = forward_part(z, a, 0, lambda e: e.part_a)
    f0 = build(
        ids,
        [small, table, message, node0],
        lambda: near_cross(z) + same_lane(z),
        2 * T,
        {0: [small.begin, table.begin(0), table.middle(0), table.begin(1), table.finish(0)], T: [node0.begin]},
        {
            1: [table.middle(1)],
            3: [table.finish(1)],
            T + 1: [ready, node0.compute],
            T + 3: [node0.spread],
            2 * T - 1: [node0.finish],
        },
        heavy,
    )
    shared = plain(dict(vecs=vm(f0.vecs), send=vm(f0.send)))

    edge = edge_part(z, a, f0)
    node1 = forward_part(z, a, 1, lambda e: e.part_b)
    back0 = backward_part(z, a, 0, f0, lambda e: (e.a_tgrad, e.a_fgrad, e.a_sgrad))
    f1 = build(
        ids,
        [shared, plain(dict(part_b=vm(f0.part_b))), edge, node1, back0],
        lambda: near_cross(z) + same_lane(z),
        2 * T,
        {0: [node1.begin], T: [back0.begin]},
        {
            1: [ready, node1.compute],
            3: [node1.spread],
            T - 1: [node1.finish],
            T + 1: [back0.gather],
            T + 2: [back0.compute],
            2 * T - 1: [back0.finish],
        },
        heavy,
    )

    at = pack_rows(z)
    last = last_part(z, a, f1.b_oall, f0.slope, f1.e_part, f0.tables)
    back1 = backward_part(z, a, 1, f1, lambda e: (e.e_tgrad, e.e_fgrad, e.e_sgrad))
    outer = nodes_part(z, a, lambda e: (e.a_all, e.b_all))
    total = sum_part(z, a, at, (f0, f1, f1, f1))
    for name, (shape, spec) in back1.outs.items():
        back1.scr[name] = pltpu.VMEM(shape.shape, shape.dtype)
    back1.outs = {}
    D, late = total.phases, ROUNDS

    def fold(d):
        return [total.fold(k, d) for k in range(ROUNDS)]

    def gather(d):
        return [total.spread(k, d) for k in range(ROUNDS)]

    tail = [outer.begin(1), total.pack_late, total.begin(late)] + fold(D - 1) + [outer.pair(1)]
    tail += [total.fold(late, 0), outer.middle(1)]
    for d in reversed(range(D)):
        tail += gather(d)
        if d:
            tail.append(total.fold(late, D - d))
        if d == D - 3:
            tail += [outer.finish(0), outer.finish(1)]
    tail += [total.spread(late, d) for d in reversed(range(D))]
    after = {
        1: [back1.gather],
        2: [ready, back1.compute, total.pack_early] + [total.begin(k) for k in range(ROUNDS)],
        3: fold(0),
        T - 1: [back1.finish],
        T: [outer.pair(0)] + fold(1),
        T + 1: fold(2),
        T + 2: [outer.middle(0)] + fold(3),
        2 * T - 1: tail,
    }
    grads = dict(e_tgrad=vm(f1.e_tgrad), e_fgrad=vm(f1.e_fgrad), e_sgrad=vm(f1.e_sgrad))
    f2 = build(
        ids,
        [shared, plain(grads), last, back1, outer, total],
        lambda: [(lax.axis_index("space"), wrap(lax.axis_index("nbr") + k, nn)) for k in range(1, nn)] + same_lane(z),
        2 * T,
        {0: [back1.begin], T: [outer.begin(0)]},
        after,
        heavy + ("p_act0", "p_act1", "p_ffn0"),
    )
    ws, wp, we, wo, wi, wf, es, ep, own, eo, *vectors = unpack_kernel(
        z, f2.s_out, at, f2.g_edge, f1.e_final, f2.o_grad, [f0.f_onew, f1.f_onew]
    )
    hidden, mb, ms, fg, fs, ob, sg, ss, eb, esh, tg, ts, edge_grad, new_edges, node_grad, new_nodes = vectors
    return (
        new_nodes,
        new_edges.transpose(0, 3, 1, 2),
        node_grad,
        edge_grad.transpose(0, 3, 1, 2),
        ws,
        wp,
        we,
        mb,
        wo,
        ms,
        fg,
        fs,
        wi,
        hidden,
        wf,
        ob,
        sg,
        ss,
        es.T,
        ep.T,
        own,
        eb,
        eo,
        esh,
        tg,
        ts,
    )


def solution(mesh):
    tall = P(None, "space", None)
    slots = P(None, "space", "nbr", None)
    marks = P(None, "space", "nbr")
    return jax.shard_map(
        local,
        mesh=mesh,
        in_specs=(tall, slots, marks, marks, tall) + (P(),) * 22 + (tall, slots),
        out_specs=(tall, slots, marks, slots) + (P(),) * 22,
        check_vma=False,
    )
```

```python
import itertools
from types import SimpleNamespace

import jax
import jax.numpy as jnp
from jax import lax
from jax.experimental import pallas as pl
from jax.experimental.pallas import tpu as pltpu
from jax.sharding import PartitionSpec as P

EPS = 1e-05
F32 = jnp.float32
BF = jnp.bfloat16
MESH = pl.DeviceIdType.MESH
VMEM_LIMIT = 62 << 20
C0 = 0.7978845608028654
C1 = C0 * 0.044715
GROUP = 3
LANES = 128
SPLITS = 5
ROUNDS = 2


def dot(left, right):
    return jnp.dot(left, right, preferred_element_type=F32)


def dot_nt(left, right):
    return lax.dot_general(left, right, (((1,), (1,)), ((), ())), preferred_element_type=F32)


def dot_tn(left, right):
    return lax.dot_general(left, right, (((0,), (0,)), ((), ())), preferred_element_type=F32)


def gelu_both(x):
    one = jnp.ones((), x.dtype)
    a, b = one * C0, one * C1
    x2 = x * x
    half = one * 0.5 * jnp.tanh(x * (a + b * x2)) + one * 0.5
    act = x * half
    return act, half + act * (one - half) * (one * (2 * C0) + one * (6 * C1) * x2)


def norm_rows(value):
    centre = value - jnp.mean(value, -1, keepdims=True)
    rstd = lax.rsqrt(jnp.mean(centre * centre, -1, keepdims=True) + EPS)
    return centre * rstd, rstd


def norm_rows_back(xhat, rstd, grad):
    return rstd * (
        grad
        - jnp.mean(grad, -1, keepdims=True)
        - xhat * jnp.mean(grad * xhat, -1, keepdims=True)
    )


def hot(index, rows):
    it = lax.broadcasted_iota(jnp.int32, (rows, index.shape[1]), 0)
    return jnp.where(it == index, 1.0, 0.0).astype(BF)


def side(refs):
    return jnp.concatenate(refs, 1)


def row_sum(value):
    return jnp.sum(value, 0, keepdims=True)


def vm(array):
    return (array, pl.BlockSpec(memory_space=pltpu.VMEM))


def out(shape, dtype):
    return (jax.ShapeDtypeStruct(shape, dtype), pl.BlockSpec(memory_space=pltpu.VMEM))


def dma(*shape):
    return pltpu.SemaphoreType.DMA(shape)


def remote(src, dst, send, recv, device):
    return pltpu.make_async_remote_copy(
        src_ref=src, dst_ref=dst, send_sem=send, recv_sem=recv, device_id=device, device_id_type=MESH
    )


def build(ids, parts, partners, steps, before, after, later=()):
    ins, outs, scr, bodies = {}, {}, {}, []
    for part in parts:
        ins.update(part.ins)
        outs.update(part.outs)
        scr.update(part.scr)
        if hasattr(part, "body"):
            bodies.append(part.body)
    for name in later:
        array, _ = ins.pop(name)
        ins["h_" + name] = (array, pl.BlockSpec(memory_space=pl.ANY))
        scr[name] = pltpu.VMEM(array.shape, array.dtype)
    scr["l_sem"] = dma(max(1, len(later)))
    names = list(ins) + list(outs) + list(scr)

    def kernel(*refs):
        e = SimpleNamespace(**dict(zip(names, refs, strict=True)))
        step = pl.program_id(0)

        def bring():
            return [
                pltpu.make_async_copy(getattr(e, "h_" + name), getattr(e, name), e.l_sem.at[k])
                for k, name in enumerate(later)
            ]

        def enter():
            barrier = pltpu.get_barrier_semaphore()
            devices = partners()
            for device in devices:
                pl.semaphore_signal(barrier, inc=1, device_id=device, device_id_type=MESH)
            pl.semaphore_wait(barrier, len(devices))

        def run(listed):
            for stage in listed:
                if stage is ready:
                    for copy in bring():
                        copy.wait()
                else:
                    stage(e)

        for t in range(steps):
            if t == 0 or t in before:

                @pl.when(step == t)
                def _(t=t):
                    if t == 0:
                        for copy in bring():
                            copy.start()
                        enter()
                    run(before.get(t, ()))

        for body in bodies:
            body(e, step)
        for t in sorted(after):
            pl.when(step == t)(lambda t=t: run(after[t]))

    got = pl.pallas_call(
        kernel,
        grid=(steps,),
        out_shape=[shape for shape, _ in outs.values()],
        in_specs=[spec for _, spec in ins.values()],
        out_specs=[spec for _, spec in outs.values()],
        scratch_shapes=list(scr.values()),
        compiler_params=pltpu.CompilerParams(
            vmem_limit_bytes=VMEM_LIMIT, collective_id=next(ids), has_side_effects=True
        ),
    )(*[array for array, _ in ins.values()])
    return SimpleNamespace(**dict(zip(outs, got, strict=True)))


def ready(e):
    raise NotImplementedError


def place():
    return lax.axis_index("space"), lax.axis_index("nbr")


def wrap(value, count):
    return lax.rem(value + count, count)


def flip(value, bit):
    return value + (1 - 2 * (lax.rem(value // (1 << bit), 2))) * (1 << bit)


def across(axis, bit):
    s, n = place()
    return (s, flip(n, bit)) if axis == "nbr" else (flip(s, bit), n)


def near_cross(z):
    s, n = place()
    found = [(s, wrap(n + k, z.nn)) for k in range(1, z.nn)]
    sides = (1, -1) if z.ns > 2 else (1,)
    return found + [(wrap(s + d, z.ns), wrap(n + k, z.nn)) for d in sides for k in range(1, z.nn)]


def same_lane(z):
    s, n = place()
    return [(wrap(s + k, z.ns), n) for k in range(1, z.ns)]


def quarter(z):
    s, n = place()
    return pl.ds(pl.multiple_of(n * z.Q, 16), z.Q)


def far_copies(z, send, recv, fs, fr):
    s, n = place()
    found = []
    for k in range(1, z.ns):
        p = wrap(s + k, z.ns)
        found.append(
            remote(
                send.at[pl.ds(p * z.CAP, z.CAP)], recv.at[pl.ds(s * z.CAP, z.CAP)], fs.at[k], fr.at[k], (p, n)
            )
        )
    return found


def far_own(z, send, recv):
    s, n = place()
    here = pl.ds(pl.multiple_of(s * z.CAP, 8), z.CAP)
    recv[here] = send[here]


def setup_part(z, a):
    lines = (
        a.message_bias,
        a.edge_bias,
        a.edge_shift,
        a.third_gain,
        a.third_shift,
        a.message_shift,
        a.first_gain,
        a.first_shift,
        a.output_bias,
        a.second_gain,
        a.second_shift,
    )
    at = (0, 1, 2, 3, 4, 8, 9, 10, 11, 12, 13)

    def begin(e):
        e.vecs[...] = jnp.zeros_like(e.vecs)
        given = (e.va, e.vb, e.vc, e.vd, e.ve, e.vf, e.vg, e.vh, e.vi, e.vj, e.vk)
        for row, line in zip(at, given, strict=True):
            wide = line.shape[0]
            e.vecs[row : row + 1, 0:wide] = line[...].astype(F32).reshape(1, wide)
        hidden = e.vl[...].astype(F32).reshape(1, z.FF)
        for k in range(z.FF // z.DN):
            e.vecs[16 + k : 17 + k] = hidden[:, k * z.DN : (k + 1) * z.DN]
        p = lax.broadcasted_iota(jnp.int32, (z.CAP, z.FAR), 0)
        q = lax.broadcasted_iota(jnp.int32, (z.CAP, z.FAR), 1)
        spread = jnp.where(lax.rem(q, z.CAP) == p, 1.0, 0.0)
        b = lax.broadcasted_iota(jnp.int32, (z.ns, z.FAR), 0)
        c = lax.broadcasted_iota(jnp.int32, (z.ns, z.FAR), 1)
        for k in range(z.B):
            wide = jnp.dot(
                e.send_rows[k].astype(F32), spread, precision=lax.Precision.HIGHEST, preferred_element_type=F32
            )
            e.send[k] = (row_sum(jnp.where(c // z.CAP == b, wide, 0.0)) + 0.5).astype(jnp.int32)

    given = dict(zip("abcdefghijkl", lines + (a.hidden_bias,)))
    return SimpleNamespace(
        begin=begin,
        ins=dict({"v" + k: vm(v) for k, v in given.items()}, send_rows=vm(a.send_rows)),
        outs=dict(vecs=out((24, z.DN), F32), send=out((z.B, 1, z.FAR), jnp.int32)),
        scr={},
    )


def table_part(z, a):
    R, DN, FAR, TP, ns, B = z.R, z.DN, z.FAR, z.TP, z.ns, z.B
    half = R // 2

    def far(e, b):
        return far_copies(z, e.t_fsend.at[b], e.t_frecv.at[b], e.t_fs.at[b], e.t_fr.at[b])

    def near(e, b):
        s, n = place()
        h = pl.multiple_of(lax.rem(n, 2) * half, 16)
        src = e.nodes.at[b, pl.ds(h, half)]
        return [
            remote(
                src, e.t_tab.at[b, pl.ds(base + h, half)], e.t_ns.at[b, k], e.t_nr.at[b, k], (wrap(s + step, ns), n)
            )
            for k, (step, base) in enumerate(((1, 0), (-1, 2 * R)))
        ]

    def mate(e, b):
        s, n = place()
        h = pl.multiple_of(lax.rem(n, 2) * half, 16)
        found = []
        for k, base in enumerate((0, 2 * R)):
            rows = e.t_tab.at[b, pl.ds(base + h, half)]
            found.append(remote(rows, rows, e.t_ms.at[b, k], e.t_mr.at[b, k], (s, flip(n, 0))))
        return found

    def launch(b):
        def stage(e):
            for copy in near(e, b):
                copy.start()

        return stage

    def begin(b):
        def stage(e):
            own = e.nodes[b]
            e.t_fsend[b] = dot_tn(hot(e.send[b], R), own)
            for copy in far(e, b):
                copy.start()
            e.t_tab[b, R : 2 * R] = own
            if TP > 3 * R + FAR:
                e.t_tab[b, 3 * R + FAR :] = jnp.zeros((TP - 3 * R - FAR, DN), BF)

        return stage

    def middle(b):
        def stage(e):
            for one, two in zip(near(e, b), mate(e, b), strict=True):
                one.wait_recv()
                two.start()

        return stage

    def finish(b):
        def stage(e):
            far_own(z, e.t_fsend.at[b], e.t_frecv.at[b])
            for copy in far(e, b):
                copy.wait()
            for copy in near(e, b):
                copy.wait_send()
            for copy in mate(e, b):
                copy.wait()
            e.t_tab[b, 3 * R : 3 * R + FAR] = e.t_frecv[b].astype(BF)
            e.tables[b] = e.t_tab[b]

        return stage

    return SimpleNamespace(
        launch=launch,
        begin=begin,
        middle=middle,
        finish=finish,
        ins=dict(nodes=vm(a.nodes)),
        outs=dict(tables=out((B, TP, DN), BF)),
        scr=dict(
            t_tab=pltpu.VMEM((B, TP, DN), BF),
            t_fsend=pltpu.VMEM((B, FAR, DN), F32),
            t_frecv=pltpu.VMEM((B, FAR, DN), F32),
            t_fs=dma(B, ns),
            t_fr=dma(B, ns),
            t_ns=dma(B, 2),
            t_nr=dma(B, 2),
            t_ms=dma(B, 2),
            t_mr=dma(B, 2),
        ),
    )


def message_part(z, a):
    R, DN, DE, TP, S, B = z.R, z.DN, z.DE, z.TP, z.S, z.B
    T = S // GROUP

    def body(e, step):
        sample, own = step // T, lax.rem(step, T)

        @pl.when(own == 0)
        def _():
            e.m_tabt[...] = dot_nt(e.m_wpt[...], e.t_tab[sample]).astype(BF)
            e.m_selft[...] = e.m_selfs[sample]
            e.m_acc[...] = jnp.zeros_like(e.m_acc)

        slots = [own * GROUP + g for g in range(GROUP)]
        line = pl.ds(sample, 1)
        value = dot(e.m_tabt[...], hot(side([e.nbr[s, line] for s in slots]), TP)) + dot(
            e.m_wet[...], side([e.m_edges[0, g] for g in range(GROUP)])
        )
        acc = e.m_acc[0:DN]
        count = e.m_acc[DN:]
        for g, s in enumerate(slots):
            live = e.live[s, line].astype(F32)
            act, slope = gelu_both(value[:, g * R : (g + 1) * R] + e.m_selft[...])
            e.slope[0, g] = slope.astype(BF)
            acc = acc + act * live
            count = count + live
        e.m_acc[0:DN] = acc
        e.m_acc[DN:] = count
        for b, ref in enumerate((e.part_a, e.part_b)):

            @pl.when(step == (b + 1) * T - 1)
            def _(ref=ref):
                ref[...] = e.m_acc[...].T.astype(BF)

    def prepare(e):
        e.m_wpt[...] = e.w_peer[...].T
        e.m_wet[...] = e.w_edge[...].T
        turned = e.w_self[...].T
        for b in range(B):
            e.m_selfs[b] = dot_nt(turned, e.nodes[b]) + e.vecs[0:8].T[:, 0:1]

    return SimpleNamespace(
        body=body,
        prepare=prepare,
        ins=dict(
            nodes=vm(a.nodes),
            m_edges=(a.edges_t, pl.BlockSpec((1, GROUP, DE, R), lambda i: (i // T, lax.rem(i, T), 0, 0))),
            nbr=vm(a.nbr),
            live=vm(a.live),
            w_self=vm(a.message_self),
            w_peer=vm(a.message_peer),
            w_edge=vm(a.message_edge),
        ),
        outs=dict(
            slope=(
                jax.ShapeDtypeStruct((B, S, DN, R), BF),
                pl.BlockSpec((1, GROUP, DN, R), lambda i: (i // T, lax.rem(i, T), 0, 0)),
            ),
            part_b=out((R, DN + LANES), BF),
        ),
        scr=dict(
            part_a=pltpu.VMEM((R, DN + LANES), BF),
            m_tabt=pltpu.VMEM((DN, TP), BF),
            m_selft=pltpu.VMEM((DN, R), F32),
            m_selfs=pltpu.VMEM((B, DN, R), F32),
            m_wpt=pltpu.VMEM((DN, DN), BF),
            m_wet=pltpu.VMEM((DN, DE), BF),
            m_acc=pltpu.VMEM((DN + LANES, R), F32),
        ),
    )


def forward_part(z, a, b, part):
    R, DN, DE, FF, Q, FAR, TP, ns, nn = z.R, z.DN, z.DE, z.FF, z.Q, z.FAR, z.TP, z.ns, z.nn
    W = DN + LANES

    def sums(e):
        s, n = place()
        found = []
        for k in range(1, nn):
            q = wrap(n + k, nn)
            rows = pl.ds(pl.multiple_of(q * Q, 16), Q)
            found.append(remote(part(e).at[rows], e.f_sum.at[k], e.f_ss.at[k], e.f_sr.at[k], (s, q)))
        return found

    def alls(e):
        s, n = place()
        rows = e.f_new.at[quarter(z)]
        return [
            remote(rows, rows, e.f_as.at[k], e.f_ar.at[k], (s, wrap(n + k, nn))) for k in range(1, nn)
        ]

    def near(e):
        s, n = place()
        found = []
        for i, (step, base) in enumerate(((1, 0), (-1, 2 * R))):
            rows = pl.ds(pl.multiple_of(base + n * Q, 16), Q)
            for k in range(nn):
                to = (wrap(s + step, ns), wrap(n + k, nn))
                found.append(remote(e.f_pe, e.f_tab.at[rows], e.f_ns.at[i, k], e.f_nr.at[i, k], to))
        return found

    def far(e):
        return far_copies(z, e.f_fsend, e.f_frecv, e.f_fs, e.f_fr)

    def begin(e):
        for copy in sums(e):
            copy.start()

    def compute(e):
        mine = quarter(z)
        for copy in sums(e):
            copy.wait()
        total = part(e)[mine].astype(F32)
        for k in range(1, nn):
            total = total + e.f_sum[k].astype(F32)
        count = total[:, DN : DN + 1]
        summed_act = total[:, :DN].astype(BF)
        summed = dot(summed_act, e.w_out[...]) + count * e.vecs[8:9]
        updated = e.nodes[b, mine].astype(F32) + summed / jnp.maximum(count, 1.0)
        xhat1, rstd1 = norm_rows(updated)
        hidden = xhat1 * e.vecs[9:10] + e.vecs[10:11]
        low = hidden.astype(BF)
        bias = side([e.vecs[16 + k : 17 + k] for k in range(FF // DN)])
        act, slope = gelu_both(dot(low, e.w_in[...]) + bias)
        act = act.astype(BF)
        xhat2, rstd2 = norm_rows(hidden + dot(act, e.w_ffn[...]) + e.vecs[11:12])
        fresh = (xhat2 * e.vecs[12:13] + e.vecs[13:14]).astype(BF)
        e.f_new[mine] = fresh
        e.f_pe[...] = dot_nt(fresh, e.ept[...]).astype(BF)
        for copy in alls(e):
            copy.start()
        for copy in near(e):
            copy.start()
        e.f_osum[...] = summed_act
        e.f_ocount[...] = total[:, DN:]
        e.f_ox1[...] = xhat1
        e.f_or1[...] = jnp.broadcast_to(rstd1, (Q, LANES))
        e.f_olow[...] = low
        e.f_oslope[...] = slope.astype(BF)
        e.f_oact[...] = act
        e.f_ox2[...] = xhat2
        e.f_or2[...] = jnp.broadcast_to(rstd2, (Q, LANES))
        e.f_oq[...] = fresh

    def spread(e):
        for copy in alls(e):
            copy.wait()
        own = dot_nt(e.f_new[...], e.ept[...]).astype(BF)
        e.f_tab[R : 2 * R] = own
        e.f_fsend[...] = dot_tn(hot(e.send[b], R), own)
        for copy in far(e):
            copy.start()
        e.f_onew[...] = e.f_new[...]
        if TP > 3 * R + FAR:
            e.f_tab[3 * R + FAR :] = jnp.zeros((TP - 3 * R - FAR, DE), BF)

    def finish(e):
        far_own(z, e.f_fsend, e.f_frecv)
        for copy in near(e):
            copy.wait()
        for copy in far(e):
            copy.wait()
        e.f_tab[3 * R : 3 * R + FAR] = e.f_frecv[...].astype(BF)
        e.f_otab[...] = e.f_tab[...]

    return SimpleNamespace(
        begin=begin,
        compute=compute,
        spread=spread,
        finish=finish,
        ins=dict(
            nodes=vm(a.nodes),
            w_out=vm(a.message_out),
            w_in=vm(a.hidden_in),
            w_ffn=vm(a.hidden_out),
            ept=vm(a.edge_peer_t),
        ),
        outs=dict(
            f_onew=out((R, DN), BF),
            f_otab=out((TP, DE), BF),
            f_osum=out((Q, DN), BF),
            f_ocount=out((Q, LANES), F32),
            f_ox1=out((Q, DN), F32),
            f_or1=out((Q, LANES), F32),
            f_olow=out((Q, DN), BF),
            f_oslope=out((Q, FF), BF),
            f_oact=out((Q, FF), BF),
            f_ox2=out((Q, DN), F32),
            f_or2=out((Q, LANES), F32),
            f_oq=out((Q, DN), BF),
        ),
        scr=dict(
            f_sum=pltpu.VMEM((nn, Q, W), BF),
            f_new=pltpu.VMEM((R, DN), BF),
            f_pe=pltpu.VMEM((Q, DE), BF),
            f_tab=pltpu.VMEM((TP, DE), BF),
            f_fsend=pltpu.VMEM((FAR, DE), F32),
            f_frecv=pltpu.VMEM((FAR, DE), F32),
            f_ss=dma(nn),
            f_sr=dma(nn),
            f_as=dma(nn),
            f_ar=dma(nn),
            f_ns=dma(2, nn),
            f_nr=dma(2, nn),
            f_fs=dma(ns),
            f_fr=dma(ns),
        ),
    )


def edge_part(z, a, first):
    R, DN, DE, TP, S, FAR, B = z.R, z.DN, z.DE, z.TP, z.S, z.FAR, z.B
    T = S // GROUP

    def body(e, step):
        sample, own = step // T, lax.rem(step, T)

        @pl.when(step == 0)
        def _():
            e.e_cols[...] = e.vecs[0:8].T[:DE]
            e.e_wnt[...] = e.e_wn[...].astype(F32).T.astype(BF)
            e.e_wot[...] = e.e_wo[...].astype(F32).T.astype(BF)
            for ref in (e.e_gacc, e.e_hacc, e.e_uacc, e.e_vacc, e.e_dwo, e.e_dwn):
                ref[...] = jnp.zeros_like(ref)

        for b, (table, fresh) in enumerate(((e.a_tab, e.a_new), (e.f_tab, e.f_new))):

            @pl.when(step == b * T)
            def _(table=table, fresh=fresh):
                e.e_tabt[...] = table[...].astype(F32).T.astype(BF)
                e.e_selft[...] = dot_nt(e.est[...], fresh[...]) + e.e_cols[:, 1:2]
                e.e_ptab[...] = jnp.zeros_like(e.e_ptab)
                e.e_sacc[...] = jnp.zeros_like(e.e_sacc)

        line = pl.ds(sample, 1)
        index = hot(side([e.nbr[own * GROUP + g, line] for g in range(GROUP)]), TP)
        edge = side([e.m_edges[0, g] for g in range(GROUP)])
        value = dot(e.e_tabt[...], index) + dot(e.e_wnt[...], edge)
        value = value + side([e.e_selft[...]] * GROUP)
        act, slope = gelu_both(value)
        act = act.astype(BF)
        shift_c, gain_c, bias_c = e.e_cols[:, 2:3], e.e_cols[:, 3:4], e.e_cols[:, 4:5]
        full = edge.astype(F32) + dot(e.e_wot[...], act) + shift_c
        full = full - jnp.mean(full, 0, keepdims=True)
        rstd = lax.rsqrt(jnp.mean(full * full, 0, keepdims=True) + EPS)
        xhat = full * rstd
        final = (xhat * gain_c + bias_c).astype(BF)
        cot = side([e.e_cot[0, g] for g in range(GROUP)]).astype(F32)
        scaled = cot * gain_c
        back = rstd * (
            scaled - jnp.mean(scaled, 0, keepdims=True) - xhat * jnp.mean(scaled * xhat, 0, keepdims=True)
        )
        low = back.astype(BF)
        e.e_dwo[...] += dot_nt(act, low)
        inner = (slope * dot(e.e_wo[...], low)).astype(BF)
        e.e_dwn[...] += dot_nt(edge, inner)
        part = (back + dot(e.e_wn[...], inner)).astype(BF)
        e.e_ptab[...] += dot_nt(index, inner)
        gain_g = cot * xhat
        low_f = low.astype(F32)
        inner_f = inner.astype(F32)
        s_acc, g_acc, h_acc, u_acc = e.e_sacc[...], e.e_gacc[...], e.e_hacc[...], e.e_uacc[...]
        for g in range(GROUP):
            cut = slice(g * R, (g + 1) * R)
            e.e_final[0, g] = final[:, cut]
            e.e_part[0, g] = part[:, cut]
            s_acc = s_acc + inner_f[:, cut]
            g_acc = g_acc + gain_g[:, cut]
            h_acc = h_acc + cot[:, cut]
            u_acc = u_acc + low_f[:, cut]
        e.e_sacc[...] = s_acc
        e.e_gacc[...] = g_acc
        e.e_hacc[...] = h_acc
        e.e_uacc[...] = u_acc
        ends = ((e.a_tgrad, e.a_fgrad, e.a_sgrad), (e.e_tgrad, e.e_fgrad, e.e_sgrad))
        for b, (tgrad, fgrad, sgrad) in enumerate(ends):

            @pl.when(step == (b + 1) * T - 1)
            def _(tgrad=tgrad, fgrad=fgrad, sgrad=sgrad):
                rows = e.e_ptab[...]
                tgrad[...] = rows.astype(BF)
                fgrad[...] = rows[3 * R : 3 * R + FAR]
                turned = e.e_sacc[...].T
                sgrad[...] = turned.astype(BF)
                e.e_vacc[0:1] += row_sum(turned)

        @pl.when(step == B * T - 1)
        def _():
            for k, ref in enumerate((e.e_uacc, e.e_gacc, e.e_hacc)):
                e.e_vacc[k + 1 : k + 2] = row_sum(ref[...].T)
            e.e_vgrad[...] = e.e_vacc[...]

    stream = pl.BlockSpec((1, GROUP, DE, R), lambda i: (i // T, lax.rem(i, T), 0, 0))
    return SimpleNamespace(
        body=body,
        ins=dict(
            a_tab=vm(first.f_otab),
            a_new=vm(first.f_onew),
            m_edges=(a.edges_t, stream),
            e_cot=(a.cot_t, stream),
            nbr=vm(a.nbr),
            est=vm(a.edge_self_t),
            e_wn=vm(a.edge_own),
            e_wo=vm(a.edge_out),
        ),
        outs=dict(
            e_final=(jax.ShapeDtypeStruct((B, S, DE, R), BF), stream),
            e_part=(jax.ShapeDtypeStruct((B, S, DE, R), BF), stream),
            e_tgrad=out((TP, DE), BF),
            e_fgrad=out((FAR, DE), F32),
            e_sgrad=out((R, DE), BF),
            e_vgrad=out((8, DE), F32),
            e_dwo=out((DE, DE), F32),
            e_dwn=out((DE, DE), F32),
        ),
        scr=dict(
            a_tgrad=pltpu.VMEM((TP, DE), BF),
            a_fgrad=pltpu.VMEM((FAR, DE), F32),
            a_sgrad=pltpu.VMEM((R, DE), BF),
            e_tabt=pltpu.VMEM((DE, TP), BF),
            e_cols=pltpu.VMEM((DE, 8), F32),
            e_selft=pltpu.VMEM((DE, R), F32),
            e_wnt=pltpu.VMEM((DE, DE), BF),
            e_wot=pltpu.VMEM((DE, DE), BF),
            e_ptab=pltpu.VMEM((TP, DE), F32),
            e_sacc=pltpu.VMEM((DE, R), F32),
            e_gacc=pltpu.VMEM((DE, R), F32),
            e_hacc=pltpu.VMEM((DE, R), F32),
            e_uacc=pltpu.VMEM((DE, R), F32),
            e_vacc=pltpu.VMEM((8, DE), F32),
        ),
    )


def backward_part(z, a, b, node, grads):
    R, DN, DE, FF, Q, FAR, TP, ns, nn = z.R, z.DN, z.DE, z.FF, z.Q, z.FAR, z.TP, z.ns, z.nn
    W = DN + LANES

    def near(e):
        s, n = place()
        tgrad = grads(e)[0]
        return [
            remote(
                tgrad.at[pl.ds(base, R)], e.b_near.at[k], e.b_ns.at[k], e.b_nr.at[k], (wrap(s + step, ns), n)
            )
            for k, (step, base) in enumerate(((-1, 0), (1, 2 * R)))
        ]

    def far(e):
        return far_copies(z, grads(e)[1], e.b_frecv, e.b_fs, e.b_fr)

    def sums(e):
        s, n = place()
        found = []
        for k in range(1, nn):
            q = wrap(n + k, nn)
            rows = pl.ds(pl.multiple_of(q * Q, 16), Q)
            found.append(remote(e.b_pair.at[:, rows], e.b_sum.at[k], e.b_ss.at[k], e.b_sr.at[k], (s, q)))
        return found

    def alls(e):
        s, n = place()
        rows = e.b_all.at[quarter(z)]
        return [
            remote(rows, rows, e.b_as.at[k], e.b_ar.at[k], (s, wrap(n + k, nn))) for k in range(1, nn)
        ]

    def begin(e):
        for copy in near(e):
            copy.start()
        for copy in far(e):
            copy.start()

    def gather(e):
        tgrad, fgrad, sgrad = grads(e)
        far_own(z, fgrad, e.b_frecv)
        for copy in near(e):
            copy.wait()
        for copy in far(e):
            copy.wait()
        peer = (
            tgrad[R : 2 * R].astype(F32)
            + e.b_near[0].astype(F32)
            + e.b_near[1].astype(F32)
            + dot(hot(e.send[b], R), e.b_frecv[...].astype(BF))
        )
        e.b_pair[0] = peer.astype(BF)
        e.b_pair[1] = sgrad[...]
        for copy in sums(e):
            copy.start()

    def compute(e):
        mine = quarter(z)
        for copy in sums(e):
            copy.wait()
        peer = e.b_pair[0, mine].astype(F32)
        own = e.b_pair[1, mine].astype(F32)
        for k in range(1, nn):
            peer = peer + e.b_sum[k, 0].astype(F32)
            own = own + e.b_sum[k, 1].astype(F32)
        peer = peer.astype(BF)
        own = own.astype(BF)
        final = e.cot[b, mine].astype(F32) + dot(own, e.est[...]) + dot(peer, e.ept[...])
        xhat2 = e.b_x2[...]
        mid = norm_rows_back(xhat2, e.b_r2[:, 0:1], final * e.vecs[12:13])
        mid_low = mid.astype(BF)
        ffn = (e.b_slope[...].astype(F32) * dot_nt(mid_low, e.w_ffn[...])).astype(BF)
        hidden = mid + dot_nt(ffn, e.w_in[...])
        xhat1 = e.b_x1[...]
        grad = norm_rows_back(xhat1, e.b_r1[:, 0:1], hidden * e.vecs[9:10])
        count = e.b_count[:, 0:1]
        low = (grad / jnp.maximum(count, 1.0)).astype(BF)
        e.b_all[mine] = side([low, e.b_count[...].astype(BF)])
        for copy in alls(e):
            copy.start()
        e.b_omid[...] = mid_low
        e.b_offn[...] = ffn
        e.b_olow[...] = low
        e.b_opeer[...] = peer
        e.b_oself[...] = own
        wide = row_sum(ffn.astype(F32))
        e.b_ovec[...] = jnp.concatenate(
            [
                row_sum(low.astype(F32) * count),
                row_sum(hidden * xhat1),
                row_sum(hidden),
                row_sum(mid_low.astype(F32)),
                row_sum(final * xhat2),
                row_sum(final),
            ]
            + [wide[:, k * DN : (k + 1) * DN] for k in range(FF // DN)]
            + [jnp.zeros((6, DN), F32)],
            0,
        )

    def finish(e):
        for copy in alls(e):
            copy.wait()
        e.b_oall[...] = e.b_all[...]

    return SimpleNamespace(
        begin=begin,
        gather=gather,
        compute=compute,
        finish=finish,
        ins=dict(
            b_count=vm(node.f_ocount),
            b_x1=vm(node.f_ox1),
            b_r1=vm(node.f_or1),
            b_slope=vm(node.f_oslope),
            b_x2=vm(node.f_ox2),
            b_r2=vm(node.f_or2),
            cot=vm(a.node_cot),
            w_in=vm(a.hidden_in),
            w_ffn=vm(a.hidden_out),
            est=vm(a.edge_self_t),
            ept=vm(a.edge_peer_t),
        ),
        outs=dict(
            b_oall=out((R, W), BF),
            b_omid=out((Q, DN), BF),
            b_offn=out((Q, FF), BF),
            b_olow=out((Q, DN), BF),
            b_opeer=out((Q, DE), BF),
            b_oself=out((Q, DE), BF),
            b_ovec=out((16, DN), F32),
        ),
        scr=dict(
            b_near=pltpu.VMEM((2, R, DE), BF),
            b_frecv=pltpu.VMEM((FAR, DE), F32),
            b_pair=pltpu.VMEM((2, R, DE), BF),
            b_sum=pltpu.VMEM((nn, 2, Q, DE), BF),
            b_all=pltpu.VMEM((R, W), BF),
            b_ns=dma(2),
            b_nr=dma(2),
            b_fs=dma(ns),
            b_fr=dma(ns),
            b_ss=dma(nn),
            b_sr=dma(nn),
            b_as=dma(nn),
            b_ar=dma(nn),
        ),
    )


def last_part(z, a, spread, slope, part, tables):
    R, DN, DE, TP, S, FAR, B = z.R, z.DN, z.DE, z.TP, z.S, z.FAR, z.B
    T = S // GROUP

    def body(e, step):
        sample, own = lax.rem(step // T, B), lax.rem(step, T)
        for b, ref in enumerate((e.a_all, e.b_all)):

            @pl.when(step == b * T)
            def _(ref=ref, b=b):
                pltpu.make_async_copy(e.g_tables.at[b], e.g_tab, e.g_ts.at[b]).start()
                e.g_ht[b] = dot_nt(e.w_out[...], ref[:, 0:DN])
                e.g_ptab[...] = jnp.zeros_like(e.g_ptab)
                e.g_sacc[...] = jnp.zeros_like(e.g_sacc)
                if b == 0:
                    e.g_dwe[...] = jnp.zeros_like(e.g_dwe)
                    e.g_vec[...] = jnp.zeros_like(e.g_vec)

        line = pl.ds(sample, 1)
        slots = [own * GROUP + g for g in range(GROUP)]

        def pieces():
            return [
                (e.g_slope[0, g].astype(F32) * (e.g_ht[sample] * e.live[s, line].astype(F32))).astype(BF)
                for g, s in enumerate(slots)
            ]

        @pl.when(step < B * T)
        def _():
            index = hot(side([e.nbr[s, line] for s in slots]), TP)
            edge = side([e.m_edges[0, g] for g in range(GROUP)])
            inner = pieces()
            acc = e.g_sacc[...]
            for piece in inner:
                acc = acc + piece.astype(F32)
            e.g_sacc[...] = acc
            inner = side(inner)
            e.g_ptab[...] += dot_nt(inner, index)
            e.g_dwe[...] += dot_nt(inner, edge)

        @pl.when(step >= B * T)
        def _():
            back = dot(e.w_edge[...], side(pieces()))
            for g in range(GROUP):
                e.g_edge[0, g] = (back[:, g * R : (g + 1) * R] + e.g_part[0, g].astype(F32)).astype(BF)

        for b in range(B):

            @pl.when(step == (b + 1) * T - 1)
            def _(b=b):
                self_t = e.g_sacc[...].astype(BF)
                peer_t = e.g_ptab[...].astype(BF)
                e.o_rows[b] = dot(e.w_peer[...], peer_t).astype(BF)
                e.o_rows[b, :, R : 2 * R] = (
                    dot(e.w_peer[...], peer_t[:, R : 2 * R]) + dot(e.w_self[...], self_t)
                ).astype(BF)
                pltpu.make_async_copy(e.g_tables.at[b], e.g_tab, e.g_ts.at[b]).wait()
                dself = dot(self_t, e.nodes[b])
                dpeer = dot(peer_t, e.g_tab[...])
                e.g_dself[...] = dself if b == 0 else e.g_dself[...] + dself
                e.g_dpeer[...] = dpeer if b == 0 else e.g_dpeer[...] + dpeer
                e.g_vec[0:1] += row_sum(e.g_sacc[...].T)

    def always(i):
        return (lax.rem(i // T, B), lax.rem(i, T), 0, 0)

    def early(i):
        k = jnp.minimum(i, B * T - 1)
        return (k // T, lax.rem(k, T), 0, 0)

    def late(i):
        k = jnp.maximum(i - B * T, 0)
        return (k // T, lax.rem(k, T), 0, 0)

    return SimpleNamespace(
        body=body,
        ins=dict(
            a_all=vm(spread),
            g_slope=(slope, pl.BlockSpec((1, GROUP, DN, R), always)),
            g_part=(part, pl.BlockSpec((1, GROUP, DE, R), late)),
            g_tables=(tables, pl.BlockSpec(memory_space=pl.ANY)),
            nodes=vm(a.nodes),
            m_edges=(a.edges_t, pl.BlockSpec((1, GROUP, DE, R), early)),
            nbr=vm(a.nbr),
            live=vm(a.live),
            w_self=vm(a.message_self),
            w_peer=vm(a.message_peer),
            w_edge=vm(a.message_edge),
            w_out=vm(a.message_out),
        ),
        outs=dict(g_edge=(jax.ShapeDtypeStruct((B, S, DE, R), BF), pl.BlockSpec((1, GROUP, DE, R), late))),
        scr=dict(
            g_tab=pltpu.VMEM((TP, DN), BF),
            g_ts=dma(B),
            g_ht=pltpu.VMEM((B, DN, R), F32),
            g_ptab=pltpu.VMEM((DN, TP), F32),
            g_sacc=pltpu.VMEM((DN, R), F32),
            g_dself=pltpu.VMEM((DN, DN), F32),
            g_dpeer=pltpu.VMEM((DN, DN), F32),
            g_dwe=pltpu.VMEM((DN, DE), F32),
            g_vec=pltpu.VMEM((8, DN), F32),
            o_rows=pltpu.VMEM((B, DN, TP), BF),
        ),
    )


def nodes_part(z, a, spreads):
    R, DN, FAR, TP, ns, nn, B = z.R, z.DN, z.FAR, z.TP, z.ns, z.nn, z.B
    L = DN // nn

    pairs = nn // 2

    def mates(e, b):
        s, n = place()
        other = flip(n, 0)
        found = []
        for k in range(pairs):
            q = lax.rem(other, 2) + 2 * k
            rows = pl.ds(pl.multiple_of(q * L, 16), L)
            found.append(
                remote(e.o_rows.at[b, rows], e.o_half.at[b, k], e.o_hs.at[b, k], e.o_hr.at[b, k], (s, other))
            )
        return found

    def sums(e, b):
        s, n = place()
        found = []
        for k in range(1, pairs):
            q = wrap(n + 2 * k, nn)
            found.append(
                remote(e.o_pair.at[b, q // 2], e.o_sum.at[b, k - 1], e.o_ss.at[b, k], e.o_sr.at[b, k], (s, q))
            )
        return found

    def near(e, b):
        s, n = place()
        return [
            remote(
                e.o_send.at[b, pl.ds(2 * k * R, R)],
                e.o_near.at[b, k],
                e.o_ns.at[b, k],
                e.o_nr.at[b, k],
                (wrap(s + step, ns), n),
            )
            for k, step in enumerate((-1, 1))
        ]

    def far(e, b):
        return far_copies(z, e.o_fsend.at[b], e.o_frecv.at[b], e.o_fs.at[b], e.o_fr.at[b])

    def begin(b):
        def stage(e):
            for copy in mates(e, b):
                copy.start()

        return stage

    def pair(b):
        def stage(e):
            s, n = place()
            for copy in mates(e, b):
                copy.wait()
            for k in range(pairs):
                q = lax.rem(n, 2) + 2 * k
                rows = pl.ds(pl.multiple_of(q * L, 16), L)
                e.o_pair[b, k] = (e.o_rows[b, rows].astype(F32) + e.o_half[b, k].astype(F32)).astype(BF)
            for copy in sums(e, b):
                copy.start()

        return stage

    def middle(b):
        def stage(e):
            s, n = place()
            for copy in sums(e, b):
                copy.wait()
            total = e.o_pair[b, n // 2].astype(F32)
            for k in range(1, pairs):
                total = total + e.o_sum[b, k - 1].astype(F32)
            turned = total.T
            e.o_send[b] = turned.astype(BF)
            e.o_fsend[b] = turned[3 * R : 3 * R + FAR]
            for copy in near(e, b):
                copy.start()
            for copy in far(e, b):
                copy.start()
            column = pl.ds(pl.multiple_of(n * L, L), L)
            spread = spreads(e)[b]
            count = spread[:, DN : DN + 1].astype(F32)
            e.o_grad[b] = turned[R : 2 * R] + spread[:, column].astype(F32) * jnp.maximum(count, 1.0)

        return stage

    def finish(b):
        def stage(e):
            far_own(z, e.o_fsend.at[b], e.o_frecv.at[b])
            for copy in near(e, b):
                copy.wait()
            for copy in far(e, b):
                copy.wait()
            e.o_grad[b] += (
                e.o_near[b, 0].astype(F32)
                + e.o_near[b, 1].astype(F32)
                + dot(hot(e.send[b], R), e.o_frecv[b].astype(BF))
            )

        return stage

    return SimpleNamespace(
        begin=begin,
        pair=pair,
        middle=middle,
        finish=finish,
        ins={},
        outs=dict(o_grad=out((B, R, L), F32)),
        scr=dict(
            o_half=pltpu.VMEM((B, pairs, L, TP), BF),
            o_pair=pltpu.VMEM((B, pairs, L, TP), BF),
            o_sum=pltpu.VMEM((B, pairs - 1, L, TP), BF),
            o_hs=dma(B, pairs),
            o_hr=dma(B, pairs),
            o_send=pltpu.VMEM((B, TP, L), BF),
            o_near=pltpu.VMEM((B, 2, R, L), BF),
            o_fsend=pltpu.VMEM((B, FAR, L), F32),
            o_frecv=pltpu.VMEM((B, FAR, L), F32),
            o_ss=dma(B, pairs),
            o_sr=dma(B, pairs),
            o_ns=dma(B, 2),
            o_nr=dma(B, 2),
            o_fs=dma(B, ns),
            o_fr=dma(B, ns),
        ),
    )


def cut(total, start, rounds):
    unit = 16 << SPLITS
    units = max(3 * rounds, -(-total // unit))
    count = 3 * rounds
    sizes = [units // count + (1 if k < units % count else 0) for k in range(count)]
    starts = [start + sum(sizes[:k]) * unit for k in range(count)]
    return start + units * unit, [(at, size * unit) for at, size in zip(starts, sizes)]


def bit_orders(z):
    nbr = [("nbr", k) for k in range(z.nn.bit_length() - 1)]
    space = [("space", k) for k in range(z.ns.bit_length() - 1)]
    first, ring, rest = nbr[:1], [nbr[1], space[0], space[1]], nbr[2:] + space[2:]
    return [first + ring[k:] + ring[:k] + rest[: SPLITS - 4] for k in range(3)], rest[SPLITS - 4 :]


def pack_rows(z):
    DN, DE, FF = z.DN, z.DE, z.FF
    early = dict(wi=FF, wf=FF, wo=DN, es=DE, ep=DE)
    late = dict(ws=DN, wp=DN, we=DE, own=DE, vec=32)
    at, row = SimpleNamespace(), 0
    for group in (early, late):
        first = row
        for name, size in group.items():
            setattr(at, name, row)
            row += size
        used = row
        row, parts = cut(used - first, first, ROUNDS if group is early else 1)
        if group is early:
            at.early, at.early_end = parts, used
        else:
            at.late, at.late_end = parts, used
    at.span = row
    at.rows = -(-row // (2 * DN)) * 2 * DN
    at.middle = at.late[0][0]
    return at


def sum_part(z, a, at, early):
    DN, DE, FF, B = z.DN, z.DE, z.FF, z.B
    orders, whole = bit_orders(z)
    phases = len(orders[0])
    most = max(size for _, size in at.early + at.late) >> phases
    parts = at.early + at.late
    groups = [range(k, k + 3) for k in range(0, len(parts), 3)]
    count = len(parts)

    def bit_value(axis, bit):
        s, n = place()
        return lax.rem((n if axis == "nbr" else s) // (1 << bit), 2)

    def segment(part, depth):
        start, size = parts[part]
        for axis, bit in orders[part % 3][:depth]:
            size //= 2
            start = start + bit_value(axis, bit) * size
        return start, size

    def down(e, part, depth):
        axis, bit = orders[part % 3][depth]
        start, size = segment(part, depth)
        size //= 2
        give = pl.multiple_of(start + (1 - bit_value(axis, bit)) * size, 16)
        base = parts[part][0] + parts[part][1] - 2 * size
        copy = remote(
            e.s_buf.at[pl.ds(give, size)],
            e.s_recv.at[pl.ds(base, size)],
            e.s_ds.at[part, depth],
            e.s_dr.at[part, depth],
            across(axis, bit),
        )
        return copy, size, base

    def up(e, part, depth):
        start, size = segment(part, depth + 1)
        rows = pl.ds(pl.multiple_of(start, 16), size)
        src = e.s_buf if depth == phases - 1 else e.s_out
        return remote(
            src.at[rows],
            e.s_out.at[rows],
            e.s_us.at[part, depth],
            e.s_ur.at[part, depth],
            across(*orders[part % 3][depth]),
        )

    def keep_own(e, part):
        start, size = segment(part, phases)
        rows = pl.ds(pl.multiple_of(start, 16), size)
        return pltpu.make_async_copy(e.s_buf.at[rows], e.s_out.at[rows], e.s_os.at[part])

    def begin(group):
        def stage(e):
            for part in groups[group]:
                down(e, part, 0)[0].start()

        return stage

    def fold(group, depth):
        def stage(e):
            for part in groups[group]:
                copy, size, base = down(e, part, depth)
                copy.wait()
                start, _ = segment(part, depth + 1)
                keep = pl.ds(pl.multiple_of(start, 16), size)
                value = (e.s_buf[keep].astype(F32) + e.s_recv[pl.ds(base, size)].astype(F32)).astype(BF)
                if depth + 1 < phases:
                    e.s_buf[keep] = value
                    down(e, part, depth + 1)[0].start()
                    continue
                for k, (axis, bit) in enumerate(whole):
                    e.s_buf[keep] = value
                    copy = remote(
                        e.s_buf.at[keep],
                        e.s_more.at[part, k, pl.ds(0, size)],
                        e.s_ms.at[part, k],
                        e.s_mr.at[part, k],
                        across(axis, bit),
                    )
                    copy.start()
                    copy.wait()
                    value = (value.astype(F32) + e.s_more[part, k, 0:size].astype(F32)).astype(BF)
                e.s_buf[keep] = value
                keep_own(e, part).start()
                up(e, part, depth).start()

        return stage

    def spread(group, depth):
        def stage(e):
            for part in groups[group]:
                up(e, part, depth).wait()
                if depth == phases - 1:
                    keep_own(e, part).wait()
                if depth:
                    up(e, part, depth - 1).start()

        return stage

    def put(e, row, value):
        e.s_buf[row : row + value.shape[0], : value.shape[1]] = value.astype(BF)

    def clear(e, first, last):
        if last > first:
            e.s_buf[first:last] = jnp.zeros((last - first, DN), BF)

    def pack_early(e):
        def two(one, other):
            return jnp.concatenate([one[...], other[...]], 0)

        low, ffn = two(e.p_low0, e.p_low1), two(e.p_ffn0, e.b_offn)
        act, mid = two(e.p_act0, e.p_act1), two(e.p_mid0, e.b_omid)
        for k in range(FF // DN):
            put(e, at.wi + k * DN, dot_tn(low, ffn[:, k * DN : (k + 1) * DN]))
        for k in range(FF // DN):
            put(e, at.wf + k * DN, dot_tn(act[:, k * DN : (k + 1) * DN], mid))
        put(e, at.wo, dot_tn(two(e.p_sum0, e.p_sum1), two(e.p_grad0, e.b_olow)))
        fresh = two(e.p_new0, e.p_new1)
        put(e, at.es, dot_tn(two(e.p_self0, e.b_oself), fresh))
        put(e, at.ep, dot_tn(two(e.p_peer0, e.b_opeer), fresh))
        clear(e, at.early_end, at.middle)

    def pack_late(e):
        put(e, at.ws, e.g_dself[...].T)
        put(e, at.wp, e.g_dpeer[...].T)
        put(e, at.we, e.g_dwe[...].T)
        gap = jnp.zeros((DE, 256 - DE), F32)
        put(e, at.own, side([e.p_dwn[...], gap, e.p_dwo[...], gap]))
        narrow = side([e.p_vec[...], jnp.zeros((8, DN - DE), F32)])
        put(e, at.vec, jnp.concatenate([e.p_vec0[...] + e.b_ovec[...], narrow, e.g_vec[...]], 0))
        clear(e, at.late_end, at.span)

    f0, f1, b0, ee = early
    return SimpleNamespace(
        begin=begin,
        fold=fold,
        spread=spread,
        pack_early=pack_early,
        pack_late=pack_late,
        phases=phases,
        ins=dict(
            p_low0=vm(f0.f_olow),
            p_low1=vm(f1.f_olow),
            p_act0=vm(f0.f_oact),
            p_act1=vm(f1.f_oact),
            p_sum0=vm(f0.f_osum),
            p_sum1=vm(f1.f_osum),
            p_new0=vm(f0.f_oq),
            p_new1=vm(f1.f_oq),
            p_ffn0=vm(b0.b_offn),
            p_mid0=vm(b0.b_omid),
            p_grad0=vm(b0.b_olow),
            p_self0=vm(b0.b_oself),
            p_peer0=vm(b0.b_opeer),
            p_vec0=vm(b0.b_ovec),
            p_vec=vm(ee.e_vgrad),
            p_dwo=vm(ee.e_dwo),
            p_dwn=vm(ee.e_dwn),
        ),
        outs=dict(s_out=(jax.ShapeDtypeStruct((at.rows, DN), BF), pl.BlockSpec(memory_space=pl.ANY))),
        scr=dict(
            s_buf=pltpu.VMEM((at.span, DN), BF),
            s_recv=pltpu.VMEM((at.span, DN), BF),
            s_os=dma(count),
            s_more=pltpu.VMEM((count, len(whole), most, DN) if whole else (16, DN), BF),
            s_ms=dma(count, max(1, len(whole))),
            s_mr=dma(count, max(1, len(whole))),
            s_ds=dma(count, phases),
            s_dr=dma(count, phases),
            s_us=dma(count, phases),
            s_ur=dma(count, phases),
        ),
    )


def unpack_kernel(z, packed, at, edge, final, node, fresh):
    DN, DE, FF, B, S, R = z.DN, z.DE, z.FF, z.B, z.S, z.R
    size, wide = 2 * DN, FF // DN
    half = wide // 2
    steps = at.rows // size
    slots = S // 3
    blocks = B * 3

    def kernel(p, *refs):
        given, (ws, wp, we, wo, wi, wf, es, ep, own, eo, *vectors), rest = refs[: B + 3], refs[B + 3 : B + 25], refs[B + 25 :]
        step = pl.program_id(0)

        @pl.when(step < blocks)
        def _():
            rest[0][...] = given[0][...]
            rest[1][...] = given[1][...]

        @pl.when(step == 0)
        def _():
            rest[2][...] = given[2][...]
            for b in range(B):
                rest[3][b] = given[3 + b][...]

        def take(row, count):
            return p[row % size : row % size + count].astype(F32)

        def at_row(row):
            return pl.when(step == row // size)

        @pl.when(step < half)
        def _():
            wi[:, :DN] = p[:DN].astype(F32)
            wi[:, DN:] = p[DN:].astype(F32)

        @pl.when(jnp.logical_and(step >= half, step < 2 * half))
        def _():
            wf[...] = p[...].astype(F32)

        @at_row(at.wo)
        def _():
            wo[...] = take(at.wo, DN)

        @at_row(at.es)
        def _():
            es[...] = take(at.es, DE)
            ep[...] = take(at.ep, DE)

        @at_row(at.ws)
        def _():
            ws[...] = take(at.ws, DN)

        @at_row(at.wp)
        def _():
            wp[...] = take(at.wp, DN)

        @at_row(at.we)
        def _():
            we[...] = take(at.we, DE)
            both = take(at.own, DE)
            own[...] = both[:, :DE]
            eo[...] = both[:, 256 : 256 + DE]
            vec = take(at.vec, 32)
            vectors[0][...] = side([vec[6 + k : 7 + k] for k in range(wide)]).reshape(FF)
            for ref, row in zip(vectors[1:], (24, 0, 1, 2, 3, 4, 5, 16, 17, 18, 19), strict=True):
                count = ref.shape[0]
                ref[...] = vec[row : row + 1, :count].reshape(count)

    shapes = [(DN, DN), (DN, DN), (DE, DN), (DN, DN), (DN, FF), (FF, DN), (DE, DN), (DE, DN), (DE, DE), (DE, DE)]
    shapes += [(FF,)] + [(DN,)] * 7 + [(DE,)] * 4
    here = pl.BlockSpec(memory_space=pltpu.VMEM)
    specs = [here] * len(shapes)
    specs[4] = pl.BlockSpec((DN, size), lambda i: (0, jnp.clip(i, 0, half - 1)))
    specs[5] = pl.BlockSpec((size, DN), lambda i: (jnp.clip(i - half, 0, half - 1), 0))

    def turn(i):
        k = jnp.minimum(i, blocks - 1)
        return (k // 3, lax.rem(k, 3), 0, 0)

    stream = pl.BlockSpec((1, slots, DE, R), turn)
    return pl.pallas_call(
        kernel,
        grid=(steps,),
        out_shape=[jax.ShapeDtypeStruct(shape, F32) for shape in shapes]
        + [jax.ShapeDtypeStruct(x.shape, x.dtype) for x in (edge, final, node)]
        + [jax.ShapeDtypeStruct((B,) + fresh[0].shape, fresh[0].dtype)],
        in_specs=[pl.BlockSpec((size, DN), lambda i: (i, 0)), stream, stream, here] + [here] * B,
        out_specs=specs + [stream, stream, here, here],
        compiler_params=pltpu.CompilerParams(vmem_limit_bytes=VMEM_LIMIT),
    )(packed, edge, final, node, *fresh)


def local(
    nodes,
    edges,
    neighbors,
    slot_live,
    send_rows,
    message_self,
    message_peer,
    message_edge,
    message_bias,
    message_out,
    message_shift,
    first_gain,
    first_shift,
    hidden_in,
    hidden_bias,
    hidden_out,
    output_bias,
    second_gain,
    second_shift,
    edge_self,
    edge_peer,
    edge_own,
    edge_bias,
    edge_out,
    edge_shift,
    third_gain,
    third_shift,
    node_cot,
    edge_cot,
):
    a = SimpleNamespace(**locals())
    B, R, DN = nodes.shape
    S, DE = edges.shape[2:]
    ns, nn = lax.axis_size("space"), lax.axis_size("nbr")
    CAP = send_rows.shape[2]
    FAR = ns * CAP
    TP = -(-(3 * R + FAR) // LANES) * LANES
    z = SimpleNamespace(
        B=B, R=R, DN=DN, S=S, DE=DE, ns=ns, nn=nn, CAP=CAP, FAR=FAR, TP=TP, FF=hidden_in.shape[1], Q=R // nn
    )
    ids = itertools.count(1)
    a.edges_t = edges.transpose(0, 2, 3, 1)
    a.cot_t = edge_cot.transpose(0, 2, 3, 1)
    a.nbr = neighbors.transpose(2, 0, 1)
    a.live = slot_live.transpose(2, 0, 1)
    a.edge_self_t, a.edge_peer_t = edge_self.T, edge_peer.T
    T = S // GROUP

    def plain(part):
        return SimpleNamespace(ins=part, outs={}, scr={})

    heavy = ("w_in", "w_ffn")
    small, table, message = setup_part(z, a), table_part(z, a), message_part(z, a)
    node0 = forward_part(z, a, 0, lambda e: e.part_a)
    f0 = build(
        ids,
        [small, table, message, node0],
        lambda: near_cross(z) + same_lane(z),
        2 * T,
        {
            0: [
                table.launch(0),
                small.begin,
                table.begin(0),
                message.prepare,
                table.middle(0),
                table.launch(1),
                table.begin(1),
                table.finish(0),
            ],
            T: [node0.begin],
        },
        {
            1: [table.middle(1)],
            3: [table.finish(1)],
            T + 1: [ready, node0.compute],
            T + 3: [node0.spread],
            2 * T - 1: [node0.finish],
        },
        heavy,
    )
    shared = plain(dict(vecs=vm(f0.vecs), send=vm(f0.send)))

    edge = edge_part(z, a, f0)
    node1 = forward_part(z, a, 1, lambda e: e.part_b)
    back0 = backward_part(z, a, 0, f0, lambda e: (e.a_tgrad, e.a_fgrad, e.a_sgrad))
    f1 = build(
        ids,
        [shared, plain(dict(part_b=vm(f0.part_b))), edge, node1, back0],
        lambda: near_cross(z) + same_lane(z),
        2 * T,
        {0: [node1.begin], T: [back0.begin]},
        {
            1: [ready, node1.compute],
            3: [node1.spread],
            T - 1: [node1.finish],
            T + 1: [back0.gather],
            T + 2: [back0.compute],
            2 * T - 1: [back0.finish],
        },
        heavy,
    )

    at = pack_rows(z)
    last = last_part(z, a, f1.b_oall, f0.slope, f1.e_part, f0.tables)
    back1 = backward_part(z, a, 1, f1, lambda e: (e.e_tgrad, e.e_fgrad, e.e_sgrad))
    outer = nodes_part(z, a, lambda e: (e.a_all, e.b_all))
    total = sum_part(z, a, at, (f0, f1, f1, f1))
    for name, (shape, spec) in back1.outs.items():
        back1.scr[name] = pltpu.VMEM(shape.shape, shape.dtype)
    back1.outs = {}
    D, late = total.phases, ROUNDS

    def fold(d):
        return [total.fold(k, d) for k in range(ROUNDS)]

    def gather(d):
        return [total.spread(k, d) for k in range(ROUNDS)]

    lf, ls = (lambda d: total.fold(late, d)), (lambda d: total.spread(late, d))
    f, g = total.fold, total.spread
    after = {
        1: [back1.gather],
        2: [ready, back1.compute, total.pack_early] + [total.begin(k) for k in range(ROUNDS)],
        3: [f(0, 0)],
        T - 1: [back1.finish, f(1, 0)],
        T: [f(0, 1)],
        T + 1: [outer.pair(0), f(1, 1)],
        T + 2: [f(0, 2)],
        T + 3: [f(1, 2)],
        2 * T - 1: [f(0, 3), outer.middle(0), outer.begin(1), total.pack_late, total.begin(late)],
        2 * T: [f(1, 3), lf(0)],
        2 * T + 1: [f(0, 4), outer.pair(1)],
        2 * T + 2: [lf(1), f(1, 4)],
        2 * T + 3: [lf(2), g(0, 4)],
        2 * T + 4: [outer.middle(1), lf(3)],
        3 * T: [g(1, 4), lf(4)],
        3 * T + 1: [g(0, 3)],
        3 * T + 2: [ls(4), g(1, 3)],
        3 * T + 3: [g(0, 2), ls(3)],
        4 * T - 1: [g(1, 2), ls(2), g(0, 1), ls(1), outer.finish(0), g(1, 1), ls(0), g(0, 0), outer.finish(1), g(1, 0)],
    }
    grads = dict(e_tgrad=vm(f1.e_tgrad), e_fgrad=vm(f1.e_fgrad), e_sgrad=vm(f1.e_sgrad))
    f2 = build(
        ids,
        [shared, plain(grads), last, back1, outer, total],
        lambda: [(lax.axis_index("space"), wrap(lax.axis_index("nbr") + k, nn)) for k in range(1, nn)] + same_lane(z),
        4 * T,
        {0: [back1.begin], T: [outer.begin(0)]},
        after,
        heavy + ("p_act0", "p_act1", "p_ffn0"),
    )
    ws, wp, we, wo, wi, wf, es, ep, own, eo, *vectors = unpack_kernel(
        z, f2.s_out, at, f2.g_edge, f1.e_final, f2.o_grad, [f0.f_onew, f1.f_onew]
    )
    hidden, mb, ms, fg, fs, ob, sg, ss, eb, esh, tg, ts, edge_grad, new_edges, node_grad, new_nodes = vectors
    return (
        new_nodes,
        new_edges.transpose(0, 3, 1, 2),
        node_grad,
        edge_grad.transpose(0, 3, 1, 2),
        ws,
        wp,
        we,
        mb,
        wo,
        ms,
        fg,
        fs,
        wi,
        hidden,
        wf,
        ob,
        sg,
        ss,
        es.T,
        ep.T,
        own,
        eb,
        eo,
        esh,
        tg,
        ts,
    )


def solution(mesh):
    tall = P(None, "space", None)
    slots = P(None, "space", "nbr", None)
    marks = P(None, "space", "nbr")
    return jax.shard_map(
        local,
        mesh=mesh,
        in_specs=(tall, slots, marks, marks, tall) + (P(),) * 22 + (tall, slots),
        out_specs=(tall, slots, marks, slots) + (P(),) * 22,
        check_vma=False,
    )
```

```python
import itertools
from types import SimpleNamespace

import jax
import jax.numpy as jnp
from jax import lax
from jax.experimental import pallas as pl
from jax.experimental.pallas import tpu as pltpu
from jax.sharding import PartitionSpec as P

EPS = 1e-05
F32 = jnp.float32
BF = jnp.bfloat16
MESH = pl.DeviceIdType.MESH
VMEM_LIMIT = 62 << 20
C0 = 0.7978845608028654
C1 = C0 * 0.044715
GROUP = 3
LANES = 128
SPLITS = 5
ROUNDS = 2


def dot(left, right):
    return jnp.dot(left, right, preferred_element_type=F32)


def dot_nt(left, right):
    return lax.dot_general(left, right, (((1,), (1,)), ((), ())), preferred_element_type=F32)


def dot_tn(left, right):
    return lax.dot_general(left, right, (((0,), (0,)), ((), ())), preferred_element_type=F32)


def gelu_both(x):
    one = jnp.ones((), x.dtype)
    a, b = one * C0, one * C1
    x2 = x * x
    half = one * 0.5 * jnp.tanh(x * (a + b * x2)) + one * 0.5
    act = x * half
    return act, half + act * (one - half) * (one * (2 * C0) + one * (6 * C1) * x2)


def norm_rows(value):
    centre = value - jnp.mean(value, -1, keepdims=True)
    rstd = lax.rsqrt(jnp.mean(centre * centre, -1, keepdims=True) + EPS)
    return centre * rstd, rstd


def norm_rows_back(xhat, rstd, grad):
    return rstd * (
        grad
        - jnp.mean(grad, -1, keepdims=True)
        - xhat * jnp.mean(grad * xhat, -1, keepdims=True)
    )


def hot(index, rows):
    it = lax.broadcasted_iota(jnp.int32, (rows, index.shape[1]), 0)
    return jnp.where(it == index, 1.0, 0.0).astype(BF)


def side(refs):
    return jnp.concatenate(refs, 1)


def row_sum(value):
    return jnp.sum(value, 0, keepdims=True)


def vm(array):
    return (array, pl.BlockSpec(memory_space=pltpu.VMEM))


def out(shape, dtype):
    return (jax.ShapeDtypeStruct(shape, dtype), pl.BlockSpec(memory_space=pltpu.VMEM))


def dma(*shape):
    return pltpu.SemaphoreType.DMA(shape)


def remote(src, dst, send, recv, device):
    return pltpu.make_async_remote_copy(
        src_ref=src, dst_ref=dst, send_sem=send, recv_sem=recv, device_id=device, device_id_type=MESH
    )


def build(ids, parts, partners, steps, before, after, later=()):
    ins, outs, scr, bodies = {}, {}, {}, []
    for part in parts:
        ins.update(part.ins)
        outs.update(part.outs)
        scr.update(part.scr)
        if hasattr(part, "body"):
            bodies.append(part.body)
    for name in later:
        array, _ = ins.pop(name)
        ins["h_" + name] = (array, pl.BlockSpec(memory_space=pl.ANY))
        scr[name] = pltpu.VMEM(array.shape, array.dtype)
    scr["l_sem"] = dma(max(1, len(later)))
    names = list(ins) + list(outs) + list(scr)

    def kernel(*refs):
        e = SimpleNamespace(**dict(zip(names, refs, strict=True)))
        step = pl.program_id(0)

        def bring():
            return [
                pltpu.make_async_copy(getattr(e, "h_" + name), getattr(e, name), e.l_sem.at[k])
                for k, name in enumerate(later)
            ]

        def enter():
            barrier = pltpu.get_barrier_semaphore()
            devices = partners()
            for device in devices:
                pl.semaphore_signal(barrier, inc=1, device_id=device, device_id_type=MESH)
            pl.semaphore_wait(barrier, len(devices))

        def run(listed):
            for stage in listed:
                if stage is ready:
                    for copy in bring():
                        copy.wait()
                else:
                    stage(e)

        for t in range(steps):
            if t == 0 or t in before:

                @pl.when(step == t)
                def _(t=t):
                    if t == 0:
                        for copy in bring():
                            copy.start()
                        enter()
                    run(before.get(t, ()))

        for body in bodies:
            body(e, step)
        for t in sorted(after):
            pl.when(step == t)(lambda t=t: run(after[t]))

    got = pl.pallas_call(
        kernel,
        grid=(steps,),
        out_shape=[shape for shape, _ in outs.values()],
        in_specs=[spec for _, spec in ins.values()],
        out_specs=[spec for _, spec in outs.values()],
        scratch_shapes=list(scr.values()),
        compiler_params=pltpu.CompilerParams(
            vmem_limit_bytes=VMEM_LIMIT, collective_id=next(ids), has_side_effects=True
        ),
    )(*[array for array, _ in ins.values()])
    return SimpleNamespace(**dict(zip(outs, got, strict=True)))


def ready(e):
    raise NotImplementedError


def place():
    return lax.axis_index("space"), lax.axis_index("nbr")


def wrap(value, count):
    return lax.rem(value + count, count)


def flip(value, bit):
    return value + (1 - 2 * (lax.rem(value // (1 << bit), 2))) * (1 << bit)


def across(axis, bit):
    s, n = place()
    return (s, flip(n, bit)) if axis == "nbr" else (flip(s, bit), n)


def near_cross(z):
    s, n = place()
    found = [(s, wrap(n + k, z.nn)) for k in range(1, z.nn)]
    sides = (1, -1) if z.ns > 2 else (1,)
    return found + [(wrap(s + d, z.ns), wrap(n + k, z.nn)) for d in sides for k in range(1, z.nn)]


def same_lane(z):
    s, n = place()
    return [(wrap(s + k, z.ns), n) for k in range(1, z.ns)]


def quarter(z):
    s, n = place()
    return pl.ds(pl.multiple_of(n * z.Q, 16), z.Q)


def far_copies(z, send, recv, fs, fr):
    s, n = place()
    found = []
    for k in range(1, z.ns):
        p = wrap(s + k, z.ns)
        found.append(
            remote(
                send.at[pl.ds(p * z.CAP, z.CAP)], recv.at[pl.ds(s * z.CAP, z.CAP)], fs.at[k], fr.at[k], (p, n)
            )
        )
    return found


def far_own(z, send, recv):
    s, n = place()
    here = pl.ds(pl.multiple_of(s * z.CAP, 8), z.CAP)
    recv[here] = send[here]


def setup_part(z, a):
    lines = (
        a.message_bias,
        a.edge_bias,
        a.edge_shift,
        a.third_gain,
        a.third_shift,
        a.message_shift,
        a.first_gain,
        a.first_shift,
        a.output_bias,
        a.second_gain,
        a.second_shift,
    )
    at = (0, 1, 2, 3, 4, 8, 9, 10, 11, 12, 13)

    def begin(e):
        e.vecs[...] = jnp.zeros_like(e.vecs)
        given = (e.va, e.vb, e.vc, e.vd, e.ve, e.vf, e.vg, e.vh, e.vi, e.vj, e.vk)
        for row, line in zip(at, given, strict=True):
            wide = line.shape[0]
            e.vecs[row : row + 1, 0:wide] = line[...].astype(F32).reshape(1, wide)
        hidden = e.vl[...].astype(F32).reshape(1, z.FF)
        for k in range(z.FF // z.DN):
            e.vecs[16 + k : 17 + k] = hidden[:, k * z.DN : (k + 1) * z.DN]
        p = lax.broadcasted_iota(jnp.int32, (z.CAP, z.FAR), 0)
        q = lax.broadcasted_iota(jnp.int32, (z.CAP, z.FAR), 1)
        spread = jnp.where(lax.rem(q, z.CAP) == p, 1.0, 0.0)
        b = lax.broadcasted_iota(jnp.int32, (z.ns, z.FAR), 0)
        c = lax.broadcasted_iota(jnp.int32, (z.ns, z.FAR), 1)
        for k in range(z.B):
            wide = jnp.dot(
                e.send_rows[k].astype(F32), spread, precision=lax.Precision.HIGHEST, preferred_element_type=F32
            )
            e.send[k] = (row_sum(jnp.where(c // z.CAP == b, wide, 0.0)) + 0.5).astype(jnp.int32)

    given = dict(zip("abcdefghijkl", lines + (a.hidden_bias,)))
    return SimpleNamespace(
        begin=begin,
        ins=dict({"v" + k: vm(v) for k, v in given.items()}, send_rows=vm(a.send_rows)),
        outs=dict(vecs=out((24, z.DN), F32), send=out((z.B, 1, z.FAR), jnp.int32)),
        scr={},
    )


def table_part(z, a):
    R, DN, FAR, TP, ns, B = z.R, z.DN, z.FAR, z.TP, z.ns, z.B
    half = R // 2

    def far(e, b):
        return far_copies(z, e.t_fsend.at[b], e.t_frecv.at[b], e.t_fs.at[b], e.t_fr.at[b])

    def near(e, b):
        s, n = place()
        h = pl.multiple_of(lax.rem(n, 2) * half, 16)
        src = e.nodes.at[b, pl.ds(h, half)]
        return [
            remote(
                src, e.t_tab.at[b, pl.ds(base + h, half)], e.t_ns.at[b, k], e.t_nr.at[b, k], (wrap(s + step, ns), n)
            )
            for k, (step, base) in enumerate(((1, 0), (-1, 2 * R)))
        ]

    def mate(e, b):
        s, n = place()
        h = pl.multiple_of(lax.rem(n, 2) * half, 16)
        found = []
        for k, base in enumerate((0, 2 * R)):
            rows = e.t_tab.at[b, pl.ds(base + h, half)]
            found.append(remote(rows, rows, e.t_ms.at[b, k], e.t_mr.at[b, k], (s, flip(n, 0))))
        return found

    def launch(b):
        def stage(e):
            for copy in near(e, b):
                copy.start()

        return stage

    def begin(b):
        def stage(e):
            own = e.nodes[b]
            e.t_fsend[b] = dot_tn(hot(e.send[b], R), own)
            for copy in far(e, b):
                copy.start()
            e.t_tab[b, R : 2 * R] = own
            if TP > 3 * R + FAR:
                e.t_tab[b, 3 * R + FAR :] = jnp.zeros((TP - 3 * R - FAR, DN), BF)

        return stage

    def middle(b):
        def stage(e):
            for one, two in zip(near(e, b), mate(e, b), strict=True):
                one.wait_recv()
                two.start()

        return stage

    def finish(b):
        def stage(e):
            far_own(z, e.t_fsend.at[b], e.t_frecv.at[b])
            for copy in far(e, b):
                copy.wait()
            for copy in near(e, b):
                copy.wait_send()
            for copy in mate(e, b):
                copy.wait()
            e.t_tab[b, 3 * R : 3 * R + FAR] = e.t_frecv[b].astype(BF)
            e.tables[b] = e.t_tab[b]

        return stage

    return SimpleNamespace(
        launch=launch,
        begin=begin,
        middle=middle,
        finish=finish,
        ins=dict(nodes=vm(a.nodes)),
        outs=dict(tables=out((B, TP, DN), BF)),
        scr=dict(
            t_tab=pltpu.VMEM((B, TP, DN), BF),
            t_fsend=pltpu.VMEM((B, FAR, DN), F32),
            t_frecv=pltpu.VMEM((B, FAR, DN), F32),
            t_fs=dma(B, ns),
            t_fr=dma(B, ns),
            t_ns=dma(B, 2),
            t_nr=dma(B, 2),
            t_ms=dma(B, 2),
            t_mr=dma(B, 2),
        ),
    )


def message_part(z, a):
    R, DN, DE, TP, S, B = z.R, z.DN, z.DE, z.TP, z.S, z.B
    T = S // GROUP

    def body(e, step):
        sample, own = step // T, lax.rem(step, T)

        @pl.when(own == 0)
        def _():
            e.m_tabt[...] = dot_nt(e.m_wpt[...], e.t_tab[sample]).astype(BF)
            e.m_selft[...] = e.m_selfs[sample]
            e.m_acc[...] = jnp.zeros_like(e.m_acc)

        slots = [own * GROUP + g for g in range(GROUP)]
        line = pl.ds(sample, 1)
        value = dot(e.m_tabt[...], hot(side([e.nbr[s, line] for s in slots]), TP)) + dot(
            e.m_wet[...], side([e.m_edges[0, g] for g in range(GROUP)])
        )
        acc = e.m_acc[0:DN]
        count = e.m_acc[DN:]
        for g, s in enumerate(slots):
            live = e.live[s, line].astype(F32)
            act, slope = gelu_both(value[:, g * R : (g + 1) * R] + e.m_selft[...])
            e.slope[0, g] = slope.astype(BF)
            acc = acc + act * live
            count = count + live
        e.m_acc[0:DN] = acc
        e.m_acc[DN:] = count
        for b, ref in enumerate((e.part_a, e.part_b)):

            @pl.when(step == (b + 1) * T - 1)
            def _(ref=ref):
                ref[...] = e.m_acc[...].T.astype(BF)

    def prepare(e):
        e.m_wpt[...] = e.w_peer[...].T
        e.m_wet[...] = e.w_edge[...].T
        turned = e.w_self[...].T
        for b in range(B):
            e.m_selfs[b] = dot_nt(turned, e.nodes[b]) + e.vecs[0:8].T[:, 0:1]

    return SimpleNamespace(
        body=body,
        prepare=prepare,
        ins=dict(
            nodes=vm(a.nodes),
            m_edges=(a.edges_t, pl.BlockSpec((1, GROUP, DE, R), lambda i: (i // T, lax.rem(i, T), 0, 0))),
            nbr=vm(a.nbr),
            live=vm(a.live),
            w_self=vm(a.message_self),
            w_peer=vm(a.message_peer),
            w_edge=vm(a.message_edge),
        ),
        outs=dict(
            slope=(
                jax.ShapeDtypeStruct((B, S, DN, R), BF),
                pl.BlockSpec((1, GROUP, DN, R), lambda i: (i // T, lax.rem(i, T), 0, 0)),
            ),
            part_b=out((R, DN + LANES), BF),
        ),
        scr=dict(
            part_a=pltpu.VMEM((R, DN + LANES), BF),
            m_tabt=pltpu.VMEM((DN, TP), BF),
            m_selft=pltpu.VMEM((DN, R), F32),
            m_selfs=pltpu.VMEM((B, DN, R), F32),
            m_wpt=pltpu.VMEM((DN, DN), BF),
            m_wet=pltpu.VMEM((DN, DE), BF),
            m_acc=pltpu.VMEM((DN + LANES, R), F32),
        ),
    )


def forward_part(z, a, b, part):
    R, DN, DE, FF, Q, FAR, TP, ns, nn = z.R, z.DN, z.DE, z.FF, z.Q, z.FAR, z.TP, z.ns, z.nn
    W = DN + LANES

    def sums(e):
        s, n = place()
        found = []
        for k in range(1, nn):
            q = wrap(n + k, nn)
            rows = pl.ds(pl.multiple_of(q * Q, 16), Q)
            found.append(remote(part(e).at[rows], e.f_sum.at[k], e.f_ss.at[k], e.f_sr.at[k], (s, q)))
        return found

    def alls(e):
        s, n = place()
        rows = e.f_new.at[quarter(z)]
        return [
            remote(rows, rows, e.f_as.at[k], e.f_ar.at[k], (s, wrap(n + k, nn))) for k in range(1, nn)
        ]

    def near(e):
        s, n = place()
        found = []
        for i, (step, base) in enumerate(((1, 0), (-1, 2 * R))):
            rows = pl.ds(pl.multiple_of(base + n * Q, 16), Q)
            for k in range(nn):
                to = (wrap(s + step, ns), wrap(n + k, nn))
                found.append(remote(e.f_pe, e.f_tab.at[rows], e.f_ns.at[i, k], e.f_nr.at[i, k], to))
        return found

    def far(e):
        return far_copies(z, e.f_fsend, e.f_frecv, e.f_fs, e.f_fr)

    def begin(e):
        for copy in sums(e):
            copy.start()

    def compute(e):
        mine = quarter(z)
        for copy in sums(e):
            copy.wait()
        total = part(e)[mine].astype(F32)
        for k in range(1, nn):
            total = total + e.f_sum[k].astype(F32)
        count = total[:, DN : DN + 1]
        summed_act = total[:, :DN].astype(BF)
        summed = dot(summed_act, e.w_out[...]) + count * e.vecs[8:9]
        updated = e.nodes[b, mine].astype(F32) + summed / jnp.maximum(count, 1.0)
        xhat1, rstd1 = norm_rows(updated)
        hidden = xhat1 * e.vecs[9:10] + e.vecs[10:11]
        low = hidden.astype(BF)
        bias = side([e.vecs[16 + k : 17 + k] for k in range(FF // DN)])
        act, slope = gelu_both(dot(low, e.w_in[...]) + bias)
        act = act.astype(BF)
        xhat2, rstd2 = norm_rows(hidden + dot(act, e.w_ffn[...]) + e.vecs[11:12])
        fresh = (xhat2 * e.vecs[12:13] + e.vecs[13:14]).astype(BF)
        e.f_new[mine] = fresh
        e.f_pe[...] = dot_nt(fresh, e.ept[...]).astype(BF)
        for copy in alls(e):
            copy.start()
        for copy in near(e):
            copy.start()
        e.f_osum[...] = summed_act
        e.f_ocount[...] = total[:, DN:]
        e.f_ox1[...] = xhat1
        e.f_or1[...] = jnp.broadcast_to(rstd1, (Q, LANES))
        e.f_olow[...] = low
        e.f_oslope[...] = slope.astype(BF)
        e.f_oact[...] = act
        e.f_ox2[...] = xhat2
        e.f_or2[...] = jnp.broadcast_to(rstd2, (Q, LANES))
        e.f_oq[...] = fresh

    def spread(e):
        for copy in alls(e):
            copy.wait()
        own = dot_nt(e.f_new[...], e.ept[...]).astype(BF)
        e.f_tab[R : 2 * R] = own
        e.f_fsend[...] = dot_tn(hot(e.send[b], R), own)
        for copy in far(e):
            copy.start()
        e.f_onew[...] = e.f_new[...]
        if TP > 3 * R + FAR:
            e.f_tab[3 * R + FAR :] = jnp.zeros((TP - 3 * R - FAR, DE), BF)

    def finish(e):
        far_own(z, e.f_fsend, e.f_frecv)
        for copy in near(e):
            copy.wait()
        for copy in far(e):
            copy.wait()
        e.f_tab[3 * R : 3 * R + FAR] = e.f_frecv[...].astype(BF)
        e.f_otab[...] = e.f_tab[...]

    return SimpleNamespace(
        begin=begin,
        compute=compute,
        spread=spread,
        finish=finish,
        ins=dict(
            nodes=vm(a.nodes),
            w_out=vm(a.message_out),
            w_in=vm(a.hidden_in),
            w_ffn=vm(a.hidden_out),
            ept=vm(a.edge_peer_t),
        ),
        outs=dict(
            f_onew=out((R, DN), BF),
            f_otab=out((TP, DE), BF),
            f_osum=out((Q, DN), BF),
            f_ocount=out((Q, LANES), F32),
            f_ox1=out((Q, DN), F32),
            f_or1=out((Q, LANES), F32),
            f_olow=out((Q, DN), BF),
            f_oslope=out((Q, FF), BF),
            f_oact=out((Q, FF), BF),
            f_ox2=out((Q, DN), F32),
            f_or2=out((Q, LANES), F32),
            f_oq=out((Q, DN), BF),
        ),
        scr=dict(
            f_sum=pltpu.VMEM((nn, Q, W), BF),
            f_new=pltpu.VMEM((R, DN), BF),
            f_pe=pltpu.VMEM((Q, DE), BF),
            f_tab=pltpu.VMEM((TP, DE), BF),
            f_fsend=pltpu.VMEM((FAR, DE), F32),
            f_frecv=pltpu.VMEM((FAR, DE), F32),
            f_ss=dma(nn),
            f_sr=dma(nn),
            f_as=dma(nn),
            f_ar=dma(nn),
            f_ns=dma(2, nn),
            f_nr=dma(2, nn),
            f_fs=dma(ns),
            f_fr=dma(ns),
        ),
    )


def edge_part(z, a, first):
    R, DN, DE, TP, S, FAR, B = z.R, z.DN, z.DE, z.TP, z.S, z.FAR, z.B
    T = S // GROUP

    def body(e, step):
        sample, own = step // T, lax.rem(step, T)

        @pl.when(step == 0)
        def _():
            e.e_cols[...] = e.vecs[0:8].T[:DE]
            e.e_wnt[...] = e.e_wn[...].astype(F32).T.astype(BF)
            e.e_wot[...] = e.e_wo[...].astype(F32).T.astype(BF)
            for ref in (e.e_gacc, e.e_hacc, e.e_uacc, e.e_vacc, e.e_dwo, e.e_dwn):
                ref[...] = jnp.zeros_like(ref)

        for b, (table, fresh) in enumerate(((e.a_tab, e.a_new), (e.f_tab, e.f_new))):

            @pl.when(step == b * T)
            def _(table=table, fresh=fresh):
                e.e_tabt[...] = table[...].astype(F32).T.astype(BF)
                e.e_selft[...] = dot_nt(e.est[...], fresh[...]) + e.e_cols[:, 1:2]
                e.e_ptab[...] = jnp.zeros_like(e.e_ptab)
                e.e_sacc[...] = jnp.zeros_like(e.e_sacc)

        line = pl.ds(sample, 1)
        index = hot(side([e.nbr[own * GROUP + g, line] for g in range(GROUP)]), TP)
        edge = side([e.m_edges[0, g] for g in range(GROUP)])
        value = dot(e.e_tabt[...], index) + dot(e.e_wnt[...], edge)
        value = value + side([e.e_selft[...]] * GROUP)
        act, slope = gelu_both(value)
        act = act.astype(BF)
        shift_c, gain_c, bias_c = e.e_cols[:, 2:3], e.e_cols[:, 3:4], e.e_cols[:, 4:5]
        full = edge.astype(F32) + dot(e.e_wot[...], act) + shift_c
        full = full - jnp.mean(full, 0, keepdims=True)
        rstd = lax.rsqrt(jnp.mean(full * full, 0, keepdims=True) + EPS)
        xhat = full * rstd
        final = (xhat * gain_c + bias_c).astype(BF)
        cot = side([e.e_cot[0, g] for g in range(GROUP)]).astype(F32)
        scaled = cot * gain_c
        back = rstd * (
            scaled - jnp.mean(scaled, 0, keepdims=True) - xhat * jnp.mean(scaled * xhat, 0, keepdims=True)
        )
        low = back.astype(BF)
        e.e_dwo[...] += dot_nt(act, low)
        inner = (slope * dot(e.e_wo[...], low)).astype(BF)
        e.e_dwn[...] += dot_nt(edge, inner)
        part = (back + dot(e.e_wn[...], inner)).astype(BF)
        e.e_ptab[...] += dot_nt(index, inner)
        gain_g = cot * xhat
        low_f = low.astype(F32)
        inner_f = inner.astype(F32)
        s_acc, g_acc, h_acc, u_acc = e.e_sacc[...], e.e_gacc[...], e.e_hacc[...], e.e_uacc[...]
        for g in range(GROUP):
            cut = slice(g * R, (g + 1) * R)
            e.e_final[0, g] = final[:, cut]
            e.e_part[0, g] = part[:, cut]
            s_acc = s_acc + inner_f[:, cut]
            g_acc = g_acc + gain_g[:, cut]
            h_acc = h_acc + cot[:, cut]
            u_acc = u_acc + low_f[:, cut]
        e.e_sacc[...] = s_acc
        e.e_gacc[...] = g_acc
        e.e_hacc[...] = h_acc
        e.e_uacc[...] = u_acc
        ends = ((e.a_tgrad, e.a_fgrad, e.a_sgrad), (e.e_tgrad, e.e_fgrad, e.e_sgrad))
        for b, (tgrad, fgrad, sgrad) in enumerate(ends):

            @pl.when(step == (b + 1) * T - 1)
            def _(tgrad=tgrad, fgrad=fgrad, sgrad=sgrad):
                rows = e.e_ptab[...]
                tgrad[...] = rows.astype(BF)
                fgrad[...] = rows[3 * R : 3 * R + FAR]
                turned = e.e_sacc[...].T
                sgrad[...] = turned.astype(BF)
                e.e_vacc[0:1] += row_sum(turned)

        @pl.when(step == B * T - 1)
        def _():
            for k, ref in enumerate((e.e_uacc, e.e_gacc, e.e_hacc)):
                e.e_vacc[k + 1 : k + 2] = row_sum(ref[...].T)
            e.e_vgrad[...] = e.e_vacc[...]

    stream = pl.BlockSpec((1, GROUP, DE, R), lambda i: (i // T, lax.rem(i, T), 0, 0))
    return SimpleNamespace(
        body=body,
        ins=dict(
            a_tab=vm(first.f_otab),
            a_new=vm(first.f_onew),
            m_edges=(a.edges_t, stream),
            e_cot=(a.cot_t, stream),
            nbr=vm(a.nbr),
            est=vm(a.edge_self_t),
            e_wn=vm(a.edge_own),
            e_wo=vm(a.edge_out),
        ),
        outs=dict(
            e_final=(jax.ShapeDtypeStruct((B, S, DE, R), BF), stream),
            e_part=(jax.ShapeDtypeStruct((B, S, DE, R), BF), stream),
            e_tgrad=out((TP, DE), BF),
            e_fgrad=out((FAR, DE), F32),
            e_sgrad=out((R, DE), BF),
            e_vgrad=out((8, DE), F32),
            e_dwo=out((DE, DE), F32),
            e_dwn=out((DE, DE), F32),
        ),
        scr=dict(
            a_tgrad=pltpu.VMEM((TP, DE), BF),
            a_fgrad=pltpu.VMEM((FAR, DE), F32),
            a_sgrad=pltpu.VMEM((R, DE), BF),
            e_tabt=pltpu.VMEM((DE, TP), BF),
            e_cols=pltpu.VMEM((DE, 8), F32),
            e_selft=pltpu.VMEM((DE, R), F32),
            e_wnt=pltpu.VMEM((DE, DE), BF),
            e_wot=pltpu.VMEM((DE, DE), BF),
            e_ptab=pltpu.VMEM((TP, DE), F32),
            e_sacc=pltpu.VMEM((DE, R), F32),
            e_gacc=pltpu.VMEM((DE, R), F32),
            e_hacc=pltpu.VMEM((DE, R), F32),
            e_uacc=pltpu.VMEM((DE, R), F32),
            e_vacc=pltpu.VMEM((8, DE), F32),
        ),
    )


def backward_part(z, a, b, node, grads):
    R, DN, DE, FF, Q, FAR, TP, ns, nn = z.R, z.DN, z.DE, z.FF, z.Q, z.FAR, z.TP, z.ns, z.nn
    W = DN + LANES

    def near(e):
        s, n = place()
        tgrad = grads(e)[0]
        return [
            remote(
                tgrad.at[pl.ds(base, R)], e.b_near.at[k], e.b_ns.at[k], e.b_nr.at[k], (wrap(s + step, ns), n)
            )
            for k, (step, base) in enumerate(((-1, 0), (1, 2 * R)))
        ]

    def far(e):
        return far_copies(z, grads(e)[1], e.b_frecv, e.b_fs, e.b_fr)

    def sums(e):
        s, n = place()
        found = []
        for k in range(1, nn):
            q = wrap(n + k, nn)
            rows = pl.ds(pl.multiple_of(q * Q, 16), Q)
            found.append(remote(e.b_pair.at[:, rows], e.b_sum.at[k], e.b_ss.at[k], e.b_sr.at[k], (s, q)))
        return found

    def alls(e):
        s, n = place()
        rows = e.b_all.at[quarter(z)]
        return [
            remote(rows, rows, e.b_as.at[k], e.b_ar.at[k], (s, wrap(n + k, nn))) for k in range(1, nn)
        ]

    def begin(e):
        for copy in near(e):
            copy.start()
        for copy in far(e):
            copy.start()

    def gather(e):
        tgrad, fgrad, sgrad = grads(e)
        far_own(z, fgrad, e.b_frecv)
        for copy in near(e):
            copy.wait()
        for copy in far(e):
            copy.wait()
        peer = (
            tgrad[R : 2 * R].astype(F32)
            + e.b_near[0].astype(F32)
            + e.b_near[1].astype(F32)
            + dot(hot(e.send[b], R), e.b_frecv[...].astype(BF))
        )
        e.b_pair[0] = peer.astype(BF)
        e.b_pair[1] = sgrad[...]
        for copy in sums(e):
            copy.start()

    def compute(e):
        mine = quarter(z)
        for copy in sums(e):
            copy.wait()
        peer = e.b_pair[0, mine].astype(F32)
        own = e.b_pair[1, mine].astype(F32)
        for k in range(1, nn):
            peer = peer + e.b_sum[k, 0].astype(F32)
            own = own + e.b_sum[k, 1].astype(F32)
        peer = peer.astype(BF)
        own = own.astype(BF)
        final = e.cot[b, mine].astype(F32) + dot(own, e.est[...]) + dot(peer, e.ept[...])
        xhat2 = e.b_x2[...]
        mid = norm_rows_back(xhat2, e.b_r2[:, 0:1], final * e.vecs[12:13])
        mid_low = mid.astype(BF)
        ffn = (e.b_slope[...].astype(F32) * dot_nt(mid_low, e.w_ffn[...])).astype(BF)
        hidden = mid + dot_nt(ffn, e.w_in[...])
        xhat1 = e.b_x1[...]
        grad = norm_rows_back(xhat1, e.b_r1[:, 0:1], hidden * e.vecs[9:10])
        count = e.b_count[:, 0:1]
        low = (grad / jnp.maximum(count, 1.0)).astype(BF)
        e.b_all[mine] = side([low, e.b_count[...].astype(BF)])
        for copy in alls(e):
            copy.start()
        e.b_omid[...] = mid_low
        e.b_offn[...] = ffn
        e.b_olow[...] = low
        e.b_opeer[...] = peer
        e.b_oself[...] = own
        wide = row_sum(ffn.astype(F32))
        e.b_ovec[...] = jnp.concatenate(
            [
                row_sum(low.astype(F32) * count),
                row_sum(hidden * xhat1),
                row_sum(hidden),
                row_sum(mid_low.astype(F32)),
                row_sum(final * xhat2),
                row_sum(final),
            ]
            + [wide[:, k * DN : (k + 1) * DN] for k in range(FF // DN)]
            + [jnp.zeros((6, DN), F32)],
            0,
        )

    def finish(e):
        for copy in alls(e):
            copy.wait()
        e.b_oall[...] = e.b_all[...]

    return SimpleNamespace(
        begin=begin,
        gather=gather,
        compute=compute,
        finish=finish,
        ins=dict(
            b_count=vm(node.f_ocount),
            b_x1=vm(node.f_ox1),
            b_r1=vm(node.f_or1),
            b_slope=vm(node.f_oslope),
            b_x2=vm(node.f_ox2),
            b_r2=vm(node.f_or2),
            cot=vm(a.node_cot),
            w_in=vm(a.hidden_in),
            w_ffn=vm(a.hidden_out),
            est=vm(a.edge_self_t),
            ept=vm(a.edge_peer_t),
        ),
        outs=dict(
            b_oall=out((R, W), BF),
            b_omid=out((Q, DN), BF),
            b_offn=out((Q, FF), BF),
            b_olow=out((Q, DN), BF),
            b_opeer=out((Q, DE), BF),
            b_oself=out((Q, DE), BF),
            b_ovec=out((16, DN), F32),
        ),
        scr=dict(
            b_near=pltpu.VMEM((2, R, DE), BF),
            b_frecv=pltpu.VMEM((FAR, DE), F32),
            b_pair=pltpu.VMEM((2, R, DE), BF),
            b_sum=pltpu.VMEM((nn, 2, Q, DE), BF),
            b_all=pltpu.VMEM((R, W), BF),
            b_ns=dma(2),
            b_nr=dma(2),
            b_fs=dma(ns),
            b_fr=dma(ns),
            b_ss=dma(nn),
            b_sr=dma(nn),
            b_as=dma(nn),
            b_ar=dma(nn),
        ),
    )


def last_part(z, a, spread, slope, part, tables):
    R, DN, DE, TP, S, FAR, B = z.R, z.DN, z.DE, z.TP, z.S, z.FAR, z.B
    T = S // GROUP

    def body(e, step):
        sample, own = lax.rem(step // T, B), lax.rem(step, T)
        for b, ref in enumerate((e.a_all, e.b_all)):

            @pl.when(step == b * T)
            def _(ref=ref, b=b):
                pltpu.make_async_copy(e.g_tables.at[b], e.g_tab, e.g_ts.at[b]).start()
                e.g_ht[b] = dot_nt(e.w_out[...], ref[:, 0:DN])
                e.g_ptab[...] = jnp.zeros_like(e.g_ptab)
                e.g_sacc[...] = jnp.zeros_like(e.g_sacc)
                if b == 0:
                    e.g_dwe[...] = jnp.zeros_like(e.g_dwe)
                    e.g_vec[...] = jnp.zeros_like(e.g_vec)

        line = pl.ds(sample, 1)
        slots = [own * GROUP + g for g in range(GROUP)]

        def pieces():
            return [
                (e.g_slope[0, g].astype(F32) * (e.g_ht[sample] * e.live[s, line].astype(F32))).astype(BF)
                for g, s in enumerate(slots)
            ]

        @pl.when(step < B * T)
        def _():
            index = hot(side([e.nbr[s, line] for s in slots]), TP)
            edge = side([e.m_edges[0, g] for g in range(GROUP)])
            inner = pieces()
            acc = e.g_sacc[...]
            for piece in inner:
                acc = acc + piece.astype(F32)
            e.g_sacc[...] = acc
            inner = side(inner)
            e.g_ptab[...] += dot_nt(inner, index)
            e.g_dwe[...] += dot_nt(inner, edge)

        @pl.when(step >= B * T)
        def _():
            back = dot(e.w_edge[...], side(pieces()))
            for g in range(GROUP):
                e.g_edge[0, g] = (back[:, g * R : (g + 1) * R] + e.g_part[0, g].astype(F32)).astype(BF)

        for b in range(B):

            @pl.when(step == (b + 1) * T - 1)
            def _(b=b):
                self_t = e.g_sacc[...].astype(BF)
                peer_t = e.g_ptab[...].astype(BF)
                e.o_rows[b] = dot(e.w_peer[...], peer_t).astype(BF)
                e.o_rows[b, :, R : 2 * R] = (
                    dot(e.w_peer[...], peer_t[:, R : 2 * R]) + dot(e.w_self[...], self_t)
                ).astype(BF)
                pltpu.make_async_copy(e.g_tables.at[b], e.g_tab, e.g_ts.at[b]).wait()
                dself = dot(self_t, e.nodes[b])
                dpeer = dot(peer_t, e.g_tab[...])
                e.g_dself[...] = dself if b == 0 else e.g_dself[...] + dself
                e.g_dpeer[...] = dpeer if b == 0 else e.g_dpeer[...] + dpeer
                e.g_vec[0:1] += row_sum(e.g_sacc[...].T)

    def always(i):
        return (lax.rem(i // T, B), lax.rem(i, T), 0, 0)

    def early(i):
        k = jnp.minimum(i, B * T - 1)
        return (k // T, lax.rem(k, T), 0, 0)

    def late(i):
        k = jnp.maximum(i - B * T, 0)
        return (k // T, lax.rem(k, T), 0, 0)

    return SimpleNamespace(
        body=body,
        ins=dict(
            a_all=vm(spread),
            g_slope=(slope, pl.BlockSpec((1, GROUP, DN, R), always)),
            g_part=(part, pl.BlockSpec((1, GROUP, DE, R), late)),
            g_tables=(tables, pl.BlockSpec(memory_space=pl.ANY)),
            nodes=vm(a.nodes),
            m_edges=(a.edges_t, pl.BlockSpec((1, GROUP, DE, R), early)),
            nbr=vm(a.nbr),
            live=vm(a.live),
            w_self=vm(a.message_self),
            w_peer=vm(a.message_peer),
            w_edge=vm(a.message_edge),
            w_out=vm(a.message_out),
        ),
        outs=dict(g_edge=(jax.ShapeDtypeStruct((B, S, DE, R), BF), pl.BlockSpec((1, GROUP, DE, R), late))),
        scr=dict(
            g_tab=pltpu.VMEM((TP, DN), BF),
            g_ts=dma(B),
            g_ht=pltpu.VMEM((B, DN, R), F32),
            g_ptab=pltpu.VMEM((DN, TP), F32),
            g_sacc=pltpu.VMEM((DN, R), F32),
            g_dself=pltpu.VMEM((DN, DN), F32),
            g_dpeer=pltpu.VMEM((DN, DN), F32),
            g_dwe=pltpu.VMEM((DN, DE), F32),
            g_vec=pltpu.VMEM((8, DN), F32),
            o_rows=pltpu.VMEM((B, DN, TP), BF),
        ),
    )


def nodes_part(z, a, spreads):
    R, DN, FAR, TP, ns, nn, B = z.R, z.DN, z.FAR, z.TP, z.ns, z.nn, z.B
    L = DN // nn

    pairs = nn // 2

    def mates(e, b):
        s, n = place()
        other = flip(n, 0)
        found = []
        for k in range(pairs):
            q = lax.rem(other, 2) + 2 * k
            rows = pl.ds(pl.multiple_of(q * L, 16), L)
            found.append(
                remote(e.o_rows.at[b, rows], e.o_half.at[b, k], e.o_hs.at[b, k], e.o_hr.at[b, k], (s, other))
            )
        return found

    def sums(e, b):
        s, n = place()
        found = []
        for k in range(1, pairs):
            q = wrap(n + 2 * k, nn)
            found.append(
                remote(e.o_pair.at[b, q // 2], e.o_sum.at[b, k - 1], e.o_ss.at[b, k], e.o_sr.at[b, k], (s, q))
            )
        return found

    def near(e, b):
        s, n = place()
        return [
            remote(
                e.o_send.at[b, pl.ds(2 * k * R, R)],
                e.o_near.at[b, k],
                e.o_ns.at[b, k],
                e.o_nr.at[b, k],
                (wrap(s + step, ns), n),
            )
            for k, step in enumerate((-1, 1))
        ]

    def far(e, b):
        return far_copies(z, e.o_fsend.at[b], e.o_frecv.at[b], e.o_fs.at[b], e.o_fr.at[b])

    def begin(b):
        def stage(e):
            for copy in mates(e, b):
                copy.start()

        return stage

    def pair(b):
        def stage(e):
            s, n = place()
            for copy in mates(e, b):
                copy.wait()
            for k in range(pairs):
                q = lax.rem(n, 2) + 2 * k
                rows = pl.ds(pl.multiple_of(q * L, 16), L)
                e.o_pair[b, k] = (e.o_rows[b, rows].astype(F32) + e.o_half[b, k].astype(F32)).astype(BF)
            for copy in sums(e, b):
                copy.start()

        return stage

    def middle(b):
        def stage(e):
            s, n = place()
            for copy in sums(e, b):
                copy.wait()
            total = e.o_pair[b, n // 2].astype(F32)
            for k in range(1, pairs):
                total = total + e.o_sum[b, k - 1].astype(F32)
            turned = total.T
            e.o_send[b] = turned.astype(BF)
            e.o_fsend[b] = turned[3 * R : 3 * R + FAR]
            for copy in near(e, b):
                copy.start()
            for copy in far(e, b):
                copy.start()
            column = pl.ds(pl.multiple_of(n * L, L), L)
            spread = spreads(e)[b]
            count = spread[:, DN : DN + 1].astype(F32)
            e.o_grad[b] = turned[R : 2 * R] + spread[:, column].astype(F32) * jnp.maximum(count, 1.0)

        return stage

    def finish(b):
        def stage(e):
            far_own(z, e.o_fsend.at[b], e.o_frecv.at[b])
            for copy in near(e, b):
                copy.wait()
            for copy in far(e, b):
                copy.wait()
            e.o_grad[b] += (
                e.o_near[b, 0].astype(F32)
                + e.o_near[b, 1].astype(F32)
                + dot(hot(e.send[b], R), e.o_frecv[b].astype(BF))
            )

        return stage

    return SimpleNamespace(
        begin=begin,
        pair=pair,
        middle=middle,
        finish=finish,
        ins={},
        outs=dict(o_grad=out((B, R, L), F32)),
        scr=dict(
            o_half=pltpu.VMEM((B, pairs, L, TP), BF),
            o_pair=pltpu.VMEM((B, pairs, L, TP), BF),
            o_sum=pltpu.VMEM((B, pairs - 1, L, TP), BF),
            o_hs=dma(B, pairs),
            o_hr=dma(B, pairs),
            o_send=pltpu.VMEM((B, TP, L), BF),
            o_near=pltpu.VMEM((B, 2, R, L), BF),
            o_fsend=pltpu.VMEM((B, FAR, L), F32),
            o_frecv=pltpu.VMEM((B, FAR, L), F32),
            o_ss=dma(B, pairs),
            o_sr=dma(B, pairs),
            o_ns=dma(B, 2),
            o_nr=dma(B, 2),
            o_fs=dma(B, ns),
            o_fr=dma(B, ns),
        ),
    )


def cut(total, start, rounds):
    unit = 16 << SPLITS
    units = max(3 * rounds, -(-total // unit))
    count = 3 * rounds
    sizes = [units // count + (1 if k < units % count else 0) for k in range(count)]
    starts = [start + sum(sizes[:k]) * unit for k in range(count)]
    return start + units * unit, [(at, size * unit) for at, size in zip(starts, sizes)]


def bit_orders(z):
    nbr = [("nbr", k) for k in range(z.nn.bit_length() - 1)]
    space = [("space", k) for k in range(z.ns.bit_length() - 1)]
    first, ring, rest = nbr[:1], [nbr[1], space[0], space[1]], nbr[2:] + space[2:]
    return [first + ring[k:] + ring[:k] + rest[: SPLITS - 4] for k in range(3)], rest[SPLITS - 4 :]


def pack_rows(z):
    DN, DE, FF = z.DN, z.DE, z.FF
    early = dict(wi=FF, wf=FF, wo=DN, es=DE, ep=DE)
    late = dict(ws=DN, wp=DN, we=DE, own=DE, vec=32)
    at, row = SimpleNamespace(), 0
    for group in (early, late):
        first = row
        for name, size in group.items():
            setattr(at, name, row)
            row += size
        used = row
        row, parts = cut(used - first, first, ROUNDS if group is early else 1)
        if group is early:
            at.early, at.early_end = parts, used
        else:
            at.late, at.late_end = parts, used
    at.span = row
    at.rows = -(-row // (2 * DN)) * 2 * DN
    at.middle = at.late[0][0]
    return at


def sum_part(z, a, at, early):
    DN, DE, FF, B = z.DN, z.DE, z.FF, z.B
    orders, whole = bit_orders(z)
    phases = len(orders[0])
    most = max(size for _, size in at.early + at.late) >> phases
    parts = at.early + at.late
    groups = [range(k, k + 3) for k in range(0, len(parts), 3)]
    count = len(parts)

    def bit_value(axis, bit):
        s, n = place()
        return lax.rem((n if axis == "nbr" else s) // (1 << bit), 2)

    def segment(part, depth):
        start, size = parts[part]
        for axis, bit in orders[part % 3][:depth]:
            size //= 2
            start = start + bit_value(axis, bit) * size
        return start, size

    def down(e, part, depth):
        axis, bit = orders[part % 3][depth]
        start, size = segment(part, depth)
        size //= 2
        give = pl.multiple_of(start + (1 - bit_value(axis, bit)) * size, 16)
        base = parts[part][0] + parts[part][1] - 2 * size
        copy = remote(
            e.s_buf.at[pl.ds(give, size)],
            e.s_recv.at[pl.ds(base, size)],
            e.s_ds.at[part, depth],
            e.s_dr.at[part, depth],
            across(axis, bit),
        )
        return copy, size, base

    def up(e, part, depth):
        start, size = segment(part, depth + 1)
        rows = pl.ds(pl.multiple_of(start, 16), size)
        src = e.s_buf if depth == phases - 1 else e.s_out
        return remote(
            src.at[rows],
            e.s_out.at[rows],
            e.s_us.at[part, depth],
            e.s_ur.at[part, depth],
            across(*orders[part % 3][depth]),
        )

    def keep_own(e, part):
        start, size = segment(part, phases)
        rows = pl.ds(pl.multiple_of(start, 16), size)
        return pltpu.make_async_copy(e.s_buf.at[rows], e.s_out.at[rows], e.s_os.at[part])

    def begin(group):
        def stage(e):
            for part in groups[group]:
                down(e, part, 0)[0].start()

        return stage

    def fold(group, depth):
        def stage(e):
            for part in groups[group]:
                copy, size, base = down(e, part, depth)
                copy.wait()
                start, _ = segment(part, depth + 1)
                keep = pl.ds(pl.multiple_of(start, 16), size)
                value = (e.s_buf[keep].astype(F32) + e.s_recv[pl.ds(base, size)].astype(F32)).astype(BF)
                if depth + 1 < phases:
                    e.s_buf[keep] = value
                    down(e, part, depth + 1)[0].start()
                    continue
                for k, (axis, bit) in enumerate(whole):
                    e.s_buf[keep] = value
                    copy = remote(
                        e.s_buf.at[keep],
                        e.s_more.at[part, k, pl.ds(0, size)],
                        e.s_ms.at[part, k],
                        e.s_mr.at[part, k],
                        across(axis, bit),
                    )
                    copy.start()
                    copy.wait()
                    value = (value.astype(F32) + e.s_more[part, k, 0:size].astype(F32)).astype(BF)
                e.s_buf[keep] = value
                keep_own(e, part).start()
                up(e, part, depth).start()

        return stage

    def spread(group, depth):
        def stage(e):
            for part in groups[group]:
                up(e, part, depth).wait()
                if depth == phases - 1:
                    keep_own(e, part).wait()
                if depth:
                    up(e, part, depth - 1).start()

        return stage

    def put(e, row, value):
        e.s_buf[row : row + value.shape[0], : value.shape[1]] = value.astype(BF)

    def clear(e, first, last):
        if last > first:
            e.s_buf[first:last] = jnp.zeros((last - first, DN), BF)

    def pack_early(e):
        def two(one, other):
            return jnp.concatenate([one[...], other[...]], 0)

        low, ffn = two(e.p_low0, e.p_low1), two(e.p_ffn0, e.b_offn)
        act, mid = two(e.p_act0, e.p_act1), two(e.p_mid0, e.b_omid)
        for k in range(FF // DN):
            put(e, at.wi + k * DN, dot_tn(low, ffn[:, k * DN : (k + 1) * DN]))
        for k in range(FF // DN):
            put(e, at.wf + k * DN, dot_tn(act[:, k * DN : (k + 1) * DN], mid))
        put(e, at.wo, dot_tn(two(e.p_sum0, e.p_sum1), two(e.p_grad0, e.b_olow)))
        fresh = two(e.p_new0, e.p_new1)
        put(e, at.es, dot_tn(two(e.p_self0, e.b_oself), fresh))
        put(e, at.ep, dot_tn(two(e.p_peer0, e.b_opeer), fresh))
        clear(e, at.early_end, at.middle)

    def pack_late(e):
        put(e, at.ws, e.g_dself[...].T)
        put(e, at.wp, e.g_dpeer[...].T)
        put(e, at.we, e.g_dwe[...].T)
        gap = jnp.zeros((DE, 256 - DE), F32)
        put(e, at.own, side([e.p_dwn[...], gap, e.p_dwo[...], gap]))
        narrow = side([e.p_vec[...], jnp.zeros((8, DN - DE), F32)])
        put(e, at.vec, jnp.concatenate([e.p_vec0[...] + e.b_ovec[...], narrow, e.g_vec[...]], 0))
        clear(e, at.late_end, at.span)

    f0, f1, b0, ee = early
    return SimpleNamespace(
        begin=begin,
        fold=fold,
        spread=spread,
        pack_early=pack_early,
        pack_late=pack_late,
        phases=phases,
        ins=dict(
            p_low0=vm(f0.f_olow),
            p_low1=vm(f1.f_olow),
            p_act0=vm(f0.f_oact),
            p_act1=vm(f1.f_oact),
            p_sum0=vm(f0.f_osum),
            p_sum1=vm(f1.f_osum),
            p_new0=vm(f0.f_oq),
            p_new1=vm(f1.f_oq),
            p_ffn0=vm(b0.b_offn),
            p_mid0=vm(b0.b_omid),
            p_grad0=vm(b0.b_olow),
            p_self0=vm(b0.b_oself),
            p_peer0=vm(b0.b_opeer),
            p_vec0=vm(b0.b_ovec),
            p_vec=vm(ee.e_vgrad),
            p_dwo=vm(ee.e_dwo),
            p_dwn=vm(ee.e_dwn),
        ),
        outs=dict(s_out=(jax.ShapeDtypeStruct((at.rows, DN), BF), pl.BlockSpec(memory_space=pl.ANY))),
        scr=dict(
            s_buf=pltpu.VMEM((at.span, DN), BF),
            s_recv=pltpu.VMEM((at.span, DN), BF),
            s_os=dma(count),
            s_more=pltpu.VMEM((count, len(whole), most, DN) if whole else (16, DN), BF),
            s_ms=dma(count, max(1, len(whole))),
            s_mr=dma(count, max(1, len(whole))),
            s_ds=dma(count, phases),
            s_dr=dma(count, phases),
            s_us=dma(count, phases),
            s_ur=dma(count, phases),
        ),
    )


def unpack_kernel(z, packed, at, edge, final, node, fresh):
    DN, DE, FF, B, S, R = z.DN, z.DE, z.FF, z.B, z.S, z.R
    size, wide = 2 * DN, FF // DN
    half = wide // 2
    steps = at.rows // size
    slots = S // 3
    blocks = B * 3

    def kernel(p, *refs):
        given, (ws, wp, we, wo, wi, wf, es, ep, own, eo, *vectors), rest = refs[: B + 3], refs[B + 3 : B + 25], refs[B + 25 :]
        step = pl.program_id(0)

        @pl.when(step < blocks)
        def _():
            rest[0][...] = given[0][...]
            rest[1][...] = given[1][...]

        @pl.when(step == 0)
        def _():
            rest[2][...] = given[2][...]
            for b in range(B):
                rest[3][b] = given[3 + b][...]

        def take(row, count):
            return p[row % size : row % size + count].astype(F32)

        def at_row(row):
            return pl.when(step == row // size)

        @pl.when(step < half)
        def _():
            wi[:, :DN] = p[:DN].astype(F32)
            wi[:, DN:] = p[DN:].astype(F32)

        @pl.when(jnp.logical_and(step >= half, step < 2 * half))
        def _():
            wf[...] = p[...].astype(F32)

        @at_row(at.wo)
        def _():
            wo[...] = take(at.wo, DN)

        @at_row(at.es)
        def _():
            es[...] = take(at.es, DE)
            ep[...] = take(at.ep, DE)

        @at_row(at.ws)
        def _():
            ws[...] = take(at.ws, DN)

        @at_row(at.wp)
        def _():
            wp[...] = take(at.wp, DN)

        @at_row(at.we)
        def _():
            we[...] = take(at.we, DE)
            both = take(at.own, DE)
            own[...] = both[:, :DE]
            eo[...] = both[:, 256 : 256 + DE]
            vec = take(at.vec, 32)
            vectors[0][...] = side([vec[6 + k : 7 + k] for k in range(wide)]).reshape(FF)
            for ref, row in zip(vectors[1:], (24, 0, 1, 2, 3, 4, 5, 16, 17, 18, 19), strict=True):
                count = ref.shape[0]
                ref[...] = vec[row : row + 1, :count].reshape(count)

    shapes = [(DN, DN), (DN, DN), (DE, DN), (DN, DN), (DN, FF), (FF, DN), (DE, DN), (DE, DN), (DE, DE), (DE, DE)]
    shapes += [(FF,)] + [(DN,)] * 7 + [(DE,)] * 4
    here = pl.BlockSpec(memory_space=pltpu.VMEM)
    specs = [here] * len(shapes)
    specs[4] = pl.BlockSpec((DN, size), lambda i: (0, jnp.clip(i, 0, half - 1)))
    specs[5] = pl.BlockSpec((size, DN), lambda i: (jnp.clip(i - half, 0, half - 1), 0))

    def turn(i):
        k = jnp.minimum(i, blocks - 1)
        return (k // 3, lax.rem(k, 3), 0, 0)

    stream = pl.BlockSpec((1, slots, DE, R), turn)
    return pl.pallas_call(
        kernel,
        grid=(steps,),
        out_shape=[jax.ShapeDtypeStruct(shape, F32) for shape in shapes]
        + [jax.ShapeDtypeStruct(x.shape, x.dtype) for x in (edge, final, node)]
        + [jax.ShapeDtypeStruct((B,) + fresh[0].shape, fresh[0].dtype)],
        in_specs=[pl.BlockSpec((size, DN), lambda i: (i, 0)), stream, stream, here] + [here] * B,
        out_specs=specs + [stream, stream, here, here],
        compiler_params=pltpu.CompilerParams(vmem_limit_bytes=VMEM_LIMIT),
    )(packed, edge, final, node, *fresh)


def local(
    nodes,
    edges,
    neighbors,
    slot_live,
    send_rows,
    message_self,
    message_peer,
    message_edge,
    message_bias,
    message_out,
    message_shift,
    first_gain,
    first_shift,
    hidden_in,
    hidden_bias,
    hidden_out,
    output_bias,
    second_gain,
    second_shift,
    edge_self,
    edge_peer,
    edge_own,
    edge_bias,
    edge_out,
    edge_shift,
    third_gain,
    third_shift,
    node_cot,
    edge_cot,
):
    a = SimpleNamespace(**locals())
    B, R, DN = nodes.shape
    S, DE = edges.shape[2:]
    ns, nn = lax.axis_size("space"), lax.axis_size("nbr")
    CAP = send_rows.shape[2]
    FAR = ns * CAP
    TP = -(-(3 * R + FAR) // LANES) * LANES
    z = SimpleNamespace(
        B=B, R=R, DN=DN, S=S, DE=DE, ns=ns, nn=nn, CAP=CAP, FAR=FAR, TP=TP, FF=hidden_in.shape[1], Q=R // nn
    )
    ids = itertools.count(1)
    a.edges_t = edges.transpose(0, 2, 3, 1)
    a.cot_t = edge_cot.transpose(0, 2, 3, 1)
    a.nbr = neighbors.transpose(2, 0, 1)
    a.live = slot_live.transpose(2, 0, 1)
    a.edge_self_t, a.edge_peer_t = edge_self.T, edge_peer.T
    T = S // GROUP

    def plain(part):
        return SimpleNamespace(ins=part, outs={}, scr={})

    heavy = ("w_in", "w_ffn")
    small, table, message = setup_part(z, a), table_part(z, a), message_part(z, a)
    node0 = forward_part(z, a, 0, lambda e: e.part_a)
    f0 = build(
        ids,
        [small, table, message, node0],
        lambda: near_cross(z) + same_lane(z),
        2 * T,
        {
            0: [
                table.launch(0),
                small.begin,
                table.begin(0),
                message.prepare,
                table.middle(0),
                table.launch(1),
                table.begin(1),
                table.finish(0),
            ],
            T: [node0.begin],
        },
        {
            2: [table.middle(1)],
            4: [table.finish(1)],
            T + 1: [ready, node0.compute],
            T + 3: [node0.spread],
            2 * T - 1: [node0.finish],
        },
        heavy,
    )
    shared = plain(dict(vecs=vm(f0.vecs), send=vm(f0.send)))

    edge = edge_part(z, a, f0)
    node1 = forward_part(z, a, 1, lambda e: e.part_b)
    back0 = backward_part(z, a, 0, f0, lambda e: (e.a_tgrad, e.a_fgrad, e.a_sgrad))
    f1 = build(
        ids,
        [shared, plain(dict(part_b=vm(f0.part_b))), edge, node1, back0],
        lambda: near_cross(z) + same_lane(z),
        2 * T,
        {0: [node1.begin], T: [back0.begin]},
        {
            1: [ready, node1.compute],
            3: [node1.spread],
            T - 1: [node1.finish],
            T + 2: [back0.gather],
            T + 3: [back0.compute],
            2 * T - 1: [back0.finish],
        },
        heavy,
    )

    at = pack_rows(z)
    last = last_part(z, a, f1.b_oall, f0.slope, f1.e_part, f0.tables)
    back1 = backward_part(z, a, 1, f1, lambda e: (e.e_tgrad, e.e_fgrad, e.e_sgrad))
    outer = nodes_part(z, a, lambda e: (e.a_all, e.b_all))
    total = sum_part(z, a, at, (f0, f1, f1, f1))
    for name, (shape, spec) in back1.outs.items():
        back1.scr[name] = pltpu.VMEM(shape.shape, shape.dtype)
    back1.outs = {}
    D, late = total.phases, ROUNDS

    def fold(d):
        return [total.fold(k, d) for k in range(ROUNDS)]

    def gather(d):
        return [total.spread(k, d) for k in range(ROUNDS)]

    lf, ls = (lambda d: total.fold(late, d)), (lambda d: total.spread(late, d))
    f, g = total.fold, total.spread
    after = {
        1: [back1.gather],
        2: [ready, back1.compute, total.pack_early] + [total.begin(k) for k in range(ROUNDS)],
        3: [f(0, 0)],
        T - 1: [back1.finish, f(1, 0)],
        T: [f(0, 1)],
        T + 1: [f(1, 1)],
        T + 2: [f(0, 2)],
        T + 3: [f(1, 2), outer.pair(0)],
        2 * T - 1: [f(0, 3), outer.begin(1), total.pack_late, total.begin(late)],
        2 * T: [f(1, 3), lf(0)],
        2 * T + 1: [f(0, 4), outer.pair(1)],
        2 * T + 2: [lf(1), f(1, 4)],
        2 * T + 3: [outer.middle(0), lf(2), g(0, 4)],
        2 * T + 4: [outer.middle(1), lf(3)],
        3 * T: [g(1, 4), lf(4)],
        3 * T + 1: [g(0, 3)],
        3 * T + 2: [ls(4), g(1, 3)],
        3 * T + 3: [g(0, 2), ls(3)],
        4 * T - 1: [g(1, 2), ls(2), g(0, 1), ls(1), outer.finish(0), g(1, 1), ls(0), g(0, 0), outer.finish(1), g(1, 0)],
    }
    grads = dict(e_tgrad=vm(f1.e_tgrad), e_fgrad=vm(f1.e_fgrad), e_sgrad=vm(f1.e_sgrad))
    f2 = build(
        ids,
        [shared, plain(grads), last, back1, outer, total],
        lambda: [(lax.axis_index("space"), wrap(lax.axis_index("nbr") + k, nn)) for k in range(1, nn)] + same_lane(z),
        4 * T,
        {0: [back1.begin], T: [outer.begin(0)]},
        after,
        heavy + ("p_act0", "p_act1", "p_ffn0"),
    )
    ws, wp, we, wo, wi, wf, es, ep, own, eo, *vectors = unpack_kernel(
        z, f2.s_out, at, f2.g_edge, f1.e_final, f2.o_grad, [f0.f_onew, f1.f_onew]
    )
    hidden, mb, ms, fg, fs, ob, sg, ss, eb, esh, tg, ts, edge_grad, new_edges, node_grad, new_nodes = vectors
    return (
        new_nodes,
        new_edges.transpose(0, 3, 1, 2),
        node_grad,
        edge_grad.transpose(0, 3, 1, 2),
        ws,
        wp,
        we,
        mb,
        wo,
        ms,
        fg,
        fs,
        wi,
        hidden,
        wf,
        ob,
        sg,
        ss,
        es.T,
        ep.T,
        own,
        eb,
        eo,
        esh,
        tg,
        ts,
    )


def solution(mesh):
    tall = P(None, "space", None)
    slots = P(None, "space", "nbr", None)
    marks = P(None, "space", "nbr")
    return jax.shard_map(
        local,
        mesh=mesh,
        in_specs=(tall, slots, marks, marks, tall) + (P(),) * 22 + (tall, slots),
        out_specs=(tall, slots, marks, slots) + (P(),) * 22,
        check_vma=False,
    )
```
